32 devices in a mesh: group: 4 (over y, x), bulk: 8 (over z, core).
Axes of the slice: x: 2, y: 2, z: 4, core: 2. Of those that a mesh axis runs over, the one named last changes fastest.
Arguments:
- rhs: float32 [128, 64, 128], P(('group', 'bulk')), may hold values from -90 to 90, as said below
- diag_tiles: float32 [128, 128, 128], P(('group', 'bulk')), may hold values from -0.06 to 0.06
- offdiag_blocks: float32 [128, 11, 128, 128], P(('group', 'bulk')), may hold values from -0.026 to 0.026
- coupling: float32 [64, 4, 128, 128], P(('group', 'bulk')), may hold values from -0.05 to 0.05, as said below
- col_index: int32 [128, 11], replicated, may hold values from 0 to 127, as said below
- load: int32 [128], replicated, may hold values from 3 to 11
- new_slot: int32 [128], replicated, may hold values from 0 to 127, as said below
Outputs:
- solution_out: float32 [128, 64, 128], P(('group', 'bulk'))
- residual_out: float32 [128, 64, 128], P(('group', 'bulk'))
The draws below stay inside these ranges and needn't reach their ends.
Inputs may be any that keep to these rules, and one draw needn't show every extreme that they name: `rhs`: made of random entries times scales of the rows and of the columns. `coupling`: entry [d * 2 + k, h] is the transpose of entry [(h * 8 + d % 8) * 2 + k, d // 8]. `col_index`: for each part g and each tile position t, the column t of the 32 block rows of part g is a permutation of that part's slots g * 32 to (g + 1) * 32 - 1. Of the 44 entries of the 4 block rows of one device (slots d * 4 to (d + 1) * 4 - 1), at most 6 name slots of any one device, and exactly 6 name slots of some device. `new_slot`: A permutation. On every device exactly one block row moves, from a slot k with 2 <= k % 4; it stays in its part, goes from owner b to owner b XOR m, where m (1 to 7) is one number for the whole part, and takes the slot that the moving row of that device leaves.
All inputs are finite; a program needn't handle non-finite values.
Results may differ from the reference program's by a relative error of at most 0.0003.
Values sent between devices are 32-bit elements; how exact they have to be, the bound alone decides.
No kernel may reach another device: no remote copies, remote signals or barrier semaphores. Data moves between devices by JAX's collectives and lax.ppermute only.
A program may use at most 64 MiB of HBM per device.

```python
import math
import jax
import jax.numpy as jnp
from jax import lax

TILE_ORDER = 128
RIGHT_HAND_COUNT = 64
OFFDIAG_TILES = 11
ROWS_DEV = 4
ITERS = 2
IFACE = 2
PART_BLOCK_ROWS = 32
TOTAL_BLOCK_ROWS = 128


def draw_rhs(key, part):
    noise_key, rows_key, key_cols = jax.random.split(key, 3)
    random_jitter = jnp.clip(jax.random.normal(noise_key, (TOTAL_BLOCK_ROWS, RIGHT_HAND_COUNT, TILE_ORDER), jnp.float32), -6.0, 6.0)
    row_history = jax.random.uniform(rows_key, (TOTAL_BLOCK_ROWS, 1, TILE_ORDER), jnp.float32, 0.0, math.log(10.0))
    col_log = jax.random.uniform(key_cols, (1, RIGHT_HAND_COUNT, 1), jnp.float32, 0.0, math.log(10.0))
    ascending_order = 1.0 + 2.0 * jnp.arange(TOTAL_BLOCK_ROWS, dtype=jnp.float32) / max(TOTAL_BLOCK_ROWS - 1, 1)
    return 0.03 * random_jitter * jnp.exp(row_history) * jnp.exp(col_log) * ascending_order[:, None, None]


def draw_diag_tiles(key, part):
    unsorted_draws = jax.random.uniform(key, (TOTAL_BLOCK_ROWS, TILE_ORDER, TILE_ORDER), jnp.float32, -0.06, 0.06)
    return 0.5 * (unsorted_draws + jnp.swapaxes(unsorted_draws, 1, 2))


def draw_coupling(key, part):
    part_count = TOTAL_BLOCK_ROWS // PART_BLOCK_ROWS
    boundary_rows = TOTAL_BLOCK_ROWS // 2 // part_count
    unsorted_draws = jax.random.uniform(key, (part_count, boundary_rows, part_count, TILE_ORDER, TILE_ORDER), jnp.float32, -0.03, 0.03)
    mirrored = jnp.swapaxes(jnp.transpose(unsorted_draws, (2, 1, 0, 3, 4)), 3, 4)
    joined = (unsorted_draws + mirrored) * 0.7071067811865476
    return joined.reshape(part_count * boundary_rows, part_count, TILE_ORDER, TILE_ORDER)


def draw_col_index(key, part):
    part_count = TOTAL_BLOCK_ROWS // PART_BLOCK_ROWS
    owner_count = PART_BLOCK_ROWS // ROWS_DEV
    read_count = OFFDIAG_TILES * ROWS_DEV
    key_off, key_row, key_shift = jax.random.split(key, 3)
    off_keys = jax.random.split(key_off, part_count)
    orders = jax.vmap(lambda one_key: jax.random.permutation(one_key, read_count))(off_keys).astype(jnp.int32)
    shifts = jax.random.randint(key_shift, (part_count, 1), 0, owner_count, dtype=jnp.int32)
    offsets = jnp.remainder(orders + shifts, owner_count).reshape(part_count, ROWS_DEV, OFFDIAG_TILES)
    row_keys = jax.random.split(key_row, part_count * OFFDIAG_TILES)
    row_perm = jax.vmap(lambda one_key: jax.random.permutation(one_key, ROWS_DEV))(row_keys).astype(jnp.int32)
    row_perm = jnp.transpose(row_perm.reshape(part_count, OFFDIAG_TILES, ROWS_DEV), (0, 2, 1))
    owners = jnp.arange(owner_count, dtype=jnp.int32)[None, :, None, None]
    target = jnp.remainder(owners + offsets[:, None], owner_count)
    bases = (jnp.arange(part_count, dtype=jnp.int32) * PART_BLOCK_ROWS)[:, None, None, None]
    column_ids = bases + target * ROWS_DEV + row_perm[:, None]
    return column_ids.reshape(TOTAL_BLOCK_ROWS, OFFDIAG_TILES).astype(jnp.int32)


def draw_new_slot(key, part):
    part_count = TOTAL_BLOCK_ROWS // PART_BLOCK_ROWS
    owner_count = PART_BLOCK_ROWS // ROWS_DEV
    device_count = part_count * owner_count
    key_mover, key_mask = jax.random.split(key, 2)
    mover = IFACE + jax.random.randint(key_mover, (device_count,), 0, ROWS_DEV - IFACE, dtype=jnp.int32)
    xor_vals = jax.random.randint(key_mask, (part_count,), 1, owner_count, dtype=jnp.int32)
    devices = jnp.arange(device_count, dtype=jnp.int32)
    group_of = devices // owner_count
    owner_of = devices % owner_count
    target_dev = group_of * owner_count + jnp.bitwise_xor(owner_of, xor_vals[group_of])
    source_rows = devices * ROWS_DEV + mover
    target_rows = target_dev * ROWS_DEV + mover[target_dev]
    return jnp.arange(TOTAL_BLOCK_ROWS, dtype=jnp.int32).at[source_rows].set(target_rows)


def place_ends(result, key, low, top_value):
    spot = [jax.random.randint(jax.random.fold_in(key, axis), (), 0, length) for axis, length in enumerate(result.shape)]
    main_axis = result.shape.index(max(result.shape))
    beside = spot[:main_axis] + [(spot[main_axis] + 1) % result.shape[main_axis]] + spot[main_axis + 1:]
    return result.at[tuple(spot)].set(low).at[tuple(beside)].set(top_value)


def steps_of(rng, dims, pieces, smallest, largest):
    gain, own = 1.0, jax.random.fold_in(rng, 6)
    for position, parts in pieces:
        steps = jnp.exp(jax.random.uniform(jax.random.fold_in(own, position), (parts,), jnp.float32, smallest / len(pieces), largest / len(pieces)))
        gain = gain * jnp.repeat(steps, dims[position] // parts).reshape([-1 if axis == position else 1 for axis in range(len(dims))])
    return gain


def setup_inputs(seed: int = 0) -> dict:
    key_of = jax.random.split(jax.random.key(seed), 8)
    return {
        "rhs": draw_rhs(jax.random.fold_in(key_of[7], 71), 0),
        "diag_tiles": draw_diag_tiles(jax.random.fold_in(key_of[7], 71), 0),
        "offdiag_blocks": jnp.clip(jax.random.uniform(key_of[2], (TOTAL_BLOCK_ROWS, OFFDIAG_TILES, TILE_ORDER, TILE_ORDER), jnp.float32, -0.026, 0.026) * steps_of(key_of[2], (TOTAL_BLOCK_ROWS, OFFDIAG_TILES, TILE_ORDER, TILE_ORDER), ((0, 32),), -0.4, 0.0), -0.026, 0.026),
        "coupling": draw_coupling(jax.random.fold_in(key_of[7], 71), 0),
        "col_index": draw_col_index(jax.random.fold_in(key_of[7], 71), 0),
        "load": place_ends(jax.random.randint(key_of[5], (TOTAL_BLOCK_ROWS,), 3, OFFDIAG_TILES + 1), jax.random.fold_in(key_of[5], 1), 3, OFFDIAG_TILES).astype(jnp.int32),
        "new_slot": draw_new_slot(jax.random.fold_in(key_of[7], 71), 0),
    }


highest = lax.Precision.HIGHEST

def chol_apply(matrix, right):
    factor = jnp.linalg.cholesky(matrix)
    middle = lax.linalg.triangular_solve(factor, right, left_side=True, lower=True)
    return lax.linalg.triangular_solve(factor, middle, left_side=True, lower=True, transpose_a=True)

def gram_of(left, right):
    total = jnp.einsum('snt,smt->nm', left, right, precision=highest)
    return 0.5 * (total + total.T)

def operate(vectors, diag_tiles, offdiag_blocks, coupling, col_index, load):
    mask = (jnp.arange(OFFDIAG_TILES)[None, :] < load[:, None]).astype(jnp.float32)
    final_output = 4.0 * vectors + jnp.einsum('snj,sij->sni', vectors, diag_tiles, precision=highest)
    for tile_pos in range(OFFDIAG_TILES):
        masked = offdiag_blocks[:, tile_pos] * mask[:, tile_pos, None, None]
        picked = vectors[col_index[:, tile_pos]]
        final_output = final_output + jnp.einsum('snj,sij->sni', picked, masked, precision=highest)
        returned = jnp.einsum('sni,sij->snj', vectors, masked, precision=highest)
        final_output = final_output.at[col_index[:, tile_pos]].add(returned)
    part_count = TOTAL_BLOCK_ROWS // PART_BLOCK_ROWS
    owner_count = PART_BLOCK_ROWS // ROWS_DEV
    shaped = vectors.reshape(part_count, owner_count, ROWS_DEV, RIGHT_HAND_COUNT, TILE_ORDER)
    border = shaped[:, :, :IFACE]
    tiles = coupling.reshape(part_count, owner_count, IFACE, part_count, TILE_ORDER, TILE_ORDER)
    crossed = jnp.einsum('gbkhij,hbknj->gbkni', tiles, border, precision=highest)
    final_output = final_output.reshape(part_count, owner_count, ROWS_DEV, RIGHT_HAND_COUNT, TILE_ORDER)
    final_output = final_output.at[:, :, :IFACE].add(crossed)
    return final_output.reshape(TOTAL_BLOCK_ROWS, RIGHT_HAND_COUNT, TILE_ORDER)

def reference(rhs, diag_tiles, offdiag_blocks, coupling, col_index, load, new_slot):
    solution = jnp.zeros_like(rhs)
    resid = rhs
    direction = rhs
    gram_rr = gram_of(resid, resid)
    for step_id in range(ITERS):
        image = operate(direction, diag_tiles, offdiag_blocks, coupling, col_index, load)
        gram_pq = gram_of(direction, image)
        alpha = chol_apply(gram_pq, gram_rr)
        solution = solution + jnp.einsum('mn,smt->snt', alpha, direction, precision=highest)
        resid = resid - jnp.einsum('mn,smt->snt', alpha, image, precision=highest)
        if step_id + 1 < ITERS:
            gram_new = gram_of(resid, resid)
            beta = chol_apply(gram_rr, gram_new)
            direction = resid + jnp.einsum('mn,smt->snt', beta, direction, precision=highest)
            gram_rr = gram_new
    solution_out = jnp.zeros_like(solution).at[new_slot].set(solution)
    residual_out = jnp.zeros_like(resid).at[new_slot].set(resid)
    return (solution_out, residual_out)
```

```python
import jax
import jax.numpy as jnp
from jax import lax
from jax.sharding import PartitionSpec as P

highest = lax.Precision.HIGHEST
diagonal_shift = 4.0


def from_partner(value, axis, bit):
    mask = 2**bit
    pairs = [(source, source ^ mask) for source in range(lax.axis_size(axis))]
    return lax.ppermute(value, axis, pairs)


def chol_apply(matrix, right):
    factor = jnp.linalg.cholesky(matrix)
    middle = lax.linalg.triangular_solve(factor, right, left_side=True, lower=True)
    return lax.linalg.triangular_solve(factor, middle, left_side=True, lower=True, transpose_a=True)


def mm(left, right):
    return jnp.dot(left, right, precision=highest)


def sym(matrix):
    return 0.5 * (matrix + matrix.T)


def partial_gram(left, right):
    return jnp.einsum("snt,smt->nm", left, right, precision=highest)


def operate(vectors, diag, masked, column_ids, coupling):
    row_count = vectors.shape[0]
    boundary_rows = coupling.shape[0]
    part_count = coupling.shape[1]
    group_rows = row_count * lax.axis_size("bulk")
    border = lax.all_gather(vectors[:boundary_rows], "group", axis=0, tiled=True)
    final_output = jnp.einsum("rnj,rij->rni", vectors, diag, precision=highest)
    returned = jnp.einsum("rni,rkij->rknj", vectors, masked, precision=highest)
    flat_terms = returned.reshape((-1,) + vectors.shape[1:])
    panel = lax.all_gather(vectors, "bulk", axis=0, tiled=True)
    buffer = jax.ops.segment_sum(flat_terms, column_ids.reshape(-1), num_segments=group_rows)
    owed = lax.psum_scatter(buffer, "bulk", scatter_dimension=0, tiled=True)
    picked = panel[column_ids]
    final_output = (
        final_output + jnp.einsum("rknj,rkij->rni", picked, masked, precision=highest) + owed
    )
    border = border.reshape((part_count, boundary_rows) + vectors.shape[1:])
    crossed = jnp.einsum("khij,hknj->kni", coupling, border, precision=highest)
    return final_output.at[:boundary_rows].add(crossed)


def combine(vectors, matrix):
    return jnp.einsum("mn,smt->snt", matrix, vectors, precision=highest)


def local(rhs, diag_tiles, offdiag_blocks, coupling, col_index, load, new_slot):
    row_count = rhs.shape[0]
    off_count = offdiag_blocks.shape[1]
    bulk_count = lax.axis_size("bulk")
    group_rows = row_count * bulk_count
    my_group = lax.axis_index("group")
    my_bulk = lax.axis_index("bulk")
    first_slot = (my_group * bulk_count + my_bulk) * row_count
    group_base = my_group * group_rows
    own_slots = first_slot + jnp.arange(row_count, dtype=jnp.int32)
    tile_ids = jnp.arange(off_count, dtype=jnp.int32)
    old_columns = col_index[own_slots] - group_base
    old_mask = (tile_ids[None, :] < load[own_slots][:, None]).astype(jnp.float32)
    old_masked = offdiag_blocks * old_mask[:, :, None, None]
    own_new = new_slot[own_slots]
    leaving = jnp.argmax((own_new != own_slots).astype(jnp.int32))
    target = own_new[leaving]
    target_bulk = target // row_count % bulk_count
    xor_mask = jnp.bitwise_xor(target_bulk, my_bulk)

    first = operate(rhs, diag_tiles, old_masked, old_columns, coupling)
    second = operate(first, diag_tiles, old_masked, old_columns, coupling)
    grams = jnp.stack(
        [
            partial_gram(rhs, rhs),
            partial_gram(rhs, first),
            partial_gram(first, first),
            partial_gram(first, second),
        ]
    )
    grams = lax.psum(grams, ("group", "bulk"))
    g0, g1, g2, g3 = (sym(grams[i]) for i in range(4))
    eye = jnp.eye(g0.shape[0], dtype=jnp.float32)
    a = chol_apply(diagonal_shift * g0 + g1, g0)
    m = eye - diagonal_shift * a
    cross = mm(m.T, mm(g1, a))
    g_new = sym(mm(m.T, mm(g0, m)) - cross - cross.T + mm(a.T, mm(g2, a)))
    b = chol_apply(g0, g_new)
    c = m + b
    cross = mm(c.T, mm(diagonal_shift * g1 + g2, a))
    g_pq = (
        mm(c.T, mm(diagonal_shift * g0 + g1, c))
        - cross
        - cross.T
        + mm(a.T, mm(diagonal_shift * g2 + g3, a))
    )
    a1 = chol_apply(sym(g_pq), g_new)
    aa1 = mm(a, a1)
    ca1 = mm(c, a1)
    solution = combine(rhs, a + ca1) - combine(first, aa1)
    resid = (
        combine(rhs, m - diagonal_shift * ca1)
        - combine(first, a + ca1 - diagonal_shift * aa1)
        + combine(second, aa1)
    )
    pieces = [solution[leaving], resid[leaving]]
    flat = jnp.concatenate([piece.reshape(-1) for piece in pieces])
    for bit_pos in range(bulk_count.bit_length() - 1):
        partner = from_partner(flat, "bulk", bit_pos)
        chosen = jnp.bitwise_and(jnp.right_shift(xor_mask, bit_pos), 1) == 1
        flat = jnp.where(chosen, partner, flat)
    outputs = []
    offset = 0
    for piece in pieces:
        outputs.append(flat[offset : offset + piece.size].reshape(piece.shape))
        offset = offset + piece.size
    return (solution.at[leaving].set(outputs[0]), resid.at[leaving].set(outputs[1]))


def solution(mesh):
    return jax.shard_map(
        local,
        mesh=mesh,
        in_specs=(
            P(("group", "bulk"), None, None),
            P(("group", "bulk"), None, None),
            P(("group", "bulk"), None, None, None),
            P(("group", "bulk"), None, None, None),
            P(),
            P(),
            P(),
        ),
        out_specs=(P(("group", "bulk"), None, None), P(("group", "bulk"), None, None)),
        check_vma=False,
    )
```

```python
import functools

import jax
import jax.numpy as jnp
from jax import lax
from jax.experimental import pallas as pl
from jax.experimental.pallas import tpu as pltpu
from jax.sharding import PartitionSpec as P

shift = 4.0
f32 = jnp.float32
bf16 = jnp.bfloat16
normal = (((1,), (0,)), ((), ()))
right_t = (((1,), (1,)), ((), ()))
left_t = (((0,), (0,)), ((), ()))
vmem = pl.BlockSpec(memory_space=pltpu.VMEM)
smem = pl.BlockSpec(memory_space=pltpu.SMEM)
vmem_bytes = 32 * 2**20


def params():
    return pltpu.CompilerParams(vmem_limit_bytes=vmem_bytes)


def swap(value, axis, mask):
    pairs = [(source, source ^ mask) for source in range(lax.axis_size(axis))]
    return lax.ppermute(value, axis, pairs)


def split(value):
    high = value.astype(bf16)
    return high, (value - high.astype(f32)).astype(bf16)


def dot16(left, right, dims):
    return lax.dot_general(left, right, dims, preferred_element_type=f32)


def dot32(left, right, dims=normal):
    return lax.dot_general(
        left, right, dims, preferred_element_type=f32, precision=lax.Precision.HIGHEST
    )


def split_rows(vectors):
    high, low = split(vectors)
    return jnp.concatenate([high, low], axis=0)


def times_tile(rows, tile, dims):
    count = rows.shape[0] // 2
    high, low = split(tile)
    both = dot16(rows, high, dims)
    return both[:count] + both[count:] + dot16(rows[:count], low, dims)


def pack(gram):
    half = gram.shape[0] // 2
    return jnp.concatenate([gram[:half], gram[half:]], axis=1)


def unpack(packed):
    half = packed.shape[1] // 2
    return jnp.concatenate([packed[:, :half], packed[:, half:]], axis=0)


def sym(gram):
    return 0.5 * (gram + gram.T)


def first_slot(row_count):
    device = lax.axis_index("group") * lax.axis_size("bulk") + lax.axis_index("bulk")
    return device * row_count


def live(load_ref, slot, tile):
    return jnp.where(tile < load_ref[slot], 1.0, 0.0)


def returned_kernel(bulk_count, moved, vectors, tiles, col, load, new_slot, *outs):
    row_count, count = vectors.shape[:2]
    me = lax.axis_index("bulk")
    base = lax.axis_index("group") * bulk_count * row_count
    total = outs[-1]
    s = pl.program_id(0)
    slot = first_slot(row_count) + s

    @pl.when(s == 0)
    def _():
        total[...] = jnp.zeros_like(total)

    rows = split_rows(vectors[s])
    for t in range(tiles.shape[1]):
        product = times_tile(rows, tiles[0, t], normal)
        target = col[slot, t]
        if moved:
            place = new_slot[target] - base
        else:
            target = target - base
            owner = target // row_count
            rel = owner ^ me
            order = (rel & 1) * (bulk_count // 2) + (rel >> 1)
            place = order * row_count + target - owner * row_count
        total[place] += live(load, slot, t) * product

    if not moved:

        @pl.when(s == row_count - 1)
        def _():
            half = total.shape[0] // 2
            outs[0][...] = total[:half]
            outs[1][...] = total[half:]


def returned(vectors, tiles, col, load, new_slot, bulk_count, moved):
    row_count, count, order = vectors.shape
    tile_count = tiles.shape[1]
    whole = (bulk_count * row_count, count, order)
    half = (bulk_count * row_count // 2, count, order)
    out_shapes = [whole] if moved else [half, half]
    return pl.pallas_call(
        functools.partial(returned_kernel, bulk_count, moved),
        grid=(row_count,),
        out_shape=[jax.ShapeDtypeStruct(shape, f32) for shape in out_shapes],
        in_specs=[
            vmem,
            pl.BlockSpec((1, tile_count, order, order), lambda s: (s, 0, 0, 0)),
            smem,
            smem,
            smem,
        ],
        out_specs=[vmem for _ in out_shapes],
        scratch_shapes=[] if moved else [pltpu.VMEM(whole, f32)],
        compiler_params=params(),
        name="returned_moved" if moved else "returned",
    )(vectors, tiles, col, load, new_slot)


def near_kernel(bulk_count, pieces, second, *refs):
    refs = list(refs)
    panel = [refs.pop(0) for _ in range(pieces)]
    vectors, tiles, diag, coupling = refs[:4]
    part_count = coupling.shape[1]
    border = refs[4 : 3 + part_count]
    col, load, new_slot, near, moving, extra, rows_of, gram = refs[3 + part_count :]
    row_count, count, order = near.shape[0], near.shape[1], near.shape[2]
    row_count = vectors.shape[0] if not second else row_count
    me = lax.axis_index("bulk")
    mine = lax.axis_index("group")
    base = mine * bulk_count * row_count
    s = pl.program_id(0)
    slot = first_slot(row_count) + s
    per_piece = bulk_count * row_count // pieces

    def place_of(target):
        target = target - base
        owner = target // row_count
        if second:
            return (owner ^ me) * row_count + target - owner * row_count
        return target

    @pl.when(s == 0)
    def _():
        for index, piece in enumerate(panel):
            for k in range(per_piece):
                value = piece[k * count : (k + 1) * count] if second else piece[k]
                rows_of[index * per_piece + k] = split_rows(value)
        gram[...] = jnp.zeros_like(gram)

    def own(k):
        return vectors[k]

    direct = None
    for t in range(tiles.shape[1]):
        rows = rows_of[place_of(col[slot, t])]
        high, low = split(tiles[0, t])
        alive = live(load, slot, t)
        both = alive * dot16(rows, high, right_t)
        rest = alive * dot16(rows[:count], low, right_t)
        direct = (both, rest) if direct is None else (direct[0] + both, direct[1] + rest)
    direct = direct[0][:count] + direct[0][count:] + direct[1]
    value = vectors[s]
    near_value = times_tile(split_rows(value), diag[0], right_t)
    near[s] = near_value + direct
    if second:
        gram[...] += dot32(value, near_value + 2.0 * direct, right_t)
    else:
        gram[...] += dot32(value, value, right_t)

    @pl.when(s < coupling.shape[0])
    def _():
        k = jnp.minimum(s, coupling.shape[0] - 1)
        crossed = times_tile(split_rows(value), coupling[k, mine], right_t)
        for index, ref in enumerate(border):
            tile = coupling[k, mine ^ (index + 1)]
            crossed = crossed + times_tile(split_rows(ref[k]), tile, right_t)
        near[s] += crossed
        if second:
            gram[...] += dot32(value, crossed, right_t)

    arriving = new_slot[slot]
    if second:
        incoming = place_of(arriving)
        for index, piece in enumerate(panel):

            @pl.when(incoming // row_count == index)
            def _(piece=piece):
                start = pl.multiple_of(incoming % row_count * count, count)
                moving[s] = piece[pl.ds(start, count)]

        @pl.when(arriving != slot)
        def _():
            extra[count // 2 :] = near[s]

    else:
        moving[s] = panel[0][place_of(arriving)]

    @pl.when(s == row_count - 1)
    def _():
        extra[: count // 2] = pack(gram[...])


def near_part(panel, vectors, tiles, diag, coupling, border, col, load, new_slot, bulk_count, second):
    row_count, count, order = vectors.shape
    tile_count = tiles.shape[1]
    extra_rows = count // 2 + (count if second else 0)
    shapes = [vectors.shape, vectors.shape, (extra_rows, order)]
    return pl.pallas_call(
        functools.partial(near_kernel, bulk_count, len(panel), second),
        grid=(row_count,),
        out_shape=[jax.ShapeDtypeStruct(shape, f32) for shape in shapes],
        in_specs=[vmem] * len(panel)
        + [
            vmem,
            pl.BlockSpec((1, tile_count, order, order), lambda s: (s, 0, 0, 0)),
            pl.BlockSpec((1, order, order), lambda s: (s, 0, 0)),
            vmem,
        ]
        + [vmem] * len(border)
        + [smem] * 3,
        out_specs=[vmem] * 3,
        scratch_shapes=[
            pltpu.VMEM((bulk_count * row_count, 2 * count, order), bf16),
            pltpu.VMEM((count, count), f32),
        ],
        compiler_params=params(),
        name="near_second" if second else "near_first",
    )(*panel, vectors, tiles, diag, coupling, *border, col, load, new_slot)


def gather_first_kernel(vectors, near, keep, *refs):
    received = refs[:-4]
    packed, first, flat, edge = refs[-4:]
    row_count, count = vectors.shape[:2]
    grams = [None, None]
    for k in range(row_count):
        value = near[k] + keep[k]
        for ref in received:
            value = value + ref[k]
        first[k] = value
        flat[k * count : (k + 1) * count] = value
        if k < edge.shape[0]:
            edge[k] = value
        terms = (dot32(vectors[k], value, right_t), dot32(value, value, right_t))
        grams = [term if old is None else old + term for old, term in zip(grams, terms)]
    start = row_count * count
    half = count // 2
    flat[start : start + half] = packed[...]
    flat[start + half : start + 2 * half] = pack(grams[0])
    flat[start + 2 * half :] = pack(grams[1])


def gather_first(vectors, near, keep, received, packed, edge_rows):
    row_count, count, order = vectors.shape
    shapes = [
        vectors.shape,
        (row_count * count + 3 * (count // 2), order),
        (edge_rows, count, order),
    ]
    specs = [pl.BlockSpec((row_count, count, order), lambda s: (0, 0, 0))] * (3 + len(received))
    return pl.pallas_call(
        gather_first_kernel,
        grid=(1,),
        out_shape=[jax.ShapeDtypeStruct(shape, f32) for shape in shapes],
        in_specs=specs + [vmem],
        out_specs=[vmem] * 3,
        compiler_params=params(),
        name="gather_first",
    )(vectors, near, keep, *received, packed)


def inverse_factors(matrices):
    count = matrices[0].shape[0]
    blocks = count // 8
    row_ids = lax.broadcasted_iota(jnp.int32, (count, count), 0)
    col_ids = lax.broadcasted_iota(jnp.int32, (count, count), 1)
    eye = (row_ids == col_ids).astype(f32)
    sub = lax.broadcasted_iota(jnp.int32, (8, 2 * count), 0)
    work = []
    for matrix in matrices:
        both = jnp.concatenate([matrix, eye], axis=1)
        work.append([both[8 * i : 8 * i + 8] for i in range(blocks)])
    for j in range(count):
        block, k = divmod(j, 8)
        for w in work:
            row = w[block][k : k + 1]
            scale = lax.rsqrt(row[:, j : j + 1])
            pivot = row * scale
            for i in range(block, blocks):
                changed = w[i] - w[i][:, j : j + 1] * scale * pivot
                if i == block:
                    changed = jnp.where(sub > k, changed, jnp.where(sub == k, pivot, w[i]))
                w[i] = changed
    return [jnp.concatenate(w, axis=0)[:, count:] for w in work]


def solve(inverse_factor, right):
    return dot32(inverse_factor, dot32(inverse_factor, right), left_t)


def early_kernel(packed, out):
    count = out.shape[1]
    half = count // 2
    g0, g1, g2 = (sym(unpack(packed[i * half : (i + 1) * half])) for i in range(3))
    eye = (
        lax.broadcasted_iota(jnp.int32, (count, count), 0)
        == lax.broadcasted_iota(jnp.int32, (count, count), 1)
    ).astype(f32)
    factor_pq, factor_rr = inverse_factors([shift * g0 + g1, g0])
    a = solve(factor_pq, g0)
    m = eye - shift * a
    cross = dot32(m, dot32(g1, a), left_t)
    g_new = dot32(m, dot32(g0, m), left_t) - cross - cross.T + dot32(a, dot32(g2, a), left_t)
    g_new = sym(g_new)
    c = m + solve(factor_rr, g_new)
    cross = dot32(c, dot32(shift * g1 + g2, a), left_t)
    g_pq = dot32(c, dot32(shift * g0 + g1, c), left_t) - cross - cross.T
    out[0] = a
    out[1] = c
    out[2] = g_new
    out[3] = g_pq + shift * dot32(a, dot32(g2, a), left_t)


def early(packed, count):
    return pl.pallas_call(
        early_kernel,
        out_shape=jax.ShapeDtypeStruct((4, count, count), f32),
        in_specs=[vmem],
        out_specs=vmem,
        compiler_params=params(),
        name="early_solves",
    )(packed)


def final_kernel(packed, small, moving, first, near, row, owed, new_slot, solution, resid):
    row_count, count = moving.shape[:2]
    a, c, g_new, g_pq = (small[i] for i in range(4))
    g3 = sym(unpack(packed[...]))
    g_pq = sym(g_pq + dot32(a, dot32(g3, a), left_t))
    (factor,) = inverse_factors([g_pq])
    a1 = solve(factor, g_new)
    aa1 = dot32(a, a1)
    ca1 = dot32(c, a1)
    eye = (
        lax.broadcasted_iota(jnp.int32, (count, count), 0)
        == lax.broadcasted_iota(jnp.int32, (count, count), 1)
    ).astype(f32)
    m = eye - shift * a
    zero = jnp.zeros_like(a)
    top = jnp.concatenate([a + ca1, -aa1, zero], axis=0)
    low = jnp.concatenate([m - shift * ca1, shift * aa1 - a - ca1, aa1], axis=0)
    coef = jnp.concatenate([top, low], axis=1)
    slot = first_slot(row_count)
    for k in range(row_count):
        stays = new_slot[slot + k] == slot + k
        second = jnp.where(stays, near[k], row[...]) + owed[k]
        basis = jnp.concatenate([moving[k], first[k], second], axis=0)
        both = dot32(coef, basis, left_t)
        solution[k] = both[:count]
        resid[k] = both[count:]


def final(packed, small, moving, first, near, row, owed, new_slot):
    return pl.pallas_call(
        final_kernel,
        out_shape=[jax.ShapeDtypeStruct(near.shape, f32)] * 2,
        in_specs=[vmem] * 7 + [smem],
        out_specs=[vmem] * 2,
        compiler_params=params(),
        name="final",
    )(packed, small, moving, first, near, row, owed, new_slot)


def local(rhs, diag_tiles, offdiag_blocks, coupling, col_index, load, new_slot):
    row_count, count, order = rhs.shape
    edge_rows, part_count = coupling.shape[:2]
    bulk_count = lax.axis_size("bulk")
    half = count // 2
    my_bulk = lax.axis_index("bulk")
    slot = first_slot(row_count)
    own_new = lax.dynamic_slice(new_slot, (slot,), (row_count,))
    own_slots = slot + jnp.arange(row_count, dtype=jnp.int32)
    target = jnp.max(jnp.where(own_new != own_slots, own_new, -1))
    xor_mask = (target // row_count % bulk_count) ^ my_bulk

    keep, send = returned(rhs, offdiag_blocks, col_index, load, new_slot, bulk_count, False)
    panel = lax.all_gather(rhs, "bulk", axis=0, tiled=True)
    border = [swap(rhs[:edge_rows], "group", mask) for mask in range(1, part_count)]
    from_core = swap(send, "bulk", 1)
    received = [from_core]
    for z in range(1, bulk_count // 2):
        rows = slice(z * row_count, (z + 1) * row_count)
        received.append(swap(keep[rows] + from_core[rows], "bulk", 2 * z))
    near, moving, packed = near_part(
        [panel], rhs, offdiag_blocks, diag_tiles, coupling, border, col_index, load, new_slot,
        bulk_count, False,
    )
    first, flat, edge = gather_first(rhs, near, keep, received, packed, edge_rows)

    far = [swap(flat, "bulk", 2 * z) for z in range(1, bulk_count // 2)]
    border = [swap(edge, "group", mask) for mask in range(1, part_count)]
    (owed,) = returned(first, offdiag_blocks, col_index, load, new_slot, bulk_count, True)
    owed = lax.psum_scatter(owed, "bulk", scatter_dimension=0, tiled=True)
    panel = []
    for piece in [flat] + far:
        panel += [piece, swap(piece, "bulk", 1)]
    grams = sum(piece[row_count * count :] for piece in panel)
    mask = 1
    while mask < part_count:
        grams = grams + swap(grams, "group", mask)
        mask *= 2
    near, first, extra = near_part(
        panel, first, offdiag_blocks, diag_tiles, coupling, border, col_index, load, new_slot,
        bulk_count, True,
    )
    small = early(grams, count)

    is_gram = lax.broadcasted_iota(jnp.int32, extra.shape, 0) < half
    mask = 1
    while mask < bulk_count:
        partner = swap(extra, "bulk", mask)
        chosen = jnp.bitwise_and(xor_mask, mask) != 0
        extra = jnp.where(is_gram, extra + partner, jnp.where(chosen, partner, extra))
        mask *= 2
    gram, row = extra[:half], extra[half:]
    mask = 1
    while mask < part_count:
        gram = gram + swap(gram, "group", mask)
        mask *= 2
    return tuple(final(gram, small, moving, first, near, row, owed, new_slot))


def solution(mesh):
    rows = P(("group", "bulk"))
    return jax.shard_map(
        local,
        mesh=mesh,
        in_specs=(rows, rows, rows, rows, P(), P(), P()),
        out_specs=(rows, rows),
        check_vma=False,
    )
```

```python
import functools

import jax
import jax.numpy as jnp
from jax import lax
from jax.experimental import pallas as pl
from jax.experimental.pallas import tpu as pltpu
from jax.sharding import PartitionSpec as P

shift = 4.0
f32 = jnp.float32
bf16 = jnp.bfloat16
normal = (((1,), (0,)), ((), ()))
right_t = (((1,), (1,)), ((), ()))
left_t = (((0,), (0,)), ((), ()))
vmem = pl.BlockSpec(memory_space=pltpu.VMEM)
smem = pl.BlockSpec(memory_space=pltpu.SMEM)
vmem_bytes = 60 * 2**20


def params():
    return pltpu.CompilerParams(vmem_limit_bytes=vmem_bytes)


def swap(value, axis, mask):
    pairs = [(source, source ^ mask) for source in range(lax.axis_size(axis))]
    return lax.ppermute(value, axis, pairs)


def split(value):
    high = value.astype(bf16)
    return high, (value - high.astype(f32)).astype(bf16)


def dot16(left, right, dims):
    return lax.dot_general(left, right, dims, preferred_element_type=f32)


def dot32(left, right, dims=normal):
    return lax.dot_general(
        left, right, dims, preferred_element_type=f32, precision=lax.Precision.HIGHEST
    )


def split_rows(vectors):
    high, low = split(vectors)
    return jnp.concatenate([high, low], axis=0)


def times_tile(rows, tile, dims):
    count = rows.shape[0] // 2
    high, low = split(tile)
    both = dot16(rows, high, dims)
    return both[:count] + both[count:] + dot16(rows[:count], low, dims)


def pack(gram):
    half = gram.shape[0] // 2
    return jnp.concatenate([gram[:half], gram[half:]], axis=1)


def unpack(packed):
    half = packed.shape[1] // 2
    return jnp.concatenate([packed[:, :half], packed[:, half:]], axis=0)


def sym(gram):
    return 0.5 * (gram + gram.T)


def first_slot(row_count):
    device = lax.axis_index("group") * lax.axis_size("bulk") + lax.axis_index("bulk")
    return device * row_count


def live(load_ref, slot, tile):
    return jnp.where(tile < load_ref[slot], 1.0, 0.0)


def returned_kernel(bulk_count, moved, vectors, tiles, col, load, new_slot, keep, send, total):
    row_count = vectors.shape[0]
    me = lax.axis_index("bulk")
    base = lax.axis_index("group") * bulk_count * row_count
    s = pl.program_id(0)
    slot = first_slot(row_count) + s

    @pl.when(s == 0)
    def _():
        total[...] = jnp.zeros_like(total)

    rows = split_rows(vectors[s])
    for t in range(tiles.shape[1]):
        product = times_tile(rows, tiles[0, t], normal)
        target = col[t, slot]
        if moved:
            target = new_slot[target]
        target = target - base
        owner = target // row_count
        rel = owner ^ me
        order = (rel & 1) * (bulk_count // 2) + (rel >> 1)
        place = order * row_count + target - owner * row_count
        total[place] += live(load, slot, t) * product

    @pl.when(s == row_count - 1)
    def _():
        half = total.shape[0] // 2
        keep[...] = total[:half]
        send[...] = total[half:]


def returned(vectors, tiles, col, load, new_slot, bulk_count, moved):
    row_count, count, order = vectors.shape
    tile_count = tiles.shape[1]
    half = (bulk_count * row_count // 2, count, order)
    return pl.pallas_call(
        functools.partial(returned_kernel, bulk_count, moved),
        grid=(row_count,),
        out_shape=[jax.ShapeDtypeStruct(half, f32)] * 2,
        in_specs=[
            vmem,
            pl.BlockSpec((1, tile_count, order, order), lambda s: (s, 0, 0, 0)),
            smem,
            smem,
            smem,
        ],
        out_specs=[vmem] * 2,
        scratch_shapes=[pltpu.VMEM((2 * half[0], count, order), f32)],
        compiler_params=params(),
        name="returned_moved" if moved else "returned",
    )(vectors, tiles, col, load, new_slot)


def near_kernel(bulk_count, second, *refs):
    panel, refs = refs[:bulk_count], refs[bulk_count:]
    vectors, tiles, diag, coupling = refs[:4]
    edge_rows, part_count = coupling.shape[:2]
    border, refs = refs[4 : 3 + part_count], refs[3 + part_count :]
    col, load, new_slot, near, moving, gram_out, *more, rows_of, gram = refs
    row_count, count = vectors.shape[:2]
    me = lax.axis_index("bulk")
    mine = lax.axis_index("group")
    base = mine * bulk_count * row_count
    s = pl.program_id(0)
    slot = first_slot(row_count) + s

    def place_of(target):
        target = target - base
        owner = target // row_count
        return (owner ^ me) * row_count + target - owner * row_count

    @pl.when(s == 0)
    def _():
        for index, piece in enumerate(panel):
            for k in range(row_count):
                rows_of[index * row_count + k] = split_rows(piece[k * count : (k + 1) * count])
        gram[...] = jnp.zeros_like(gram)
        if second:
            tail = panel[0][row_count * count :]
            for piece in panel[1:]:
                tail = tail + piece[row_count * count :]
            gram_out[count // 2 :] = tail

    direct = None
    for t in range(tiles.shape[1]):
        rows = rows_of[place_of(col[t, slot])]
        high, low = split(tiles[0, t])
        alive = live(load, slot, t)
        both = alive * dot16(rows, high, right_t)
        rest = alive * dot16(rows[:count], low, right_t)
        direct = (both, rest) if direct is None else (direct[0] + both, direct[1] + rest)
    direct = direct[0][:count] + direct[0][count:] + direct[1]
    value = vectors[s]
    near_value = times_tile(split_rows(value), diag[0], right_t)
    near[s] = near_value + direct
    if second:
        gram[...] += dot32(value, near_value + 2.0 * direct, right_t)
    else:
        gram[...] += dot32(value, value, right_t)

    @pl.when(s < edge_rows)
    def _():
        k = jnp.minimum(s, edge_rows - 1)
        crossed = times_tile(split_rows(value), coupling[k, mine], right_t)
        for index, ref in enumerate(border):
            tile = coupling[k, mine ^ (index + 1)]
            crossed = crossed + times_tile(split_rows(ref[k]), tile, right_t)
        near[s] += crossed
        if second:
            gram[...] += dot32(value, crossed, right_t)

    arriving = new_slot[slot]
    incoming = place_of(arriving)
    for index, piece in enumerate(panel):

        @pl.when(incoming // row_count == index)
        def _(piece=piece):
            start = pl.multiple_of(incoming % row_count * count, count)
            moving[s] = piece[pl.ds(start, count)]

    if second:
        (leaving,) = more

        @pl.when(arriving != slot)
        def _():
            leaving[count // 2 :] = near[s]

    @pl.when(s == row_count - 1)
    def _():
        if second:
            leaving[: count // 2] = pack(gram[...])
        else:
            gram_out[...] = pack(gram[...])


def near_part(panel, vectors, tiles, diag, coupling, border, col, load, new_slot, second):
    row_count, count, order = vectors.shape
    bulk_count = len(panel)
    tile_count = tiles.shape[1]
    half = count // 2
    shapes = [vectors.shape, vectors.shape, (half, order)]
    if second:
        shapes = [vectors.shape, vectors.shape, (4 * half, order), (half + count, order)]
    return pl.pallas_call(
        functools.partial(near_kernel, bulk_count, second),
        grid=(row_count,),
        out_shape=[jax.ShapeDtypeStruct(shape, f32) for shape in shapes],
        in_specs=[vmem] * bulk_count
        + [
            vmem,
            pl.BlockSpec((1, tile_count, order, order), lambda s: (s, 0, 0, 0)),
            pl.BlockSpec((1, order, order), lambda s: (s, 0, 0)),
            vmem,
        ]
        + [vmem] * len(border)
        + [smem] * 3,
        out_specs=[vmem] * len(shapes),
        scratch_shapes=[
            pltpu.VMEM((bulk_count * row_count, 2 * count, order), bf16),
            pltpu.VMEM((count, count), f32),
        ],
        compiler_params=params(),
        name="near_second" if second else "near_first",
    )(*panel, vectors, tiles, diag, coupling, *border, col, load, new_slot)


def gather_first_kernel(vectors, near, keep, *refs):
    received = refs[:-4]
    packed, first, flat, edge = refs[-4:]
    row_count, count = vectors.shape[:2]
    grams = [None, None]
    for k in range(row_count):
        value = near[k] + keep[k]
        for ref in received:
            value = value + ref[k]
        first[k] = value
        flat[k * count : (k + 1) * count] = value
        if k < edge.shape[0]:
            edge[k] = value
        terms = (dot32(vectors[k], value, right_t), dot32(value, value, right_t))
        grams = [term if old is None else old + term for old, term in zip(grams, terms)]
    start = row_count * count
    half = count // 2
    flat[start : start + half] = packed[...]
    flat[start + half : start + 2 * half] = pack(grams[0])
    flat[start + 2 * half :] = pack(grams[1])


def gather_first(vectors, near, keep, received, packed, edge_rows):
    row_count, count, order = vectors.shape
    shapes = [
        vectors.shape,
        (row_count * count + 3 * (count // 2), order),
        (edge_rows, count, order),
    ]
    specs = [pl.BlockSpec((row_count, count, order), lambda s: (0, 0, 0))] * (3 + len(received))
    return pl.pallas_call(
        gather_first_kernel,
        grid=(1,),
        out_shape=[jax.ShapeDtypeStruct(shape, f32) for shape in shapes],
        in_specs=specs + [vmem],
        out_specs=[vmem] * 3,
        compiler_params=params(),
        name="gather_first",
    )(vectors, near, keep, *received, packed)


def inverse_factors(matrices):
    count = matrices[0].shape[0]
    blocks = count // 8
    row_ids = lax.broadcasted_iota(jnp.int32, (count, count), 0)
    col_ids = lax.broadcasted_iota(jnp.int32, (count, count), 1)
    eye = (row_ids == col_ids).astype(f32)
    sub = lax.broadcasted_iota(jnp.int32, (8, 2 * count), 0)
    work = []
    for matrix in matrices:
        both = jnp.concatenate([matrix, eye], axis=1)
        work.append([both[8 * i : 8 * i + 8] for i in range(blocks)])
    for j in range(count):
        block, k = divmod(j, 8)
        for w in work:
            row = w[block][k : k + 1]
            scale = lax.rsqrt(row[:, j : j + 1])
            pivot = row * scale
            for i in range(block, blocks):
                changed = w[i] - w[i][:, j : j + 1] * scale * pivot
                if i == block:
                    changed = jnp.where(sub > k, changed, jnp.where(sub == k, pivot, w[i]))
                w[i] = changed
    return [jnp.concatenate(w, axis=0)[:, count:] for w in work]


def solve(inverse_factor, right):
    return dot32(inverse_factor, dot32(inverse_factor, right), left_t)


def final_kernel(packed, moving, first, near, row, new_slot, keep, *refs):
    received, (solution, resid) = refs[:-2], refs[-2:]
    row_count, count = moving.shape[:2]
    half = count // 2
    grams = [unpack(packed[i * half : (i + 1) * half]) for i in range(4)]
    g3, g0, g1, g2 = (sym(gram) for gram in grams)
    eye = (
        lax.broadcasted_iota(jnp.int32, (count, count), 0)
        == lax.broadcasted_iota(jnp.int32, (count, count), 1)
    ).astype(f32)
    factor_pq, factor_rr = inverse_factors([shift * g0 + g1, g0])
    a = solve(factor_pq, g0)
    m = eye - shift * a
    g2a = dot32(g2, a)
    cross = dot32(m, dot32(g1, a), left_t)
    g_new = dot32(m, dot32(g0, m), left_t) - cross - cross.T + dot32(a, g2a, left_t)
    g_new = sym(g_new)
    c = m + solve(factor_rr, g_new)
    cross = dot32(c, shift * dot32(g1, a) + g2a, left_t)
    g_pq = dot32(c, dot32(shift * g0 + g1, c), left_t) - cross - cross.T
    g_pq = sym(g_pq + dot32(a, shift * g2a + dot32(g3, a), left_t))
    (factor,) = inverse_factors([g_pq])
    a1 = solve(factor, g_new)
    aa1 = dot32(a, a1)
    ca1 = dot32(c, a1)
    zero = jnp.zeros_like(a)
    top = jnp.concatenate([a + ca1, -aa1, zero], axis=0)
    low = jnp.concatenate([m - shift * ca1, shift * aa1 - a - ca1, aa1], axis=0)
    coef = jnp.concatenate([top, low], axis=1)
    slot = first_slot(row_count)
    for k in range(row_count):
        stays = new_slot[slot + k] == slot + k
        second = jnp.where(stays, near[k], row[half:]) + keep[k]
        for ref in received:
            second = second + ref[k]
        basis = jnp.concatenate([moving[k], first[k], second], axis=0)
        both = dot32(coef, basis, left_t)
        solution[k] = both[:count]
        resid[k] = both[count:]


def final(packed, moving, first, near, row, new_slot, keep, received):
    block = pl.BlockSpec(near.shape, lambda s: (0, 0, 0))
    return pl.pallas_call(
        final_kernel,
        grid=(1,),
        out_shape=[jax.ShapeDtypeStruct(near.shape, f32)] * 2,
        in_specs=[vmem] * 5 + [smem] + [block] * (1 + len(received)),
        out_specs=[vmem] * 2,
        compiler_params=params(),
        name="final",
    )(packed, moving, first, near, row, new_slot, keep, *received)


def spread(piece, bulk_count):
    pieces = [piece] + [swap(piece, "bulk", 2 * z) for z in range(1, bulk_count // 2)]
    return [own for piece in pieces for own in (piece, swap(piece, "bulk", 1))]


def give_back(keep, send, row_count, bulk_count):
    from_core = swap(send, "bulk", 1)
    received = [from_core]
    for z in range(1, bulk_count // 2):
        rows = slice(z * row_count, (z + 1) * row_count)
        received.append(swap(keep[rows] + from_core[rows], "bulk", 2 * z))
    return received


def local(rhs, diag_tiles, offdiag_blocks, coupling, col_index, load, new_slot):
    row_count, count, order = rhs.shape
    edge_rows, part_count = coupling.shape[:2]
    bulk_count = lax.axis_size("bulk")
    half = count // 2
    my_bulk = lax.axis_index("bulk")
    slot = first_slot(row_count)
    col = col_index.T
    own_new = lax.dynamic_slice(new_slot, (slot,), (row_count,))
    own_slots = slot + jnp.arange(row_count, dtype=jnp.int32)
    target = jnp.max(jnp.where(own_new != own_slots, own_new, -1))
    xor_mask = (target // row_count % bulk_count) ^ my_bulk

    panel = spread(rhs.reshape(row_count * count, order), bulk_count)
    border = [swap(rhs[:edge_rows], "group", mask) for mask in range(1, part_count)]
    keep, send = returned(rhs, offdiag_blocks, col, load, new_slot, bulk_count, False)
    received = give_back(keep, send, row_count, bulk_count)
    near, moving, packed = near_part(
        panel, rhs, offdiag_blocks, diag_tiles, coupling, border, col, load, new_slot, False
    )
    first, flat, edge = gather_first(rhs, near, keep, received, packed, edge_rows)

    panel = spread(flat, bulk_count)
    border = [swap(edge, "group", mask) for mask in range(1, part_count)]
    keep, send = returned(first, offdiag_blocks, col, load, new_slot, bulk_count, True)
    received = give_back(keep, send, row_count, bulk_count)
    near, first, grams, leaving = near_part(
        panel, first, offdiag_blocks, diag_tiles, coupling, border, col, load, new_slot, True
    )

    is_gram = lax.broadcasted_iota(jnp.int32, leaving.shape, 0) < half
    mask = 1
    while mask < bulk_count:
        partner = swap(leaving, "bulk", mask)
        chosen = jnp.bitwise_and(xor_mask, mask) != 0
        leaving = jnp.where(is_gram, leaving + partner, jnp.where(chosen, partner, leaving))
        mask *= 2
    grams = jnp.concatenate([leaving[:half], grams[half:]], axis=0)
    mask = 1
    while mask < part_count:
        grams = grams + swap(grams, "group", mask)
        mask *= 2
    return tuple(final(grams, moving, first, near, leaving, new_slot, keep, received))


def solution(mesh):
    rows = P(("group", "bulk"))
    return jax.shard_map(
        local,
        mesh=mesh,
        in_specs=(rows, rows, rows, rows, P(), P(), P()),
        out_specs=(rows, rows),
        check_vma=False,
    )
```

```python
import functools

import jax
import jax.numpy as jnp
from jax import lax
from jax.experimental import pallas as pl
from jax.experimental.pallas import tpu as pltpu
from jax.sharding import PartitionSpec as P

shift = 4.0
f32 = jnp.float32
bf16 = jnp.bfloat16
normal = (((1,), (0,)), ((), ()))
right_t = (((1,), (1,)), ((), ()))
left_t = (((0,), (0,)), ((), ()))
vmem = pl.BlockSpec(memory_space=pltpu.VMEM)
smem = pl.BlockSpec(memory_space=pltpu.SMEM)
vmem_bytes = 40 * 2**20
all_vmem = 60 * 2**20


def params(limit=vmem_bytes):
    return pltpu.CompilerParams(vmem_limit_bytes=limit)


def swap(value, axis, mask):
    pairs = [(source, source ^ mask) for source in range(lax.axis_size(axis))]
    return lax.ppermute(value, axis, pairs)


def split(value):
    high = value.astype(bf16)
    return high, (value - high.astype(f32)).astype(bf16)


def dot16(left, right, dims):
    return lax.dot_general(left, right, dims, preferred_element_type=f32)


def dot32(left, right, dims=normal):
    return lax.dot_general(
        left, right, dims, preferred_element_type=f32, precision=lax.Precision.HIGHEST
    )


def split_rows(vectors):
    high, low = split(vectors)
    return jnp.concatenate([high, low], axis=0)


def times_tile(rows, tile, dims):
    count = rows.shape[0] // 2
    high, low = split(tile)
    both = dot16(rows, high, dims)
    return both[:count] + both[count:] + dot16(rows[:count], low, dims)


def pack(gram):
    half = gram.shape[0] // 2
    return jnp.concatenate([gram[:half], gram[half:]], axis=1)


def unpack(packed):
    half = packed.shape[1] // 2
    return jnp.concatenate([packed[:, :half], packed[:, half:]], axis=0)


def sym(gram):
    return 0.5 * (gram + gram.T)


def first_slot(row_count):
    device = lax.axis_index("group") * lax.axis_size("bulk") + lax.axis_index("bulk")
    return device * row_count


def live(load_ref, slot, tile):
    return jnp.where(tile < load_ref[slot], 1.0, 0.0)


def returned_kernel(bulk_count, moved, vectors, tiles, col, load, new_slot, keep, send, total):
    row_count = vectors.shape[0]
    me = lax.axis_index("bulk")
    base = lax.axis_index("group") * bulk_count * row_count
    s = pl.program_id(0)
    slot = first_slot(row_count) + s

    @pl.when(s == 0)
    def _():
        total[...] = jnp.zeros_like(total)

    rows = split_rows(vectors[s])
    for t in range(tiles.shape[1]):
        product = times_tile(rows, tiles[0, t], normal)
        target = col[t, slot]
        if moved:
            target = new_slot[target]
        target = target - base
        owner = target // row_count
        rel = owner ^ me
        order = (rel & 1) * (bulk_count // 2) + (rel >> 1)
        place = order * row_count + target - owner * row_count
        total[place] += live(load, slot, t) * product

    @pl.when(s == row_count - 1)
    def _():
        half = total.shape[0] // 2
        keep[...] = total[:half]
        send[...] = total[half:]


def returned(vectors, tiles, col, load, new_slot, bulk_count, moved):
    row_count, count, order = vectors.shape
    tile_count = tiles.shape[1]
    half = (bulk_count * row_count // 2, count, order)
    return pl.pallas_call(
        functools.partial(returned_kernel, bulk_count, moved),
        grid=(row_count,),
        out_shape=[jax.ShapeDtypeStruct(half, f32)] * 2,
        in_specs=[
            vmem,
            pl.BlockSpec((1, tile_count, order, order), lambda s: (s, 0, 0, 0)),
            smem,
            smem,
            smem,
        ],
        out_specs=[vmem] * 2,
        scratch_shapes=[pltpu.VMEM((2 * half[0], count, order), f32)],
        compiler_params=params(vmem_bytes if moved else all_vmem),
        name="returned_moved" if moved else "returned",
    )(vectors, tiles, col, load, new_slot)


def near_kernel(bulk_count, second, *refs):
    panel, refs = refs[:bulk_count], refs[bulk_count:]
    vectors, tiles, diag, coupling, sides, other_sides, col, load, new_slot, near, moving = refs[:11]
    extra, *more, rows_of, gram = refs[11:]
    edge_rows, part_count = coupling.shape[:2]
    row_count, count = vectors.shape[:2]
    half = count // 2
    me = lax.axis_index("bulk")
    mine = lax.axis_index("group")
    base = mine * bulk_count * row_count
    s = pl.program_id(0)
    slot = first_slot(row_count) + s

    def place_of(target):
        target = target - base
        owner = target // row_count
        return (owner ^ me) * row_count + target - owner * row_count

    @pl.when(s == 0)
    def _():
        for index, piece in enumerate(panel):
            for k in range(row_count):
                rows_of[index * row_count + k] = split_rows(piece[k])
        gram[...] = jnp.zeros_like(gram)

    direct = None
    for t in range(tiles.shape[1]):
        rows = rows_of[place_of(col[t, slot])]
        high, low = split(tiles[0, t])
        alive = live(load, slot, t)
        both = alive * dot16(rows, high, right_t)
        rest = alive * dot16(rows[:count], low, right_t)
        direct = (both, rest) if direct is None else (direct[0] + both, direct[1] + rest)
    direct = direct[0][:count] + direct[0][count:] + direct[1]
    value = vectors[s]
    near_value = times_tile(split_rows(value), diag[0], right_t)
    near[s] = near_value + direct
    if second:
        gram[...] += dot32(value, near_value + 2.0 * direct, right_t)
    else:
        gram[...] += dot32(value, value, right_t)

    @pl.when(s < edge_rows)
    def _():
        k = jnp.minimum(s, edge_rows - 1)
        crossed = None
        for h in range(part_count):
            ref = sides if h < part_count // 2 else other_sides
            start = (h % (part_count // 2) * edge_rows + k) * count
            rows = split_rows(ref[pl.ds(pl.multiple_of(start, count), count)])
            term = times_tile(rows, coupling[k, mine ^ h], right_t)
            crossed = term if crossed is None else crossed + term
        near[s] += crossed
        if second:
            gram[...] += dot32(value, crossed, right_t)

    arriving = new_slot[slot]
    incoming = place_of(arriving)
    for index, piece in enumerate(panel):

        @pl.when(incoming // row_count == index)
        def _(piece=piece):
            moving[s] = piece[incoming % row_count]

    if second:

        @pl.when(arriving != slot)
        def _():
            extra[4 * half :] = near[s]

    else:
        (flags,) = more

        @pl.when(arriving != slot)
        def _():
            distance = ((arriving - base) // row_count) ^ me
            for index in range(flags.shape[0] // 8):
                bit = ((distance >> index) & 1).astype(f32)
                flags[8 * index : 8 * index + 8] = jnp.full((8, flags.shape[1]), bit, f32)

    @pl.when(s == row_count - 1)
    def _():
        extra[:half] = pack(gram[...])
        if second:
            start = part_count // 2 * edge_rows * count
            extra[half : 4 * half] = sides[start:] + other_sides[start:]


def near_part(panel, vectors, tiles, diag, coupling, border, col, load, new_slot, second):
    row_count, count, order = vectors.shape
    bulk_count = len(panel)
    tile_count = tiles.shape[1]
    half = count // 2
    shapes = [vectors.shape, vectors.shape]
    if second:
        shapes += [(4 * half + count, order)]
    else:
        shapes += [(half, order), (8 * (bulk_count.bit_length() - 1), order)]
    return pl.pallas_call(
        functools.partial(near_kernel, bulk_count, second),
        grid=(row_count,),
        out_shape=[jax.ShapeDtypeStruct(shape, f32) for shape in shapes],
        in_specs=[vmem] * bulk_count
        + [
            vmem,
            pl.BlockSpec((1, tile_count, order, order), lambda s: (s, 0, 0, 0)),
            pl.BlockSpec((1, order, order), lambda s: (s, 0, 0)),
            vmem,
            vmem,
            vmem,
            smem,
            smem,
            smem,
        ],
        out_specs=[vmem] * len(shapes),
        scratch_shapes=[
            pltpu.VMEM((bulk_count * row_count, 2 * count, order), bf16),
            pltpu.VMEM((count, count), f32),
        ],
        compiler_params=params(),
        name="near_second" if second else "near_first",
    )(*panel, vectors, tiles, diag, coupling, *border, col, load, new_slot)


def gather_first_kernel(vectors, near, keep, *refs):
    received = refs[:-3]
    packed, first, side = refs[-3:]
    row_count, count = vectors.shape[:2]
    half = count // 2
    edge_rows = (side.shape[0] - 3 * half) // count
    grams = [None, None]
    for k in range(row_count):
        value = near[k] + keep[k]
        for ref in received:
            value = value + ref[k]
        first[k] = value
        if k < edge_rows:
            side[k * count : (k + 1) * count] = value
        terms = (dot32(vectors[k], value, right_t), dot32(value, value, right_t))
        grams = [term if old is None else old + term for old, term in zip(grams, terms)]
    start = edge_rows * count
    side[start : start + half] = packed[...]
    side[start + half : start + 2 * half] = pack(grams[0])
    side[start + 2 * half :] = pack(grams[1])


def gather_first(vectors, near, keep, received, packed, edge_rows):
    row_count, count, order = vectors.shape
    shapes = [vectors.shape, (edge_rows * count + 3 * (count // 2), order)]
    specs = [pl.BlockSpec((row_count, count, order), lambda s: (0, 0, 0))] * (3 + len(received))
    return pl.pallas_call(
        gather_first_kernel,
        grid=(1,),
        out_shape=[jax.ShapeDtypeStruct(shape, f32) for shape in shapes],
        in_specs=specs + [vmem],
        out_specs=[vmem] * 2,
        compiler_params=params(),
        name="gather_first",
    )(vectors, near, keep, *received, packed)


def spread_row(rows, index):
    return jnp.broadcast_to(rows[index : index + 1], rows.shape)


def inverse_factors(matrices):
    count = matrices[0].shape[0]
    step = 8
    shape = (step, 2 * count)
    row_ids = lax.broadcasted_iota(jnp.int32, (count, count), 0)
    col_ids = lax.broadcasted_iota(jnp.int32, (count, count), 1)
    eye = (row_ids == col_ids).astype(f32)
    sub = lax.broadcasted_iota(jnp.int32, shape, 0)
    work = []
    for matrix in matrices:
        both = jnp.concatenate([matrix, eye], axis=1)
        work.append([both[i : i + step] for i in range(0, count, step)])
    for block in range(count // step):
        start = block * step
        for w in work:
            cols = [
                [jnp.broadcast_to(rows[:, start + m : start + m + 1], shape) for m in range(step)]
                for rows in w[block:]
            ]
            factor = [[None] * step for _ in range(step)]
            scales, pivots = [], []
            for m in range(step):
                value = spread_row(cols[0][m], m)
                row = spread_row(w[block], m)
                for u in range(m):
                    value = value - factor[m][u] * factor[m][u]
                    row = row - factor[m][u] * pivots[u]
                scales.append(lax.rsqrt(value))
                pivots.append(row * scales[m])
                for v in range(m + 1, step):
                    value = spread_row(cols[0][m], v)
                    for u in range(m):
                        value = value - factor[v][u] * factor[m][u]
                    factor[v][m] = value * scales[m]
            for i in range(block + 1, count // step):
                left = []
                for m in range(step):
                    value = cols[i - block][m]
                    for u in range(m):
                        value = value - left[u] * factor[m][u]
                    left.append(value * scales[m])
                terms = [one * pivot for one, pivot in zip(left, pivots)]
                while len(terms) > 1:
                    terms = [x + y for x, y in zip(terms[::2], terms[1::2])]
                w[i] = w[i] - terms[0]
            rows = pivots[0]
            for m in range(1, step):
                rows = jnp.where(sub == m, pivots[m], rows)
            w[block] = rows
    return [jnp.concatenate(w, axis=0)[:, count:] for w in work]


def solve(inverse_factor, right):
    return dot32(inverse_factor, dot32(inverse_factor, right), left_t)


def final_kernel(gram, extra, moving, first, other, new_slot, solution, resid):
    row_count, count = moving.shape[:2]
    half = count // 2
    g3 = sym(unpack(gram[...]))
    g0, g1, g2 = (sym(unpack(extra[i * half : (i + 1) * half])) for i in (1, 2, 3))
    eye = (
        lax.broadcasted_iota(jnp.int32, (count, count), 0)
        == lax.broadcasted_iota(jnp.int32, (count, count), 1)
    ).astype(f32)
    factor_pq, factor_rr = inverse_factors([shift * g0 + g1, g0])
    a = solve(factor_pq, g0)
    m = eye - shift * a
    g2a = dot32(g2, a)
    cross = dot32(m, dot32(g1, a), left_t)
    g_new = dot32(m, dot32(g0, m), left_t) - cross - cross.T + dot32(a, g2a, left_t)
    g_new = sym(g_new)
    c = m + solve(factor_rr, g_new)
    cross = dot32(c, shift * dot32(g1, a) + g2a, left_t)
    g_pq = dot32(c, dot32(shift * g0 + g1, c), left_t) - cross - cross.T
    g_pq = sym(g_pq + dot32(a, shift * g2a + dot32(g3, a), left_t))
    (factor,) = inverse_factors([g_pq])
    a1 = solve(factor, g_new)
    aa1 = dot32(a, a1)
    ca1 = dot32(c, a1)
    zero = jnp.zeros_like(a)
    top = jnp.concatenate([a + ca1, -aa1, zero], axis=0)
    low = jnp.concatenate([m - shift * ca1, shift * aa1 - a - ca1, aa1], axis=0)
    coef = jnp.concatenate([top, low], axis=1)
    slot = first_slot(row_count)
    for k in range(row_count):
        moved = new_slot[slot + k] != slot + k
        second = other[k] + jnp.where(moved, extra[4 * half :], 0.0)
        basis = jnp.concatenate([moving[k], first[k], second], axis=0)
        both = dot32(coef, basis, left_t)
        solution[k] = both[:count]
        resid[k] = both[count:]


def final(gram, extra, moving, first, other, new_slot):
    return pl.pallas_call(
        final_kernel,
        out_shape=[jax.ShapeDtypeStruct(other.shape, f32)] * 2,
        in_specs=[vmem] * 5 + [smem],
        out_specs=[vmem] * 2,
        compiler_params=params(),
        name="final",
    )(gram, extra, moving, first, other, new_slot)


def settle_kernel(extra, partner, flags, new_slot, near, keep, *refs):
    received, (new_extra, other) = refs[:-2], refs[-2:]
    row_count, count = near.shape[:2]
    start = extra.shape[0] - count
    new_extra[:start] = extra[:start] + partner[:start]
    new_extra[start:] = jnp.where(flags[:1] > 0.5, partner[start:], extra[start:])
    slot = first_slot(row_count)
    for k in range(row_count):
        stays = new_slot[slot + k] == slot + k
        value = jnp.where(stays, near[k], 0.0) + keep[k]
        for ref in received:
            value = value + ref[k]
        other[k] = value


def settle(extra, partner, flags, new_slot, near, keep, received):
    block = pl.BlockSpec(near.shape, lambda s: (0, 0, 0))
    return pl.pallas_call(
        settle_kernel,
        grid=(1,),
        out_shape=[jax.ShapeDtypeStruct(extra.shape, f32), jax.ShapeDtypeStruct(near.shape, f32)],
        in_specs=[vmem] * 3 + [smem, vmem] + [block] * (1 + len(received)),
        out_specs=[vmem] * 2,
        compiler_params=params(),
        name="settle",
    )(extra, partner, flags, new_slot, near, keep, *received)


def spread(piece, bulk_count):
    pieces = [piece] + [swap(piece, "bulk", rel) for rel in range(2, bulk_count, 2)]
    return [own for piece in pieces for own in (piece, swap(piece, "bulk", 1))]


def share_side(side, edge, part_count):
    mask = 1
    while 2 * mask < part_count:
        other = swap(side, "group", mask)
        side = jnp.concatenate([side[:edge], other[:edge], side[edge:] + other[edge:]], axis=0)
        edge *= 2
        mask *= 2
    return side, swap(side, "group", mask)


def give_back(keep, send, row_count, bulk_count):
    from_core = swap(send, "bulk", 1)
    received = [from_core]
    for z in range(1, bulk_count // 2):
        rows = slice(z * row_count, (z + 1) * row_count)
        received.append(swap(keep[rows] + from_core[rows], "bulk", 2 * z))
    return received


def local(rhs, diag_tiles, offdiag_blocks, coupling, col_index, load, new_slot):
    row_count, count, order = rhs.shape
    edge_rows, part_count = coupling.shape[:2]
    bulk_count = lax.axis_size("bulk")
    half = count // 2
    edge = edge_rows * count
    indices = (col_index.T, load, new_slot)

    panel = spread(rhs, bulk_count)
    border = share_side(rhs.reshape(row_count * count, order)[:edge], edge, part_count)
    keep, send = returned(rhs, offdiag_blocks, *indices, bulk_count, False)
    received = give_back(keep, send, row_count, bulk_count)
    near, moving, packed, flags = near_part(
        panel, rhs, offdiag_blocks, diag_tiles, coupling, border, *indices, False
    )
    first, side = gather_first(rhs, near, keep, received, packed, edge_rows)

    panel = spread(first, bulk_count)
    border = share_side(side, edge, part_count)
    keep, send = returned(first, offdiag_blocks, *indices, bulk_count, True)
    received = give_back(keep, send, row_count, bulk_count)
    near, first, extra = near_part(
        panel, first, offdiag_blocks, diag_tiles, coupling, border, *indices, True
    )

    partner = swap(extra, "bulk", 1)
    extra, other = settle(extra, partner, flags, new_slot, near, keep, received)
    is_gram = lax.broadcasted_iota(jnp.int32, extra.shape, 0) < 4 * half
    for index in range(1, bulk_count.bit_length() - 1):
        partner = swap(extra, "bulk", 2**index)
        chosen = flags[8 * index : 8 * index + 1] > 0.5
        extra = jnp.where(is_gram, extra + partner, jnp.where(chosen, partner, extra))
    gram = extra[:half]
    mask = 1
    while mask < part_count:
        gram = gram + swap(gram, "group", mask)
        mask *= 2
    return tuple(final(gram, extra, moving, first, other, new_slot))


def solution(mesh):
    rows = P(("group", "bulk"))
    return jax.shard_map(
        local,
        mesh=mesh,
        in_specs=(rows, rows, rows, rows, P(), P(), P()),
        out_specs=(rows, rows),
        check_vma=False,
    )
```

```python
import functools

import jax
import jax.numpy as jnp
from jax import lax
from jax.experimental import pallas as pl
from jax.experimental.pallas import tpu as pltpu
from jax.sharding import PartitionSpec as P

shift = 4.0
f32 = jnp.float32
bf16 = jnp.bfloat16
normal = (((1,), (0,)), ((), ()))
right_t = (((1,), (1,)), ((), ()))
left_t = (((0,), (0,)), ((), ()))
vmem = pl.BlockSpec(memory_space=pltpu.VMEM)
smem = pl.BlockSpec(memory_space=pltpu.SMEM)
anywhere = pl.BlockSpec(memory_space=pl.ANY)
vmem_bytes = 40 * 2**20
all_vmem = 60 * 2**20


def params(limit=vmem_bytes):
    return pltpu.CompilerParams(vmem_limit_bytes=limit)


def swap(value, axis, mask):
    pairs = [(source, source ^ mask) for source in range(lax.axis_size(axis))]
    return lax.ppermute(value, axis, pairs)


def split(value):
    high = value.astype(bf16)
    return high, (value - high.astype(f32)).astype(bf16)


def dot16(left, right, dims):
    return lax.dot_general(left, right, dims, preferred_element_type=f32)


def dot32(left, right, dims=normal):
    return lax.dot_general(
        left, right, dims, preferred_element_type=f32, precision=lax.Precision.HIGHEST
    )


def split_rows(vectors):
    high, low = split(vectors)
    return jnp.concatenate([high, low], axis=0)


def times_tile(rows, tile, dims):
    count = rows.shape[0] // 2
    high, low = split(tile)
    both = dot16(rows, high, dims)
    return both[:count] + both[count:] + dot16(rows[:count], low, dims)


def pack(gram):
    half = gram.shape[0] // 2
    return jnp.concatenate([gram[:half], gram[half:]], axis=1)


def unpack(packed):
    half = packed.shape[1] // 2
    return jnp.concatenate([packed[:, :half], packed[:, half:]], axis=0)


def above(count):
    rows = lax.broadcasted_iota(jnp.int32, (count, count), 0)
    cols = lax.broadcasted_iota(jnp.int32, (count, count), 1)
    return cols > rows, cols == rows


def identity(count):
    return above(count)[1].astype(f32)


def join_symmetric(upper, lower):
    over, diagonal = above(upper.shape[0])
    row = jnp.sum(jnp.where(diagonal, upper, 0.0), axis=0, keepdims=True)
    return jnp.where(over, upper, lower), row


def part_symmetric(joined, row):
    over, diagonal = above(joined.shape[0])
    turned = joined.T
    upper = jnp.where(diagonal, row, jnp.where(over, joined, turned))
    return upper, jnp.where(over, turned, joined)


def sym(gram):
    return 0.5 * (gram + gram.T)


def first_slot(row_count):
    device = lax.axis_index("group") * lax.axis_size("bulk") + lax.axis_index("bulk")
    return device * row_count


def live(load_ref, slot, tile):
    return jnp.where(tile < load_ref[slot], 1.0, 0.0)


def far_masks(bulk_count):
    masks = []
    bit = bulk_count // 2
    while bit >= 4:
        masks += [bit | bit // 2, bit // 2]
        bit //= 4
    return masks + ([bit] if bit == 2 else [])


def owed_place(rel, bulk_count):
    place = 0
    index = 0
    bit = bulk_count.bit_length() - 2
    while bit >= 2:
        high = (rel >> bit) & 1
        low = (rel >> (bit - 1)) & 1
        place = place | (high << index) | ((high ^ low) << (index + 1))
        index += 2
        bit -= 2
    if bit == 1:
        place = place | (((rel >> 1) & 1) << index)
        index += 1
    return place | ((rel & 1) << index)


def returned_kernel(bulk_count, moved, vectors, tiles, col, load, new_slot, *refs):
    keep, send, total = refs[-3:]
    row_count = vectors.shape[0]
    me = lax.axis_index("bulk")
    base = lax.axis_index("group") * bulk_count * row_count
    s = pl.program_id(0)
    slot = first_slot(row_count) + s

    @pl.when(s == 0)
    def _():
        total[...] = jnp.zeros_like(total)

    rows = split_rows(vectors[s])
    for t in range(tiles.shape[1]):
        product = times_tile(rows, tiles[0, t], normal)
        target = col[t, slot]
        if moved:
            target = new_slot[target]
        target = target - base
        owner = target // row_count
        place = owed_place(owner ^ me, bulk_count) * row_count + target - owner * row_count
        total[place] += live(load, slot, t) * product

    @pl.when(s == row_count - 1)
    def _():
        half = total.shape[0] // 2
        keep[...] = total[:half]
        send[...] = total[half:]


def returned(vectors, tiles, col, load, new_slot, bulk_count, moved, *earlier):
    row_count, count, order = vectors.shape
    tile_count = tiles.shape[1]
    half = (bulk_count * row_count // 2, count, order)
    return pl.pallas_call(
        functools.partial(returned_kernel, bulk_count, moved),
        grid=(row_count,),
        out_shape=[jax.ShapeDtypeStruct(half, f32)] * 2,
        in_specs=[
            vmem,
            pl.BlockSpec((1, tile_count, order, order), lambda s: (s, 0, 0, 0)),
            smem,
            smem,
            smem,
        ]
        + [anywhere] * len(earlier),
        out_specs=[vmem] * 2,
        scratch_shapes=[pltpu.VMEM((2 * half[0], count, order), f32)],
        compiler_params=params(vmem_bytes if moved else all_vmem),
        name="returned_moved" if moved else "returned",
    )(vectors, tiles, col, load, new_slot, *earlier)


def near_kernel(bulk_count, pieces, second, *refs):
    panel, refs = refs[:pieces], refs[pieces:]
    vectors, tiles, diag, col, load, new_slot, near, moving, packed, *more, rows_of, gram = refs
    row_count, count = vectors.shape[:2]
    me = lax.axis_index("bulk")
    mine = lax.axis_index("group")
    base = mine * bulk_count * row_count
    s = pl.program_id(0)
    slot = first_slot(row_count) + s
    half_rows = bulk_count * row_count // 2
    held = [piece.shape[0] // count for piece in panel]
    starts = [sum(held[:index]) for index in range(pieces)]

    def place_of(target):
        target = target - base
        owner = target // row_count
        rel = owner ^ me
        return (rel & 1) * half_rows + (rel >> 1) * row_count + target - owner * row_count

    @pl.when(s == 0)
    def _():
        for piece, first, rows in zip(panel, starts, held):
            for k in range(rows):
                rows_of[first + k] = split_rows(piece[k * count : (k + 1) * count])
        gram[...] = jnp.zeros_like(gram)

    direct = None
    for t in range(tiles.shape[1]):
        rows = rows_of[place_of(col[t, slot])]
        high, low = split(tiles[0, t])
        alive = live(load, slot, t)
        both = alive * dot16(rows, high, right_t)
        rest = alive * dot16(rows[:count], low, right_t)
        direct = (both, rest) if direct is None else (direct[0] + both, direct[1] + rest)
    direct = direct[0][:count] + direct[0][count:] + direct[1]
    value = vectors[s]
    near_value = times_tile(split_rows(value), diag[0], right_t)
    near[s] = near_value + direct
    if second:
        gram[...] += dot32(value, near_value + 2.0 * direct, right_t)
    else:
        gram[...] += dot32(value, value, right_t)

    arriving = new_slot[slot]
    incoming = place_of(arriving)
    for piece, first, rows in zip(panel, starts, held):

        @pl.when((incoming >= first) & (incoming < first + rows))
        def _(piece=piece, first=first):
            start = pl.multiple_of((incoming - first) * count, count)
            moving[s] = piece[pl.ds(start, count)]

    if not second:
        (flags,) = more

        @pl.when(arriving != slot)
        def _():
            route = owed_place(((arriving - base) // row_count) ^ me, bulk_count)
            steps = flags.shape[0] // 8
            for index in range(steps):
                bit = ((route >> (steps - 1 - index)) & 1).astype(f32)
                flags[8 * index : 8 * index + 8] = jnp.full((8, flags.shape[1]), bit, f32)

    @pl.when(s == row_count - 1)
    def _():
        packed[...] = pack(gram[...])


def near_part(panel, vectors, tiles, diag, col, load, new_slot, second):
    row_count, count, order = vectors.shape
    bulk_count = sum(piece.shape[0] for piece in panel) // (row_count * count)
    tile_count = tiles.shape[1]
    shapes = [vectors.shape, vectors.shape, (count // 2, order)]
    if not second:
        shapes += [(8 * (bulk_count.bit_length() - 1), order)]
    return pl.pallas_call(
        functools.partial(near_kernel, bulk_count, len(panel), second),
        grid=(row_count,),
        out_shape=[jax.ShapeDtypeStruct(shape, f32) for shape in shapes],
        in_specs=[vmem] * len(panel)
        + [
            vmem,
            pl.BlockSpec((1, tile_count, order, order), lambda s: (s, 0, 0, 0)),
            pl.BlockSpec((1, order, order), lambda s: (s, 0, 0)),
            smem,
            smem,
            smem,
        ],
        out_specs=[vmem] * len(shapes),
        scratch_shapes=[
            pltpu.VMEM((bulk_count * row_count, 2 * count, order), bf16),
            pltpu.VMEM((count, count), f32),
        ],
        compiler_params=params(),
        name="near_second" if second else "near_first",
    )(*panel, vectors, tiles, diag, col, load, new_slot)


def crossed(side, coupling, k):
    edge_rows, part_count = coupling.shape[:2]
    count = side.shape[1] // 2
    mine = lax.axis_index("group")
    total = None
    for h in range(part_count):
        start = (h * edge_rows + k) * count
        rows = split_rows(side[start : start + count])
        term = times_tile(rows, coupling[k, mine ^ h], right_t)
        total = term if total is None else total + term
    return total


def gather_first_kernel(vectors, near, keep, *refs):
    received = refs[:-5]
    coupling, old_side, packed, first, side = refs[-5:]
    row_count, count = vectors.shape[:2]
    half = count // 2
    edge_rows = (side.shape[0] - 2 * half - 8) // count
    grams = [None, None]
    for k in range(row_count):
        value = near[k] + keep[k]
        for ref in received:
            value = value + ref[k]
        if k < edge_rows:
            value = value + crossed(old_side, coupling, k)
        first[k] = value
        if k < edge_rows:
            side[k * count : (k + 1) * count] = value
        terms = (dot32(vectors[k], value, right_t), dot32(value, value, right_t))
        grams = [term if old is None else old + term for old, term in zip(grams, terms)]
    start = edge_rows * count
    joined, row = join_symmetric(unpack(packed[...]), grams[1])
    side[start : start + half] = pack(joined)
    side[start + half : start + 2 * half] = pack(sym(grams[0]))
    rows = jnp.concatenate([row, jnp.zeros_like(row)], axis=1)
    side[start + 2 * half :] = jnp.broadcast_to(rows, (8, 2 * count))


def gather_first(vectors, near, terms, coupling, old_side, packed):
    row_count, count, order = vectors.shape
    edge_rows = coupling.shape[0]
    shapes = [vectors.shape, (edge_rows * count + count + 8, order)]
    specs = [pl.BlockSpec((row_count, count, order), lambda s: (0, 0, 0))] * (2 + len(terms))
    return pl.pallas_call(
        gather_first_kernel,
        grid=(1,),
        out_shape=[jax.ShapeDtypeStruct(shape, f32) for shape in shapes],
        in_specs=specs + [vmem] * 3,
        out_specs=[vmem] * 2,
        compiler_params=params(),
        name="gather_first",
    )(vectors, near, *terms, coupling, old_side, packed)


def edge_second_kernel(first, near, packed, coupling, side, new_slot, out, extra):
    row_count, count = first.shape[:2]
    edge_rows, part_count = coupling.shape[:2]
    half = count // 2
    gram = unpack(packed[...])
    for k in range(row_count):
        value = near[k]
        if k < edge_rows:
            more = crossed(side, coupling, k)
            gram = gram + dot32(first[k], more, right_t)
            value = value + more
        out[k] = value
    start = part_count * edge_rows * count
    joined, row = join_symmetric(unpack(side[start + half : start + 2 * half]), sym(gram))
    extra[:count] = jnp.concatenate([unpack(side[start : start + half]), joined], axis=1)
    row = jnp.concatenate([jnp.zeros_like(row), row], axis=1)
    extra[count : count + 8] = side[start + 2 * half :] + jnp.broadcast_to(row, (8, 2 * count))
    slot = first_slot(row_count)
    for k in range(row_count):

        @pl.when(new_slot[slot + k] != slot + k)
        def _(k=k):
            extra[count + 8 :] = out[k]


def edge_second(first, near, packed, coupling, side, new_slot):
    count, order = first.shape[1:]
    shapes = [near.shape, (2 * count + 8, order)]
    return pl.pallas_call(
        edge_second_kernel,
        out_shape=[jax.ShapeDtypeStruct(shape, f32) for shape in shapes],
        in_specs=[vmem] * 5 + [smem],
        out_specs=[vmem] * 2,
        compiler_params=params(),
        name="edge_second",
    )(first, near, packed, coupling, side, new_slot)


def spread_row(rows, index):
    return jnp.broadcast_to(rows[index : index + 1], rows.shape)


def inverse_factors(matrices):
    count = matrices[0].shape[0]
    step = 8
    shape = (step, 2 * count)
    eye = identity(count)
    sub = lax.broadcasted_iota(jnp.int32, shape, 0)
    work = []
    for matrix in matrices:
        both = jnp.concatenate([matrix, eye], axis=1)
        work.append([both[i : i + step] for i in range(0, count, step)])
    for block in range(count // step):
        start = block * step
        for w in work:
            cols = [
                [jnp.broadcast_to(rows[:, start + m : start + m + 1], shape) for m in range(step)]
                for rows in w[block:]
            ]
            factor = [[None] * step for _ in range(step)]
            scales, pivots = [], []
            for m in range(step):
                value = spread_row(cols[0][m], m)
                row = spread_row(w[block], m)
                for u in range(m):
                    value = value - factor[m][u] * factor[m][u]
                    row = row - factor[m][u] * pivots[u]
                scales.append(lax.rsqrt(value))
                pivots.append(row * scales[m])
                for v in range(m + 1, step):
                    value = spread_row(cols[0][m], v)
                    for u in range(m):
                        value = value - factor[v][u] * factor[m][u]
                    factor[v][m] = value * scales[m]
            for i in range(block + 1, count // step):
                left = []
                for m in range(step):
                    value = cols[i - block][m]
                    for u in range(m):
                        value = value - left[u] * factor[m][u]
                    left.append(value * scales[m])
                terms = [one * pivot for one, pivot in zip(left, pivots)]
                while len(terms) > 1:
                    terms = [x + y for x, y in zip(terms[::2], terms[1::2])]
                w[i] = w[i] - terms[0]
            rows = pivots[0]
            for m in range(1, step):
                rows = jnp.where(sub == m, pivots[m], rows)
            w[block] = rows
    return [jnp.concatenate(w, axis=0)[:, count:] for w in work]


def solve(inverse_factor, right):
    return dot32(inverse_factor, dot32(inverse_factor, right), left_t)


def grams_of(sums):
    count = sums.shape[1] // 2
    row = sums[count : count + 1]
    g0, g2 = part_symmetric(sums[:count, :count], row[:, :count])
    g1, g3 = part_symmetric(sums[:count, count:], row[:, count:])
    return g0, g1, g2, g3


def first_solves_kernel(extra, out):
    g0, g1, _, _ = grams_of(extra[...])
    factor_pq, factor_rr = inverse_factors([shift * g0 + g1, g0])
    out[0] = solve(factor_pq, g0)
    out[1] = dot32(factor_rr, factor_rr, left_t)


def next_gram_kernel(extra, solved, out):
    g0, g1, g2, _ = grams_of(extra[...])
    a, inverse_rr = solved[0], solved[1]
    count = a.shape[0]
    m = identity(count) - shift * a
    by_a = dot32(jnp.concatenate([g0, g1, g2], axis=0), a)
    g0a, g1a, g2a = (by_a[i * count : (i + 1) * count] for i in range(3))
    g0m, g1m = g0 - shift * g0a, g1 - shift * g1a
    left = jnp.concatenate([m, a], axis=0)
    g_new = sym(dot32(left, jnp.concatenate([g0m - g1a, g2a - g1m], axis=0), left_t))
    c = m + dot32(inverse_rr, g_new)
    by_c = dot32(jnp.concatenate([shift * g0 + g1, shift * g1 + g2], axis=0), c)
    left = jnp.concatenate([c, a], axis=0)
    upper = by_c[:count] - (shift * g1a + g2a)
    lower = shift * g2a - by_c[count:]
    out[0] = c
    out[1] = g_new
    out[2] = dot32(left, jnp.concatenate([upper, lower], axis=0), left_t)


def small_call(kernel, count, matrices, name, *operands):
    return pl.pallas_call(
        kernel,
        out_shape=jax.ShapeDtypeStruct((matrices, count, count), f32),
        in_specs=[vmem] * len(operands),
        out_specs=vmem,
        compiler_params=params(),
        name=name,
    )(*operands)


def final_kernel(gram, solved, following, moving, first, near, new_slot, row, *refs):
    last_row, flags, *terms, solution, resid = refs
    row_count, count = moving.shape[:2]
    arrived = jnp.where(flags[flags.shape[0] - 8 :][:1] > 0.5, last_row[0], row[...])
    a, c, g_new = solved[0], following[0], following[1]
    g3 = sym(unpack(gram[...]))
    g_pq = sym(following[2] + dot32(a, dot32(g3, a), left_t))
    (factor,) = inverse_factors([g_pq])
    a1 = solve(factor, g_new)
    by_a1 = dot32(jnp.concatenate([a, c], axis=0), a1)
    aa1, ca1 = by_a1[:count], by_a1[count:]
    m = identity(count) - shift * a
    top = jnp.concatenate([a + ca1, -aa1, jnp.zeros_like(a)], axis=0)
    low = jnp.concatenate([m - shift * ca1, shift * aa1 - a - ca1, aa1], axis=0)
    coef = jnp.concatenate([top, low], axis=1)
    slot = first_slot(row_count)
    basis = []
    for k in range(row_count):
        stays = new_slot[slot + k] == slot + k
        second = jnp.where(stays, near[k], arrived)
        for ref in terms:
            second = second + ref[k]
        basis.append(jnp.concatenate([moving[k], first[k], second], axis=0))
    order = moving.shape[2]
    both = dot32(coef, jnp.concatenate(basis, axis=1), left_t)
    for k in range(row_count):
        solution[k] = both[:count, k * order : (k + 1) * order]
        resid[k] = both[count:, k * order : (k + 1) * order]


def final(gram, solved, following, moving, first, near, new_slot, row, flags, terms):
    block = pl.BlockSpec(near.shape, lambda s: (0, 0, 0))
    last = pl.BlockSpec((1,) + near.shape[1:], lambda s: (terms[-1].shape[0] - 1, 0, 0))
    return pl.pallas_call(
        final_kernel,
        grid=(1,),
        out_shape=[jax.ShapeDtypeStruct(near.shape, f32)] * 2,
        in_specs=[vmem] * 6 + [smem, vmem, last, vmem] + [block] * len(terms),
        out_specs=[vmem] * 2,
        compiler_params=params(),
        name="final",
    )(gram, solved, following, moving, first, near, new_slot, row, terms[-1], flags, *terms)


def add_kernel(count, *refs):
    total = refs[0][...]
    for ref in refs[1:count]:
        total = total + ref[...]
    refs[-1][...] = total


def add_upper(terms, rows, *earlier):
    shape = (rows,) + terms[0].shape[1:]
    block = pl.BlockSpec(shape, lambda s: (1, 0, 0))
    return pl.pallas_call(
        functools.partial(add_kernel, len(terms)),
        grid=(1,),
        out_shape=jax.ShapeDtypeStruct(shape, f32),
        in_specs=[block] * len(terms) + [anywhere] * len(earlier),
        out_specs=vmem,
        compiler_params=params(),
        name="add_upper",
    )(*terms, *earlier)


def add_with_row_kernel(step, count, row, other, flags, *refs):
    terms, out, held = refs[:count], refs[-2], refs[-1]
    total = terms[0][...]
    for ref in terms[1:]:
        total = total + ref[...]
    out[: total.shape[0]] = total
    value = row[...]
    if step > 1:
        value = jnp.where(flags[8 * step : 8 * step + 1] > 0.5, other[0], value)
    out[total.shape[0]] = value
    held[...] = value


def add_with_row(terms, rows, row, flags, step, *earlier):
    shape = (rows,) + terms[0].shape[1:]
    block = pl.BlockSpec(shape, lambda s: (1, 0, 0))
    last = pl.BlockSpec((1,) + shape[1:], lambda s: (terms[-1].shape[0] - 1, 0, 0))
    return pl.pallas_call(
        functools.partial(add_with_row_kernel, step, len(terms)),
        grid=(1,),
        out_shape=[
            jax.ShapeDtypeStruct((rows + 1,) + shape[1:], f32),
            jax.ShapeDtypeStruct(row.shape, f32),
        ],
        in_specs=[vmem, last, vmem] + [block] * len(terms) + [anywhere] * len(earlier),
        out_specs=[vmem] * 2,
        compiler_params=params(),
        name="add_with_row",
    )(row, terms[-1], flags, *terms, *earlier)


def settle_kernel(index, sums, extra, partner, flags, *refs):
    out = refs[-1]
    out[:sums] = extra[:sums] + partner[:sums]
    if extra.shape[0] > sums:
        chosen = flags[8 * index : 8 * index + 1] > 0.5
        out[sums:] = jnp.where(chosen, partner[sums:], extra[sums:])


def settle(extra, partner, flags, index, sums, *earlier):
    return pl.pallas_call(
        functools.partial(settle_kernel, index, sums),
        out_shape=jax.ShapeDtypeStruct(extra.shape, f32),
        in_specs=[vmem] * 3 + [anywhere] * len(earlier),
        out_specs=vmem,
        compiler_params=params(),
        name="settle",
    )(extra, partner, flags, *earlier)


def leave_row_kernel(sums, extra, partner, flags, out, row):
    out[...] = extra[:sums] + partner[:sums]
    row[...] = jnp.where(flags[8:9] > 0.5, partner[sums:], extra[sums:])


def leave_row(extra, partner, flags, sums):
    order = extra.shape[1]
    return pl.pallas_call(
        functools.partial(leave_row_kernel, sums),
        out_shape=[
            jax.ShapeDtypeStruct((sums, order), f32),
            jax.ShapeDtypeStruct((extra.shape[0] - sums, order), f32),
        ],
        in_specs=[vmem] * 3,
        out_specs=[vmem] * 2,
        compiler_params=params(),
        name="leave_row",
    )(extra, partner, flags)


def last_gram_kernel(sums, partner, out, gram):
    total = sums[...] + partner[...]
    out[...] = total
    gram[...] = pack(grams_of(total)[3])


def last_gram(sums, partner):
    rows, order = sums.shape
    return pl.pallas_call(
        last_gram_kernel,
        out_shape=[
            jax.ShapeDtypeStruct((rows, order), f32),
            jax.ShapeDtypeStruct((order // 4, order), f32),
        ],
        in_specs=[vmem] * 2,
        out_specs=[vmem] * 2,
        compiler_params=params(),
        name="last_gram",
    )(sums, partner)


def add_whole(left, right, *earlier):
    return pl.pallas_call(
        functools.partial(add_kernel, 2),
        out_shape=jax.ShapeDtypeStruct(left.shape, f32),
        in_specs=[vmem] * 2 + [anywhere] * len(earlier),
        out_specs=vmem,
        compiler_params=params(),
        name="add_whole",
    )(left, right, *earlier)


def join_kernel(count, *refs):
    out = refs[-1]
    rows = refs[0].shape[0]
    for index, ref in enumerate(refs[:count]):
        out[index * rows : (index + 1) * rows] = ref[...]


def join(pieces, *earlier):
    rows, order = pieces[0].shape
    return pl.pallas_call(
        functools.partial(join_kernel, len(pieces)),
        out_shape=jax.ShapeDtypeStruct((len(pieces) * rows, order), f32),
        in_specs=[vmem] * len(pieces) + [anywhere] * len(earlier),
        out_specs=vmem,
        compiler_params=params(),
        name="join",
    )(*pieces, *earlier)


def merge_kernel(edge, mine, other, *refs):
    out = refs[-1]
    out[:edge] = mine[:edge]
    out[edge : 2 * edge] = other[:edge]
    if mine.shape[0] > edge:
        out[2 * edge :] = mine[edge:] + other[edge:]


def merge_side(side, other, edge, *earlier):
    return pl.pallas_call(
        functools.partial(merge_kernel, edge),
        out_shape=jax.ShapeDtypeStruct((side.shape[0] + edge, side.shape[1]), f32),
        in_specs=[vmem] * 2 + [anywhere] * len(earlier),
        out_specs=vmem,
        compiler_params=params(),
        name="merge_side",
    )(side, other, *earlier)


def share_side(side, edge, part_count):
    mask = 1
    while 2 * mask < part_count:
        side = merge_side(side, swap(side, "group", mask), mask * edge)
        mask *= 2
    return side, swap(side, "group", mask)


def share_panel(piece, bulk_count, *earlier):
    own = [piece] + [swap(piece, "bulk", rel) for rel in range(2, bulk_count, 2)]
    middle = len(own) // 2
    joined = [join(own[:middle]), join(own[middle:], *earlier)]
    return own + [swap(one, "bulk", 1) for one in joined], joined[-1]


def local(rhs, diag_tiles, offdiag_blocks, coupling, col_index, load, new_slot):
    row_count, count, order = rhs.shape
    edge_rows, part_count = coupling.shape[:2]
    bulk_count = lax.axis_size("bulk")
    steps = bulk_count.bit_length() - 1
    masks = far_masks(bulk_count)[::-1]
    edge = edge_rows * count
    half_edges = part_count // 2 * edge
    indices = (col_index.T, load, new_slot)

    flat = rhs.reshape(row_count * count, order)
    side, other_side = share_side(flat[:edge], edge, part_count)
    keep, send = returned(rhs, offdiag_blocks, *indices, bulk_count, False)
    panel, joined = share_panel(flat, bulk_count, side)
    terms = [keep, swap(send, "bulk", 1)]
    rows = bulk_count // 2 * row_count
    for step, mask in enumerate(masks):
        rows //= 2
        total = add_upper(terms, rows, *([joined] if step else []))
        terms.append(swap(total, "bulk", mask))
    near, moving, packed, flags = near_part(
        panel, rhs, offdiag_blocks, diag_tiles, *indices, False
    )
    side = merge_side(side, other_side, half_edges, near)
    first, side = gather_first(rhs, near, terms, coupling, side, packed)

    side, other_side = share_side(side, edge, part_count)
    keep, send = returned(first, offdiag_blocks, *indices, bulk_count, True)
    panel, joined = share_panel(
        first.reshape(row_count * count, order), bulk_count, side, keep
    )
    terms = [keep, swap(send, "bulk", 1)]
    rows = bulk_count // 4 * row_count
    terms.append(swap(add_upper(terms, rows, joined), "bulk", masks[0]))
    near, moved, packed = near_part(panel, first, offdiag_blocks, diag_tiles, *indices, True)
    side = merge_side(side, other_side, half_edges, near)
    near, extra = edge_second(first, near, packed, coupling, side, new_slot)

    sums = count + 8
    extra = settle(extra, swap(extra, "bulk", 1), flags, 0, sums, terms[-1])
    extra, row = leave_row(extra, swap(extra, "bulk", masks[0]), flags, sums)
    mask = 4
    while 2 * mask < bulk_count:
        extra = settle(extra, swap(extra, "bulk", mask), flags, 0, sums)
        mask *= 2
    extra, gram = last_gram(extra, swap(extra, "bulk", mask))
    for step in range(1, steps - 1):
        rows //= 2
        total, row = add_with_row(terms, rows, row, flags, step, extra)
        terms.append(swap(total, "bulk", masks[step]))
    solved = small_call(first_solves_kernel, count, 2, "first_solves", extra)
    following = small_call(next_gram_kernel, count, 3, "next_gram", extra, solved)
    mask = 1
    while mask < part_count:
        partner = swap(gram, "group", mask)
        gram = add_whole(gram, partner, *([solved] if mask == 1 else []))
        mask *= 2
    return tuple(
        final(gram, solved, following, moving, moved, near, new_slot, row, flags, terms)
    )


def solution(mesh):
    rows = P(("group", "bulk"))
    return jax.shard_map(
        local,
        mesh=mesh,
        in_specs=(rows, rows, rows, rows, P(), P(), P()),
        out_specs=(rows, rows),
        check_vma=False,
    )
```

```python
import functools

import jax
import jax.numpy as jnp
from jax import lax
from jax.experimental import pallas as pl
from jax.experimental.pallas import tpu as pltpu
from jax.sharding import PartitionSpec as P

shift = 4.0
f32 = jnp.float32
bf16 = jnp.bfloat16
normal = (((1,), (0,)), ((), ()))
right_t = (((1,), (1,)), ((), ()))
left_t = (((0,), (0,)), ((), ()))
vmem = pl.BlockSpec(memory_space=pltpu.VMEM)
smem = pl.BlockSpec(memory_space=pltpu.SMEM)
anywhere = pl.BlockSpec(memory_space=pl.ANY)
vmem_bytes = 40 * 2**20
all_vmem = 60 * 2**20


def params(limit=vmem_bytes):
    return pltpu.CompilerParams(vmem_limit_bytes=limit)


def swap(value, axis, mask):
    pairs = [(source, source ^ mask) for source in range(lax.axis_size(axis))]
    return lax.ppermute(value, axis, pairs)


def split(value):
    high = value.astype(bf16)
    return high, (value - high.astype(f32)).astype(bf16)


def dot16(left, right, dims):
    return lax.dot_general(left, right, dims, preferred_element_type=f32)


def dot32(left, right, dims=normal):
    return lax.dot_general(
        left, right, dims, preferred_element_type=f32, precision=lax.Precision.HIGHEST
    )


def split_rows(vectors):
    high, low = split(vectors)
    return jnp.concatenate([high, low], axis=0)


def times_tile(rows, tile, dims):
    count = rows.shape[0] // 2
    high, low = split(tile)
    both = dot16(rows, high, dims)
    return both[:count] + both[count:] + dot16(rows[:count], low, dims)


def pack(gram):
    half = gram.shape[0] // 2
    return jnp.concatenate([gram[:half], gram[half:]], axis=1)


def unpack(packed):
    half = packed.shape[1] // 2
    return jnp.concatenate([packed[:, :half], packed[:, half:]], axis=0)


def above(count):
    rows = lax.broadcasted_iota(jnp.int32, (count, count), 0)
    cols = lax.broadcasted_iota(jnp.int32, (count, count), 1)
    return cols > rows, cols == rows


def identity(count):
    return above(count)[1].astype(f32)


def join_symmetric(upper, lower):
    over, diagonal = above(upper.shape[0])
    row = jnp.sum(jnp.where(diagonal, upper, 0.0), axis=0, keepdims=True)
    return jnp.where(over, upper, lower), row


def part_symmetric(joined, row):
    over, diagonal = above(joined.shape[0])
    turned = joined.T
    upper = jnp.where(diagonal, row, jnp.where(over, joined, turned))
    return upper, jnp.where(over, turned, joined)


def sym(gram):
    return 0.5 * (gram + gram.T)


def first_slot(row_count):
    device = lax.axis_index("group") * lax.axis_size("bulk") + lax.axis_index("bulk")
    return device * row_count


def live(load_ref, slot, tile):
    return jnp.where(tile < load_ref[slot], 1.0, 0.0)


def far_masks(bulk_count):
    masks = []
    bit = bulk_count // 2
    while bit >= 4:
        masks += [bit | bit // 2, bit // 2]
        bit //= 4
    return masks + ([bit] if bit == 2 else [])


def owed_place(rel, bulk_count):
    place = 0
    index = 0
    bit = bulk_count.bit_length() - 2
    while bit >= 2:
        high = (rel >> bit) & 1
        low = (rel >> (bit - 1)) & 1
        place = place | (high << index) | ((high ^ low) << (index + 1))
        index += 2
        bit -= 2
    if bit == 1:
        place = place | (((rel >> 1) & 1) << index)
        index += 1
    return place | ((rel & 1) << index)


def returned_kernel(bulk_count, moved, vectors, tiles, col, load, new_slot, *refs):
    keep, send, total = refs[-3:]
    row_count = vectors.shape[0]
    me = lax.axis_index("bulk")
    base = lax.axis_index("group") * bulk_count * row_count
    s = pl.program_id(0)
    slot = first_slot(row_count) + s

    @pl.when(s == 0)
    def _():
        total[...] = jnp.zeros_like(total)

    rows = split_rows(vectors[s])
    for t in range(tiles.shape[1]):
        product = times_tile(rows, tiles[0, t], normal)
        target = col[t, slot]
        if moved:
            target = new_slot[target]
        target = target - base
        owner = target // row_count
        place = owed_place(owner ^ me, bulk_count) * row_count + target - owner * row_count
        total[place] += live(load, slot, t) * product

    @pl.when(s == row_count - 1)
    def _():
        half = total.shape[0] // 2
        keep[...] = total[:half]
        send[...] = total[half:]


def returned(vectors, tiles, col, load, new_slot, bulk_count, moved, *earlier):
    row_count, count, order = vectors.shape
    tile_count = tiles.shape[1]
    half = (bulk_count * row_count // 2, count, order)
    return pl.pallas_call(
        functools.partial(returned_kernel, bulk_count, moved),
        grid=(row_count,),
        out_shape=[jax.ShapeDtypeStruct(half, f32)] * 2,
        in_specs=[
            vmem,
            pl.BlockSpec((1, tile_count, order, order), lambda s: (s, 0, 0, 0)),
            smem,
            smem,
            smem,
        ]
        + [anywhere] * len(earlier),
        out_specs=[vmem] * 2,
        scratch_shapes=[pltpu.VMEM((2 * half[0], count, order), f32)],
        compiler_params=params(vmem_bytes if moved else all_vmem),
        name="returned_moved" if moved else "returned",
    )(vectors, tiles, col, load, new_slot, *earlier)


def near_kernel(bulk_count, pieces, second, *refs):
    panel, refs = refs[:pieces], refs[pieces:]
    vectors, tiles, diag, col, load, new_slot, near, moving, packed, *more, rows_of, gram = refs
    row_count, count = vectors.shape[:2]
    me = lax.axis_index("bulk")
    mine = lax.axis_index("group")
    base = mine * bulk_count * row_count
    s = pl.program_id(0)
    slot = first_slot(row_count) + s
    half_rows = bulk_count * row_count // 2
    held = [piece.shape[0] // count for piece in panel]
    starts = [sum(held[:index]) for index in range(pieces)]

    def place_of(target):
        target = target - base
        owner = target // row_count
        rel = owner ^ me
        return (rel & 1) * half_rows + (rel >> 1) * row_count + target - owner * row_count

    @pl.when(s == 0)
    def _():
        for piece, first, rows in zip(panel, starts, held):
            for k in range(rows):
                rows_of[first + k] = split_rows(piece[k * count : (k + 1) * count])
        gram[...] = jnp.zeros_like(gram)

    direct = None
    for t in range(tiles.shape[1]):
        rows = rows_of[place_of(col[t, slot])]
        high, low = split(tiles[0, t])
        alive = live(load, slot, t)
        both = alive * dot16(rows, high, right_t)
        rest = alive * dot16(rows[:count], low, right_t)
        direct = (both, rest) if direct is None else (direct[0] + both, direct[1] + rest)
    direct = direct[0][:count] + direct[0][count:] + direct[1]
    value = vectors[s]
    near_value = times_tile(split_rows(value), diag[0], right_t)
    near[s] = near_value + direct
    if second:
        gram[...] += dot32(value, near_value + 2.0 * direct, right_t)
    else:
        gram[...] += dot32(value, value, right_t)

    arriving = new_slot[slot]
    incoming = place_of(arriving)
    for piece, first, rows in zip(panel, starts, held):

        @pl.when((incoming >= first) & (incoming < first + rows))
        def _(piece=piece, first=first):
            start = pl.multiple_of((incoming - first) * count, count)
            moving[s] = piece[pl.ds(start, count)]

    if not second:
        (flags,) = more

        @pl.when(arriving != slot)
        def _():
            route = owed_place(((arriving - base) // row_count) ^ me, bulk_count)
            steps = flags.shape[0] // 8
            for index in range(steps):
                bit = ((route >> (steps - 1 - index)) & 1).astype(f32)
                flags[8 * index : 8 * index + 8] = jnp.full((8, flags.shape[1]), bit, f32)

    @pl.when(s == row_count - 1)
    def _():
        packed[...] = pack(gram[...])


def near_part(panel, vectors, tiles, diag, col, load, new_slot, second):
    row_count, count, order = vectors.shape
    bulk_count = sum(piece.shape[0] for piece in panel) // (row_count * count)
    tile_count = tiles.shape[1]
    shapes = [vectors.shape, vectors.shape, (count // 2, order)]
    if not second:
        shapes += [(8 * (bulk_count.bit_length() - 1), order)]
    return pl.pallas_call(
        functools.partial(near_kernel, bulk_count, len(panel), second),
        grid=(row_count,),
        out_shape=[jax.ShapeDtypeStruct(shape, f32) for shape in shapes],
        in_specs=[vmem] * len(panel)
        + [
            vmem,
            pl.BlockSpec((1, tile_count, order, order), lambda s: (s, 0, 0, 0)),
            pl.BlockSpec((1, order, order), lambda s: (s, 0, 0)),
            smem,
            smem,
            smem,
        ],
        out_specs=[vmem] * len(shapes),
        scratch_shapes=[
            pltpu.VMEM((bulk_count * row_count, 2 * count, order), bf16),
            pltpu.VMEM((count, count), f32),
        ],
        compiler_params=params(),
        name="near_second" if second else "near_first",
    )(*panel, vectors, tiles, diag, col, load, new_slot)


def crossed(side, coupling, k):
    edge_rows, part_count = coupling.shape[:2]
    count = side.shape[1] // 2
    mine = lax.axis_index("group")
    total = None
    for h in range(part_count):
        start = (h * edge_rows + k) * count
        rows = split_rows(side[start : start + count])
        term = times_tile(rows, coupling[k, mine ^ h], right_t)
        total = term if total is None else total + term
    return total


def gather_first_kernel(vectors, near, keep, *refs):
    received = refs[:-5]
    coupling, old_side, packed, first, side = refs[-5:]
    row_count, count = vectors.shape[:2]
    half = count // 2
    edge_rows = (side.shape[0] - 2 * half - 8) // count
    grams = [None, None]
    for k in range(row_count):
        value = near[k] + keep[k]
        for ref in received:
            value = value + ref[k]
        if k < edge_rows:
            value = value + crossed(old_side, coupling, k)
        first[k] = value
        if k < edge_rows:
            side[k * count : (k + 1) * count] = value
        terms = (dot32(vectors[k], value, right_t), dot32(value, value, right_t))
        grams = [term if old is None else old + term for old, term in zip(grams, terms)]
    start = edge_rows * count
    joined, row = join_symmetric(unpack(packed[...]), grams[1])
    side[start : start + half] = pack(joined)
    side[start + half : start + 2 * half] = pack(sym(grams[0]))
    rows = jnp.concatenate([row, jnp.zeros_like(row)], axis=1)
    side[start + 2 * half :] = jnp.broadcast_to(rows, (8, 2 * count))


def gather_first(vectors, near, terms, coupling, old_side, packed):
    row_count, count, order = vectors.shape
    edge_rows = coupling.shape[0]
    shapes = [vectors.shape, (edge_rows * count + count + 8, order)]
    specs = [pl.BlockSpec((row_count, count, order), lambda s: (0, 0, 0))] * (2 + len(terms))
    return pl.pallas_call(
        gather_first_kernel,
        grid=(1,),
        out_shape=[jax.ShapeDtypeStruct(shape, f32) for shape in shapes],
        in_specs=specs + [vmem] * 3,
        out_specs=[vmem] * 2,
        compiler_params=params(),
        name="gather_first",
    )(vectors, near, *terms, coupling, old_side, packed)


def edge_second_kernel(first, near, packed, coupling, side, new_slot, out, extra):
    row_count, count = first.shape[:2]
    edge_rows, part_count = coupling.shape[:2]
    half = count // 2
    gram = unpack(packed[...])
    for k in range(row_count):
        value = near[k]
        if k < edge_rows:
            more = crossed(side, coupling, k)
            gram = gram + dot32(first[k], more, right_t)
            value = value + more
        out[k] = value
    start = part_count * edge_rows * count
    joined, row = join_symmetric(unpack(side[start + half : start + 2 * half]), sym(gram))
    extra[:count] = jnp.concatenate([unpack(side[start : start + half]), joined], axis=1)
    row = jnp.concatenate([jnp.zeros_like(row), row], axis=1)
    extra[count : count + 8] = side[start + 2 * half :] + jnp.broadcast_to(row, (8, 2 * count))
    slot = first_slot(row_count)
    for k in range(row_count):

        @pl.when(new_slot[slot + k] != slot + k)
        def _(k=k):
            extra[count + 8 :] = out[k]


def edge_second(first, near, packed, coupling, side, new_slot):
    count, order = first.shape[1:]
    shapes = [near.shape, (2 * count + 8, order)]
    return pl.pallas_call(
        edge_second_kernel,
        out_shape=[jax.ShapeDtypeStruct(shape, f32) for shape in shapes],
        in_specs=[vmem] * 5 + [smem],
        out_specs=[vmem] * 2,
        compiler_params=params(),
        name="edge_second",
    )(first, near, packed, coupling, side, new_slot)


def spread_row(rows, index):
    return jnp.broadcast_to(rows[index : index + 1], rows.shape)


def inverse_factors(matrices):
    count = matrices[0].shape[0]
    step = 8
    shape = (step, 2 * count)
    eye = identity(count)
    sub = lax.broadcasted_iota(jnp.int32, shape, 0)
    work = []
    for matrix in matrices:
        both = jnp.concatenate([matrix, eye], axis=1)
        work.append([both[i : i + step] for i in range(0, count, step)])
    for block in range(count // step):
        start = block * step
        for w in work:
            cols = [
                [jnp.broadcast_to(rows[:, start + m : start + m + 1], shape) for m in range(step)]
                for rows in w[block:]
            ]
            factor = [[None] * step for _ in range(step)]
            scales, pivots = [], []
            for m in range(step):
                value = spread_row(cols[0][m], m)
                row = spread_row(w[block], m)
                for u in range(m):
                    value = value - factor[m][u] * factor[m][u]
                    row = row - factor[m][u] * pivots[u]
                scales.append(lax.rsqrt(value))
                pivots.append(row * scales[m])
                for v in range(m + 1, step):
                    value = spread_row(cols[0][m], v)
                    for u in range(m):
                        value = value - factor[v][u] * factor[m][u]
                    factor[v][m] = value * scales[m]
            for i in range(block + 1, count // step):
                left = []
                for m in range(step):
                    value = cols[i - block][m]
                    for u in range(m):
                        value = value - left[u] * factor[m][u]
                    left.append(value * scales[m])
                terms = [one * pivot for one, pivot in zip(left, pivots)]
                while len(terms) > 1:
                    terms = [x + y for x, y in zip(terms[::2], terms[1::2])]
                w[i] = w[i] - terms[0]
            rows = pivots[0]
            for m in range(1, step):
                rows = jnp.where(sub == m, pivots[m], rows)
            w[block] = rows
    return [jnp.concatenate(w, axis=0)[:, count:] for w in work]


def solve(inverse_factor, right):
    return dot32(inverse_factor, dot32(inverse_factor, right), left_t)


def grams_of(sums):
    count = sums.shape[1] // 2
    row = sums[count : count + 1]
    g0, g2 = part_symmetric(sums[:count, :count], row[:, :count])
    g1, g3 = part_symmetric(sums[:count, count:], row[:, count:])
    return g0, g1, g2, g3


def first_solves_kernel(extra, out):
    g0, g1, _, _ = grams_of(extra[...])
    factor_pq, factor_rr = inverse_factors([shift * g0 + g1, g0])
    out[0] = solve(factor_pq, g0)
    out[1] = dot32(factor_rr, factor_rr, left_t)


def next_gram_kernel(extra, solved, out):
    g0, g1, g2, _ = grams_of(extra[...])
    a, inverse_rr = solved[0], solved[1]
    count = a.shape[0]
    m = identity(count) - shift * a
    by_a = dot32(jnp.concatenate([g0, g1, g2], axis=0), a)
    g0a, g1a, g2a = (by_a[i * count : (i + 1) * count] for i in range(3))
    g0m, g1m = g0 - shift * g0a, g1 - shift * g1a
    left = jnp.concatenate([m, a], axis=0)
    g_new = sym(dot32(left, jnp.concatenate([g0m - g1a, g2a - g1m], axis=0), left_t))
    c = m + dot32(inverse_rr, g_new)
    by_c = dot32(jnp.concatenate([shift * g0 + g1, shift * g1 + g2], axis=0), c)
    left = jnp.concatenate([c, a], axis=0)
    upper = by_c[:count] - (shift * g1a + g2a)
    lower = shift * g2a - by_c[count:]
    out[0] = c
    out[1] = g_new
    out[2] = dot32(left, jnp.concatenate([upper, lower], axis=0), left_t)


def small_call(kernel, count, matrices, name, *operands):
    return pl.pallas_call(
        kernel,
        out_shape=jax.ShapeDtypeStruct((matrices, count, count), f32),
        in_specs=[vmem] * len(operands),
        out_specs=vmem,
        compiler_params=params(),
        name=name,
    )(*operands)


def final_kernel(gram, solved, following, moving, first, near, new_slot, row, *refs):
    last_row, flags, *terms, solution, resid = refs
    row_count, count = moving.shape[:2]
    arrived = jnp.where(flags[flags.shape[0] - 8 :][:1] > 0.5, last_row[0], row[...])
    a, c, g_new = solved[0], following[0], following[1]
    g3 = sym(unpack(gram[...]))
    g_pq = sym(following[2] + dot32(a, dot32(g3, a), left_t))
    (factor,) = inverse_factors([g_pq])
    a1 = solve(factor, g_new)
    by_a1 = dot32(jnp.concatenate([a, c], axis=0), a1)
    aa1, ca1 = by_a1[:count], by_a1[count:]
    m = identity(count) - shift * a
    top = jnp.concatenate([a + ca1, -aa1, jnp.zeros_like(a)], axis=0)
    low = jnp.concatenate([m - shift * ca1, shift * aa1 - a - ca1, aa1], axis=0)
    coef = jnp.concatenate([top, low], axis=1)
    slot = first_slot(row_count)
    basis = []
    for k in range(row_count):
        stays = new_slot[slot + k] == slot + k
        second = jnp.where(stays, near[k], arrived)
        for ref in terms:
            second = second + ref[k]
        basis.append(jnp.concatenate([moving[k], first[k], second], axis=0))
    order = moving.shape[2]
    both = dot32(coef, jnp.concatenate(basis, axis=1), left_t)
    for k in range(row_count):
        solution[k] = both[:count, k * order : (k + 1) * order]
        resid[k] = both[count:, k * order : (k + 1) * order]


def final(gram, solved, following, moving, first, near, new_slot, row, flags, terms):
    block = pl.BlockSpec(near.shape, lambda s: (0, 0, 0))
    last = pl.BlockSpec((1,) + near.shape[1:], lambda s: (terms[-1].shape[0] - 1, 0, 0))
    return pl.pallas_call(
        final_kernel,
        grid=(1,),
        out_shape=[jax.ShapeDtypeStruct(near.shape, f32)] * 2,
        in_specs=[vmem] * 6 + [smem, vmem, last, vmem] + [block] * len(terms),
        out_specs=[vmem] * 2,
        compiler_params=params(),
        name="final",
    )(gram, solved, following, moving, first, near, new_slot, row, terms[-1], flags, *terms)


def add_kernel(count, *refs):
    total = refs[0][...]
    for ref in refs[1:count]:
        total = total + ref[...]
    refs[-1][...] = total


def add_upper(terms, rows, *earlier):
    shape = (rows,) + terms[0].shape[1:]
    block = pl.BlockSpec(shape, lambda s: (1, 0, 0))
    return pl.pallas_call(
        functools.partial(add_kernel, len(terms)),
        grid=(1,),
        out_shape=jax.ShapeDtypeStruct(shape, f32),
        in_specs=[block] * len(terms) + [anywhere] * len(earlier),
        out_specs=vmem,
        compiler_params=params(),
        name="add_upper",
    )(*terms, *earlier)


def add_with_row_kernel(step, count, row, other, flags, *refs):
    terms, out, held = refs[:count], refs[-2], refs[-1]
    total = terms[0][...]
    for ref in terms[1:]:
        total = total + ref[...]
    out[: total.shape[0]] = total
    value = row[...]
    if step > 1:
        value = jnp.where(flags[8 * step : 8 * step + 1] > 0.5, other[0], value)
    out[total.shape[0]] = value
    held[...] = value


def add_with_row(terms, rows, row, flags, step, *earlier):
    shape = (rows,) + terms[0].shape[1:]
    block = pl.BlockSpec(shape, lambda s: (1, 0, 0))
    last = pl.BlockSpec((1,) + shape[1:], lambda s: (terms[-1].shape[0] - 1, 0, 0))
    return pl.pallas_call(
        functools.partial(add_with_row_kernel, step, len(terms)),
        grid=(1,),
        out_shape=[
            jax.ShapeDtypeStruct((rows + 1,) + shape[1:], f32),
            jax.ShapeDtypeStruct(row.shape, f32),
        ],
        in_specs=[vmem, last, vmem] + [block] * len(terms) + [anywhere] * len(earlier),
        out_specs=[vmem] * 2,
        compiler_params=params(),
        name="add_with_row",
    )(row, terms[-1], flags, *terms, *earlier)


def settle_kernel(index, sums, extra, partner, flags, *refs):
    out = refs[-1]
    out[:sums] = extra[:sums] + partner[:sums]
    if extra.shape[0] > sums:
        chosen = flags[8 * index : 8 * index + 1] > 0.5
        out[sums:] = jnp.where(chosen, partner[sums:], extra[sums:])


def settle(extra, partner, flags, index, sums, *earlier):
    return pl.pallas_call(
        functools.partial(settle_kernel, index, sums),
        out_shape=jax.ShapeDtypeStruct(extra.shape, f32),
        in_specs=[vmem] * 3 + [anywhere] * len(earlier),
        out_specs=vmem,
        compiler_params=params(),
        name="settle",
    )(extra, partner, flags, *earlier)


def leave_row_kernel(sums, extra, partner, flags, out, row):
    out[...] = extra[:sums] + partner[:sums]
    row[...] = jnp.where(flags[8:9] > 0.5, partner[sums:], extra[sums:])


def leave_row(extra, partner, flags, sums):
    order = extra.shape[1]
    return pl.pallas_call(
        functools.partial(leave_row_kernel, sums),
        out_shape=[
            jax.ShapeDtypeStruct((sums, order), f32),
            jax.ShapeDtypeStruct((extra.shape[0] - sums, order), f32),
        ],
        in_specs=[vmem] * 3,
        out_specs=[vmem] * 2,
        compiler_params=params(),
        name="leave_row",
    )(extra, partner, flags)


def last_gram_kernel(sums, partner, out, gram):
    total = sums[...] + partner[...]
    out[...] = total
    gram[...] = pack(grams_of(total)[3])


def last_gram(sums, partner):
    rows, order = sums.shape
    return pl.pallas_call(
        last_gram_kernel,
        out_shape=[
            jax.ShapeDtypeStruct((rows, order), f32),
            jax.ShapeDtypeStruct((order // 4, order), f32),
        ],
        in_specs=[vmem] * 2,
        out_specs=[vmem] * 2,
        compiler_params=params(),
        name="last_gram",
    )(sums, partner)


def add_whole(left, right, *earlier):
    return pl.pallas_call(
        functools.partial(add_kernel, 2),
        out_shape=jax.ShapeDtypeStruct(left.shape, f32),
        in_specs=[vmem] * 2 + [anywhere] * len(earlier),
        out_specs=vmem,
        compiler_params=params(),
        name="add_whole",
    )(left, right, *earlier)


def pass_on(value, *earlier):
    return pl.pallas_call(
        functools.partial(add_kernel, 1),
        out_shape=jax.ShapeDtypeStruct(value.shape, f32),
        in_specs=[vmem] + [anywhere] * len(earlier),
        out_specs=vmem,
        compiler_params=params(),
        name="pass_on",
    )(value, *earlier)


def join_kernel(count, *refs):
    out = refs[-1]
    rows = refs[0].shape[0]
    for index, ref in enumerate(refs[:count]):
        out[index * rows : (index + 1) * rows] = ref[...]


def join(pieces, *earlier):
    rows, order = pieces[0].shape
    return pl.pallas_call(
        functools.partial(join_kernel, len(pieces)),
        out_shape=jax.ShapeDtypeStruct((len(pieces) * rows, order), f32),
        in_specs=[vmem] * len(pieces) + [anywhere] * len(earlier),
        out_specs=vmem,
        compiler_params=params(),
        name="join",
    )(*pieces, *earlier)


def merge_kernel(edge, mine, other, *refs):
    out = refs[-1]
    out[:edge] = mine[:edge]
    out[edge : 2 * edge] = other[:edge]
    if mine.shape[0] > edge:
        out[2 * edge :] = mine[edge:] + other[edge:]


def merge_side(side, other, edge, *earlier):
    return pl.pallas_call(
        functools.partial(merge_kernel, edge),
        out_shape=jax.ShapeDtypeStruct((side.shape[0] + edge, side.shape[1]), f32),
        in_specs=[vmem] * 2 + [anywhere] * len(earlier),
        out_specs=vmem,
        compiler_params=params(),
        name="merge_side",
    )(side, other, *earlier)


def share_side(side, edge, part_count):
    mask = 1
    while 2 * mask < part_count:
        side = merge_side(side, swap(side, "group", mask), mask * edge)
        mask *= 2
    return side, swap(side, "group", mask)


def share_panel(piece, bulk_count, pieces, *earlier):
    own = [piece] + [swap(piece, "bulk", rel) for rel in range(2, bulk_count, 2)]
    size = len(own) // pieces
    joined = [join(own[i * size : (i + 1) * size]) for i in range(pieces - 1)]
    joined.append(join(own[(pieces - 1) * size :], *earlier))
    return own + [swap(one, "bulk", 1) for one in joined], joined[-1]


def local(rhs, diag_tiles, offdiag_blocks, coupling, col_index, load, new_slot):
    row_count, count, order = rhs.shape
    edge_rows, part_count = coupling.shape[:2]
    bulk_count = lax.axis_size("bulk")
    steps = bulk_count.bit_length() - 1
    masks = far_masks(bulk_count)[::-1]
    edge = edge_rows * count
    half_edges = part_count // 2 * edge
    indices = (col_index.T, load, new_slot)

    flat = rhs.reshape(row_count * count, order)
    side, other_side = share_side(flat[:edge], edge, part_count)
    keep, send = returned(rhs, offdiag_blocks, *indices, bulk_count, False)
    panel, joined = share_panel(flat, bulk_count, 2, side)
    terms = [keep, swap(send, "bulk", 1)]
    rows = bulk_count // 2 * row_count
    for step, mask in enumerate(masks):
        rows //= 2
        total = add_upper(terms, rows, *([joined] if step else []))
        terms.append(swap(total, "bulk", mask))
    near, moving, packed, flags = near_part(
        panel, rhs, offdiag_blocks, diag_tiles, *indices, False
    )
    side = merge_side(side, other_side, half_edges, near)
    first, side = gather_first(rhs, near, terms, coupling, side, packed)

    side, other_side = share_side(side, edge, part_count)
    keep, send = returned(first, offdiag_blocks, *indices, bulk_count, True)
    panel, joined = share_panel(
        first.reshape(row_count * count, order), bulk_count, 1, side, keep
    )
    terms = [keep, swap(pass_on(send, joined), "bulk", 1)]
    rows = bulk_count // 4 * row_count
    terms.append(swap(add_upper(terms, rows), "bulk", masks[0]))
    near, moved, packed = near_part(panel, first, offdiag_blocks, diag_tiles, *indices, True)
    side = merge_side(side, other_side, half_edges, near)
    near, extra = edge_second(first, near, packed, coupling, side, new_slot)

    sums = count + 8
    extra = settle(extra, swap(extra, "bulk", 1), flags, 0, sums, terms[-1])
    extra, row = leave_row(extra, swap(extra, "bulk", masks[0]), flags, sums)
    mask = 4
    while 2 * mask < bulk_count:
        extra = settle(extra, swap(extra, "bulk", mask), flags, 0, sums)
        mask *= 2
    extra, gram = last_gram(extra, swap(extra, "bulk", mask))
    for step in range(1, steps - 1):
        rows //= 2
        total, row = add_with_row(terms, rows, row, flags, step, extra)
        terms.append(swap(total, "bulk", masks[step]))
    solved = small_call(first_solves_kernel, count, 2, "first_solves", extra)
    following = small_call(next_gram_kernel, count, 3, "next_gram", extra, solved)
    mask = 1
    while mask < part_count:
        partner = swap(gram, "group", mask)
        gram = add_whole(gram, partner, *([solved] if mask == 1 else []))
        mask *= 2
    return tuple(
        final(gram, solved, following, moving, moved, near, new_slot, row, flags, terms)
    )


def solution(mesh):
    rows = P(("group", "bulk"))
    return jax.shard_map(
        local,
        mesh=mesh,
        in_specs=(rows, rows, rows, rows, P(), P(), P()),
        out_specs=(rows, rows),
        check_vma=False,
    )
```

```python
import functools

import jax
import jax.numpy as jnp
from jax import lax
from jax.experimental import pallas as pl
from jax.experimental.pallas import tpu as pltpu
from jax.sharding import PartitionSpec as P

shift = 4.0
f32 = jnp.float32
bf16 = jnp.bfloat16
normal = (((1,), (0,)), ((), ()))
right_t = (((1,), (1,)), ((), ()))
left_t = (((0,), (0,)), ((), ()))
vmem = pl.BlockSpec(memory_space=pltpu.VMEM)
smem = pl.BlockSpec(memory_space=pltpu.SMEM)
anywhere = pl.BlockSpec(memory_space=pl.ANY)
vmem_bytes = 40 * 2**20
all_vmem = 60 * 2**20


def params(limit=vmem_bytes):
    return pltpu.CompilerParams(vmem_limit_bytes=limit)


def swap(value, axis, mask):
    pairs = [(source, source ^ mask) for source in range(lax.axis_size(axis))]
    return lax.ppermute(value, axis, pairs)


def split(value):
    high = value.astype(bf16)
    return high, (value - high.astype(f32)).astype(bf16)


def dot16(left, right, dims):
    return lax.dot_general(left, right, dims, preferred_element_type=f32)


def dot32(left, right, dims=normal):
    return lax.dot_general(
        left, right, dims, preferred_element_type=f32, precision=lax.Precision.HIGHEST
    )


def split_rows(vectors):
    high, low = split(vectors)
    return jnp.concatenate([high, low], axis=0)


def times_tile(rows, tile, dims):
    count = rows.shape[0] // 2
    high, low = split(tile)
    left = jnp.concatenate([rows[:count], rows[count:], rows[:count]], axis=1)
    return dot16(left, jnp.concatenate([high, high, low], axis=dims[0][1][0]), dims)


def dot24(left, right):
    high, low = split(left)
    other_high, other_low = split(right)
    left = jnp.concatenate([high, low, high], axis=1)
    return dot16(left, jnp.concatenate([other_high, other_high, other_low], axis=1), right_t)


def pack(gram):
    half = gram.shape[0] // 2
    return jnp.concatenate([gram[:half], gram[half:]], axis=1)


def unpack(packed):
    half = packed.shape[1] // 2
    return jnp.concatenate([packed[:, :half], packed[:, half:]], axis=0)


def above(count):
    rows = lax.broadcasted_iota(jnp.int32, (count, count), 0)
    cols = lax.broadcasted_iota(jnp.int32, (count, count), 1)
    return cols > rows, cols == rows


def identity(count):
    return above(count)[1].astype(f32)


def join_symmetric(upper, lower):
    over, diagonal = above(upper.shape[0])
    row = jnp.sum(jnp.where(diagonal, upper, 0.0), axis=0, keepdims=True)
    return jnp.where(over, upper, lower), row


def part_symmetric(joined, row):
    over, diagonal = above(joined.shape[0])
    turned = joined.T
    upper = jnp.where(diagonal, row, jnp.where(over, joined, turned))
    return upper, jnp.where(over, turned, joined)


def sym(gram):
    return 0.5 * (gram + gram.T)


def first_slot(row_count):
    device = lax.axis_index("group") * lax.axis_size("bulk") + lax.axis_index("bulk")
    return device * row_count


def live(load_ref, slot, tile):
    return jnp.where(tile < load_ref[slot], 1.0, 0.0)


def far_masks(bulk_count):
    masks = []
    bit = bulk_count // 2
    while bit >= 4:
        masks += [bit | bit // 2, bit // 2]
        bit //= 4
    return masks + ([bit] if bit == 2 else [])


def owed_place(rel, bulk_count):
    place = 0
    index = 0
    bit = bulk_count.bit_length() - 2
    while bit >= 2:
        high = (rel >> bit) & 1
        low = (rel >> (bit - 1)) & 1
        place = place | (high << index) | ((high ^ low) << (index + 1))
        index += 2
        bit -= 2
    if bit == 1:
        place = place | (((rel >> 1) & 1) << index)
        index += 1
    return place | ((rel & 1) << index)


def returned_kernel(bulk_count, moved, vectors, tiles, col, load, new_slot, *refs):
    keep, send, total = refs[-3:]
    row_count = vectors.shape[0]
    me = lax.axis_index("bulk")
    base = lax.axis_index("group") * bulk_count * row_count
    s = pl.program_id(0)
    slot = first_slot(row_count) + s

    @pl.when(s == 0)
    def _():
        total[...] = jnp.zeros_like(total)

    rows = split_rows(vectors[s])
    for t in range(tiles.shape[1]):
        product = times_tile(rows, tiles[0, t], normal)
        target = col[t, slot]
        if moved:
            target = new_slot[target]
        target = target - base
        owner = target // row_count
        place = owed_place(owner ^ me, bulk_count) * row_count + target - owner * row_count
        total[place] += live(load, slot, t) * product

    @pl.when(s == row_count - 1)
    def _():
        half = total.shape[0] // 2
        keep[...] = total[:half]
        send[...] = total[half:]


def returned(vectors, tiles, col, load, new_slot, bulk_count, moved, *earlier):
    row_count, count, order = vectors.shape
    tile_count = tiles.shape[1]
    half = (bulk_count * row_count // 2, count, order)
    return pl.pallas_call(
        functools.partial(returned_kernel, bulk_count, moved),
        grid=(row_count,),
        out_shape=[jax.ShapeDtypeStruct(half, f32)] * 2,
        in_specs=[
            vmem,
            pl.BlockSpec((1, tile_count, order, order), lambda s: (s, 0, 0, 0)),
            smem,
            smem,
            smem,
        ]
        + [anywhere] * len(earlier),
        out_specs=[vmem] * 2,
        scratch_shapes=[pltpu.VMEM((2 * half[0], count, order), f32)],
        compiler_params=params(vmem_bytes if moved else all_vmem),
        name="returned_moved" if moved else "returned",
    )(vectors, tiles, col, load, new_slot, *earlier)


def near_kernel(bulk_count, pieces, second, *refs):
    panel, refs = refs[:pieces], refs[pieces:]
    vectors, tiles, diag, col, load, new_slot, near, moving, packed, *more, rows_of, gram = refs
    row_count, count = vectors.shape[:2]
    me = lax.axis_index("bulk")
    mine = lax.axis_index("group")
    base = mine * bulk_count * row_count
    s = pl.program_id(0)
    slot = first_slot(row_count) + s
    half_rows = bulk_count * row_count // 2
    held = [piece.shape[0] // count for piece in panel]
    starts = [sum(held[:index]) for index in range(pieces)]

    def place_of(target):
        target = target - base
        owner = target // row_count
        rel = owner ^ me
        return (rel & 1) * half_rows + (rel >> 1) * row_count + target - owner * row_count

    @pl.when(s == 0)
    def _():
        for piece, first, rows in zip(panel, starts, held):
            for k in range(rows):
                rows_of[first + k] = split_rows(piece[k * count : (k + 1) * count])
        gram[...] = jnp.zeros_like(gram)

    left, right = [], []
    for t in range(tiles.shape[1]):
        rows = rows_of[place_of(col[t, slot])]
        rows = jnp.where(t < load[slot], rows, jnp.zeros_like(rows))
        high, low = split(tiles[0, t])
        left += [rows[:count], rows[count:], rows[:count]]
        right += [high, high, low]
    direct = dot16(jnp.concatenate(left, axis=1), jnp.concatenate(right, axis=1), right_t)
    value = vectors[s]
    near_value = times_tile(split_rows(value), diag[0], right_t)
    near[s] = near_value + direct
    if second:
        gram[...] += dot24(value, near_value + 2.0 * direct)
    else:
        gram[...] += dot24(value, value)

    arriving = new_slot[slot]
    incoming = place_of(arriving)
    for piece, first, rows in zip(panel, starts, held):

        @pl.when((incoming >= first) & (incoming < first + rows))
        def _(piece=piece, first=first):
            start = pl.multiple_of((incoming - first) * count, count)
            moving[s] = piece[pl.ds(start, count)]

    if not second:
        (flags,) = more

        @pl.when(arriving != slot)
        def _():
            route = owed_place(((arriving - base) // row_count) ^ me, bulk_count)
            steps = flags.shape[0] // 8
            for index in range(steps):
                bit = ((route >> (steps - 1 - index)) & 1).astype(f32)
                flags[8 * index : 8 * index + 8] = jnp.full((8, flags.shape[1]), bit, f32)

    @pl.when(s == row_count - 1)
    def _():
        packed[...] = pack(gram[...])


def near_part(panel, vectors, tiles, diag, col, load, new_slot, second):
    row_count, count, order = vectors.shape
    bulk_count = sum(piece.shape[0] for piece in panel) // (row_count * count)
    tile_count = tiles.shape[1]
    shapes = [vectors.shape, vectors.shape, (count // 2, order)]
    if not second:
        shapes += [(8 * (bulk_count.bit_length() - 1), order)]
    return pl.pallas_call(
        functools.partial(near_kernel, bulk_count, len(panel), second),
        grid=(row_count,),
        out_shape=[jax.ShapeDtypeStruct(shape, f32) for shape in shapes],
        in_specs=[vmem] * len(panel)
        + [
            vmem,
            pl.BlockSpec((1, tile_count, order, order), lambda s: (s, 0, 0, 0)),
            pl.BlockSpec((1, order, order), lambda s: (s, 0, 0)),
            smem,
            smem,
            smem,
        ],
        out_specs=[vmem] * len(shapes),
        scratch_shapes=[
            pltpu.VMEM((bulk_count * row_count, 2 * count, order), bf16),
            pltpu.VMEM((count, count), f32),
        ],
        compiler_params=params(),
        name="near_second" if second else "near_first",
    )(*panel, vectors, tiles, diag, col, load, new_slot)


def crossed(side, coupling, k):
    edge_rows, part_count = coupling.shape[:2]
    count = side.shape[1] // 2
    mine = lax.axis_index("group")
    total = None
    for h in range(part_count):
        start = (h * edge_rows + k) * count
        rows = split_rows(side[start : start + count])
        term = times_tile(rows, coupling[k, mine ^ h], right_t)
        total = term if total is None else total + term
    return total


def gather_first_kernel(vectors, near, keep, *refs):
    received = refs[:-5]
    coupling, old_side, packed, first, side = refs[-5:]
    row_count, count = vectors.shape[:2]
    half = count // 2
    edge_rows = (side.shape[0] - 2 * half - 8) // count
    grams = [None, None]
    for k in range(row_count):
        value = near[k] + keep[k]
        for ref in received:
            value = value + ref[k]
        if k < edge_rows:
            value = value + crossed(old_side, coupling, k)
        first[k] = value
        if k < edge_rows:
            side[k * count : (k + 1) * count] = value
        terms = (dot24(vectors[k], value), dot24(value, value))
        grams = [term if old is None else old + term for old, term in zip(grams, terms)]
    start = edge_rows * count
    joined, row = join_symmetric(unpack(packed[...]), grams[1])
    side[start : start + half] = pack(joined)
    side[start + half : start + 2 * half] = pack(sym(grams[0]))
    rows = jnp.concatenate([row, jnp.zeros_like(row)], axis=1)
    side[start + 2 * half :] = jnp.broadcast_to(rows, (8, 2 * count))


def gather_first(vectors, near, terms, coupling, old_side, packed):
    row_count, count, order = vectors.shape
    edge_rows = coupling.shape[0]
    shapes = [vectors.shape, (edge_rows * count + count + 8, order)]
    specs = [pl.BlockSpec((row_count, count, order), lambda s: (0, 0, 0))] * (2 + len(terms))
    return pl.pallas_call(
        gather_first_kernel,
        grid=(1,),
        out_shape=[jax.ShapeDtypeStruct(shape, f32) for shape in shapes],
        in_specs=specs + [vmem] * 3,
        out_specs=[vmem] * 2,
        compiler_params=params(),
        name="gather_first",
    )(vectors, near, *terms, coupling, old_side, packed)


def edge_second_kernel(first, near, packed, coupling, side, new_slot, more, extra):
    row_count, count = first.shape[:2]
    edge_rows, part_count = coupling.shape[:2]
    half = count // 2
    gram = unpack(packed[...])
    for k in range(edge_rows):
        value = crossed(side, coupling, k)
        gram = gram + dot24(first[k], value)
        more[k] = value
    start = part_count * edge_rows * count
    joined, row = join_symmetric(unpack(side[start + half : start + 2 * half]), sym(gram))
    extra[:count] = jnp.concatenate([unpack(side[start : start + half]), joined], axis=1)
    row = jnp.concatenate([jnp.zeros_like(row), row], axis=1)
    extra[count : count + 8] = side[start + 2 * half :] + jnp.broadcast_to(row, (8, 2 * count))
    slot = first_slot(row_count)
    for k in range(edge_rows, row_count):

        @pl.when(new_slot[slot + k] != slot + k)
        def _(k=k):
            extra[count + 8 :] = near[k]


def edge_second(first, near, packed, coupling, side, new_slot):
    count, order = first.shape[1:]
    shapes = [(coupling.shape[0], count, order), (2 * count + 8, order)]
    return pl.pallas_call(
        edge_second_kernel,
        out_shape=[jax.ShapeDtypeStruct(shape, f32) for shape in shapes],
        in_specs=[vmem] * 5 + [smem],
        out_specs=[vmem] * 2,
        compiler_params=params(),
        name="edge_second",
    )(first, near, packed, coupling, side, new_slot)


def spread_row(rows, index):
    return jnp.broadcast_to(rows[index : index + 1], rows.shape)


def inverse_factors(matrices):
    count = matrices[0].shape[0]
    step = 8
    shape = (step, 2 * count)
    eye = identity(count)
    sub = lax.broadcasted_iota(jnp.int32, shape, 0)
    work = []
    for matrix in matrices:
        both = jnp.concatenate([matrix, eye], axis=1)
        work.append([both[i : i + step] for i in range(0, count, step)])
    for block in range(count // step):
        start = block * step
        for w in work:
            cols = [
                [jnp.broadcast_to(rows[:, start + m : start + m + 1], shape) for m in range(step)]
                for rows in w[block:]
            ]
            factor = [[None] * step for _ in range(step)]
            scales, pivots = [], []
            for m in range(step):
                value = spread_row(cols[0][m], m)
                row = spread_row(w[block], m)
                for u in range(m):
                    value = value - factor[m][u] * factor[m][u]
                    row = row - factor[m][u] * pivots[u]
                scales.append(lax.rsqrt(value))
                pivots.append(row * scales[m])
                for v in range(m + 1, step):
                    value = spread_row(cols[0][m], v)
                    for u in range(m):
                        value = value - factor[v][u] * factor[m][u]
                    factor[v][m] = value * scales[m]
            for i in range(block + 1, count // step):
                left = []
                for m in range(step):
                    value = cols[i - block][m]
                    for u in range(m):
                        value = value - left[u] * factor[m][u]
                    left.append(value * scales[m])
                terms = [one * pivot for one, pivot in zip(left, pivots)]
                while len(terms) > 1:
                    terms = [x + y for x, y in zip(terms[::2], terms[1::2])]
                w[i] = w[i] - terms[0]
            rows = pivots[0]
            for m in range(1, step):
                rows = jnp.where(sub == m, pivots[m], rows)
            w[block] = rows
    return [jnp.concatenate(w, axis=0)[:, count:] for w in work]


def solve(inverse_factor, right):
    return dot32(inverse_factor, dot32(inverse_factor, right), left_t)


def grams_of(sums):
    count = sums.shape[1] // 2
    row = sums[count : count + 1]
    g0, g2 = part_symmetric(sums[:count, :count], row[:, :count])
    g1, g3 = part_symmetric(sums[:count, count:], row[:, count:])
    return g0, g1, g2, g3


def first_solves_kernel(extra, out):
    g0, g1, _, _ = grams_of(extra[...])
    factor_pq, factor_rr = inverse_factors([shift * g0 + g1, g0])
    out[0] = solve(factor_pq, g0)
    out[1] = dot32(factor_rr, factor_rr, left_t)


def next_gram_kernel(extra, solved, out):
    g0, g1, g2, _ = grams_of(extra[...])
    a, inverse_rr = solved[0], solved[1]
    count = a.shape[0]
    m = identity(count) - shift * a
    by_a = dot32(jnp.concatenate([g0, g1, g2], axis=0), a)
    g0a, g1a, g2a = (by_a[i * count : (i + 1) * count] for i in range(3))
    g0m, g1m = g0 - shift * g0a, g1 - shift * g1a
    left = jnp.concatenate([m, a], axis=0)
    g_new = sym(dot32(left, jnp.concatenate([g0m - g1a, g2a - g1m], axis=0), left_t))
    c = m + dot32(inverse_rr, g_new)
    by_c = dot32(jnp.concatenate([shift * g0 + g1, shift * g1 + g2], axis=0), c)
    left = jnp.concatenate([c, a], axis=0)
    upper = by_c[:count] - (shift * g1a + g2a)
    lower = shift * g2a - by_c[count:]
    out[0] = c
    out[1] = g_new
    out[2] = dot32(left, jnp.concatenate([upper, lower], axis=0), left_t)


def small_call(kernel, count, matrices, name, *operands):
    return pl.pallas_call(
        kernel,
        out_shape=jax.ShapeDtypeStruct((matrices, count, count), f32),
        in_specs=[vmem] * len(operands),
        out_specs=vmem,
        compiler_params=params(),
        name=name,
    )(*operands)


def final_kernel(gram, solved, following, moving, first, near, more, new_slot, row, *refs):
    last_row, flags, *terms, solution, resid = refs
    row_count, count = moving.shape[:2]
    arrived = jnp.where(flags[flags.shape[0] - 8 :][:1] > 0.5, last_row[0], row[...])
    a, c, g_new = solved[0], following[0], following[1]
    g3 = sym(unpack(gram[...]))
    g_pq = sym(following[2] + dot32(a, dot32(g3, a), left_t))
    (factor,) = inverse_factors([g_pq])
    a1 = solve(factor, g_new)
    by_a1 = dot32(jnp.concatenate([a, c], axis=0), a1)
    aa1, ca1 = by_a1[:count], by_a1[count:]
    m = identity(count) - shift * a
    top = jnp.concatenate([a + ca1, -aa1, jnp.zeros_like(a)], axis=0)
    low = jnp.concatenate([m - shift * ca1, shift * aa1 - a - ca1, aa1], axis=0)
    coef = jnp.concatenate([top, low], axis=1)
    slot = first_slot(row_count)
    basis = []
    for k in range(row_count):
        stays = new_slot[slot + k] == slot + k
        second = jnp.where(stays, near[k], arrived)
        if k < more.shape[0]:
            second = second + more[k]
        for ref in terms:
            second = second + ref[k]
        basis.append(jnp.concatenate([moving[k], first[k], second], axis=0))
    order = moving.shape[2]
    both = dot32(coef, jnp.concatenate(basis, axis=1), left_t)
    for k in range(row_count):
        solution[k] = both[:count, k * order : (k + 1) * order]
        resid[k] = both[count:, k * order : (k + 1) * order]


def final(gram, solved, following, moving, first, near, more, new_slot, row, flags, terms):
    block = pl.BlockSpec(near.shape, lambda s: (0, 0, 0))
    last = pl.BlockSpec((1,) + near.shape[1:], lambda s: (terms[-1].shape[0] - 1, 0, 0))
    return pl.pallas_call(
        final_kernel,
        grid=(1,),
        out_shape=[jax.ShapeDtypeStruct(near.shape, f32)] * 2,
        in_specs=[vmem] * 7 + [smem, vmem, last, vmem] + [block] * len(terms),
        out_specs=[vmem] * 2,
        compiler_params=params(),
        name="final",
    )(gram, solved, following, moving, first, near, more, new_slot, row, terms[-1], flags, *terms)


def add_kernel(count, *refs):
    total = refs[0][...]
    for ref in refs[1:count]:
        total = total + ref[...]
    refs[-1][...] = total


def add_upper(terms, rows, *earlier):
    shape = (rows,) + terms[0].shape[1:]
    block = pl.BlockSpec(shape, lambda s: (1, 0, 0))
    return pl.pallas_call(
        functools.partial(add_kernel, len(terms)),
        grid=(1,),
        out_shape=jax.ShapeDtypeStruct(shape, f32),
        in_specs=[block] * len(terms) + [anywhere] * len(earlier),
        out_specs=vmem,
        compiler_params=params(),
        name="add_upper",
    )(*terms, *earlier)


def add_with_row_kernel(step, count, row, other, flags, *refs):
    terms, out, held = refs[:count], refs[-2], refs[-1]
    total = terms[0][...]
    for ref in terms[1:]:
        total = total + ref[...]
    out[: total.shape[0]] = total
    value = row[...]
    if step > 1:
        value = jnp.where(flags[8 * step : 8 * step + 1] > 0.5, other[0], value)
    out[total.shape[0]] = value
    held[...] = value


def add_with_row(terms, rows, row, flags, step, *earlier):
    shape = (rows,) + terms[0].shape[1:]
    block = pl.BlockSpec(shape, lambda s: (1, 0, 0))
    last = pl.BlockSpec((1,) + shape[1:], lambda s: (terms[-1].shape[0] - 1, 0, 0))
    return pl.pallas_call(
        functools.partial(add_with_row_kernel, step, len(terms)),
        grid=(1,),
        out_shape=[
            jax.ShapeDtypeStruct((rows + 1,) + shape[1:], f32),
            jax.ShapeDtypeStruct(row.shape, f32),
        ],
        in_specs=[vmem, last, vmem] + [block] * len(terms) + [anywhere] * len(earlier),
        out_specs=[vmem] * 2,
        compiler_params=params(),
        name="add_with_row",
    )(row, terms[-1], flags, *terms, *earlier)


def settle_kernel(index, sums, extra, partner, flags, *refs):
    out = refs[-1]
    out[:sums] = extra[:sums] + partner[:sums]
    if extra.shape[0] > sums:
        chosen = flags[8 * index : 8 * index + 1] > 0.5
        out[sums:] = jnp.where(chosen, partner[sums:], extra[sums:])


def settle(extra, partner, flags, index, sums, *earlier):
    return pl.pallas_call(
        functools.partial(settle_kernel, index, sums),
        out_shape=jax.ShapeDtypeStruct(extra.shape, f32),
        in_specs=[vmem] * 3 + [anywhere] * len(earlier),
        out_specs=vmem,
        compiler_params=params(),
        name="settle",
    )(extra, partner, flags, *earlier)


def leave_row_kernel(sums, extra, partner, flags, out, row):
    out[...] = extra[:sums] + partner[:sums]
    row[...] = jnp.where(flags[8:9] > 0.5, partner[sums:], extra[sums:])


def leave_row(extra, partner, flags, sums):
    order = extra.shape[1]
    return pl.pallas_call(
        functools.partial(leave_row_kernel, sums),
        out_shape=[
            jax.ShapeDtypeStruct((sums, order), f32),
            jax.ShapeDtypeStruct((extra.shape[0] - sums, order), f32),
        ],
        in_specs=[vmem] * 3,
        out_specs=[vmem] * 2,
        compiler_params=params(),
        name="leave_row",
    )(extra, partner, flags)


def last_gram_kernel(sums, partner, out, gram):
    total = sums[...] + partner[...]
    out[...] = total
    gram[...] = pack(grams_of(total)[3])


def last_gram(sums, partner):
    rows, order = sums.shape
    return pl.pallas_call(
        last_gram_kernel,
        out_shape=[
            jax.ShapeDtypeStruct((rows, order), f32),
            jax.ShapeDtypeStruct((order // 4, order), f32),
        ],
        in_specs=[vmem] * 2,
        out_specs=[vmem] * 2,
        compiler_params=params(),
        name="last_gram",
    )(sums, partner)


def add_whole(left, right, *earlier):
    return pl.pallas_call(
        functools.partial(add_kernel, 2),
        out_shape=jax.ShapeDtypeStruct(left.shape, f32),
        in_specs=[vmem] * 2 + [anywhere] * len(earlier),
        out_specs=vmem,
        compiler_params=params(),
        name="add_whole",
    )(left, right, *earlier)


def pass_on(value, *earlier):
    return pl.pallas_call(
        functools.partial(add_kernel, 1),
        out_shape=jax.ShapeDtypeStruct(value.shape, f32),
        in_specs=[vmem] + [anywhere] * len(earlier),
        out_specs=vmem,
        compiler_params=params(),
        name="pass_on",
    )(value, *earlier)


def join_kernel(count, *refs):
    out = refs[-1]
    rows = refs[0].shape[0]
    for index, ref in enumerate(refs[:count]):
        out[index * rows : (index + 1) * rows] = ref[...]


def join(pieces, *earlier):
    rows, order = pieces[0].shape
    return pl.pallas_call(
        functools.partial(join_kernel, len(pieces)),
        out_shape=jax.ShapeDtypeStruct((len(pieces) * rows, order), f32),
        in_specs=[vmem] * len(pieces) + [anywhere] * len(earlier),
        out_specs=vmem,
        compiler_params=params(),
        name="join",
    )(*pieces, *earlier)


def merge_kernel(edge, mine, other, *refs):
    out = refs[-1]
    out[:edge] = mine[:edge]
    out[edge : 2 * edge] = other[:edge]
    if mine.shape[0] > edge:
        out[2 * edge :] = mine[edge:] + other[edge:]


def merge_side(side, other, edge, *earlier):
    return pl.pallas_call(
        functools.partial(merge_kernel, edge),
        out_shape=jax.ShapeDtypeStruct((side.shape[0] + edge, side.shape[1]), f32),
        in_specs=[vmem] * 2 + [anywhere] * len(earlier),
        out_specs=vmem,
        compiler_params=params(),
        name="merge_side",
    )(side, other, *earlier)


def share_side(side, edge, part_count):
    mask = 1
    while 2 * mask < part_count:
        side = merge_side(side, swap(side, "group", mask), mask * edge)
        mask *= 2
    return side, swap(side, "group", mask)


def share_panel(piece, bulk_count, pieces, *earlier):
    own = [piece] + [swap(piece, "bulk", rel) for rel in range(2, bulk_count, 2)]
    size = len(own) // pieces
    joined = [join(own[i * size : (i + 1) * size]) for i in range(pieces - 1)]
    joined.append(join(own[(pieces - 1) * size :], *earlier))
    return own + [swap(one, "bulk", 1) for one in joined], joined[-1]


def local(rhs, diag_tiles, offdiag_blocks, coupling, col_index, load, new_slot):
    row_count, count, order = rhs.shape
    edge_rows, part_count = coupling.shape[:2]
    bulk_count = lax.axis_size("bulk")
    steps = bulk_count.bit_length() - 1
    masks = far_masks(bulk_count)[::-1]
    edge = edge_rows * count
    half_edges = part_count // 2 * edge
    indices = (col_index.T, load, new_slot)

    flat = rhs.reshape(row_count * count, order)
    side, other_side = share_side(flat[:edge], edge, part_count)
    keep, send = returned(rhs, offdiag_blocks, *indices, bulk_count, False)
    panel, joined = share_panel(flat, bulk_count, 2, side)
    terms = [keep, swap(send, "bulk", 1)]
    rows = bulk_count // 2 * row_count
    for step, mask in enumerate(masks):
        rows //= 2
        total = add_upper(terms, rows, *([joined] if step else []))
        terms.append(swap(total, "bulk", mask))
    near, moving, packed, flags = near_part(
        panel, rhs, offdiag_blocks, diag_tiles, *indices, False
    )
    side = merge_side(side, other_side, half_edges, near)
    first, side = gather_first(rhs, near, terms, coupling, side, packed)

    side, other_side = share_side(side, edge, part_count)
    keep, send = returned(first, offdiag_blocks, *indices, bulk_count, True)
    panel, joined = share_panel(
        first.reshape(row_count * count, order), bulk_count, 1, side, keep
    )
    terms = [keep, swap(pass_on(send, joined), "bulk", 1)]
    rows = bulk_count // 4 * row_count
    terms.append(swap(add_upper(terms, rows), "bulk", masks[0]))
    near, moved, packed = near_part(panel, first, offdiag_blocks, diag_tiles, *indices, True)
    side = merge_side(side, other_side, half_edges, near)
    more, extra = edge_second(first, near, packed, coupling, side, new_slot)

    sums = count + 8
    extra = settle(extra, swap(extra, "bulk", 1), flags, 0, sums, terms[-1])
    extra, row = leave_row(extra, swap(extra, "bulk", masks[0]), flags, sums)
    mask = 4
    while 2 * mask < bulk_count:
        extra = settle(extra, swap(extra, "bulk", mask), flags, 0, sums)
        mask *= 2
    extra, gram = last_gram(extra, swap(extra, "bulk", mask))
    for step in range(1, steps - 1):
        rows //= 2
        total, row = add_with_row(terms, rows, row, flags, step, extra)
        terms.append(swap(total, "bulk", masks[step]))
    solved = small_call(first_solves_kernel, count, 2, "first_solves", extra)
    following = small_call(next_gram_kernel, count, 3, "next_gram", extra, solved)
    mask = 1
    while mask < part_count:
        partner = swap(gram, "group", mask)
        gram = add_whole(gram, partner, *([solved] if mask == 1 else []))
        mask *= 2
    return tuple(
        final(gram, solved, following, moving, moved, near, more, new_slot, row, flags, terms)
    )


def solution(mesh):
    rows = P(("group", "bulk"))
    return jax.shard_map(
        local,
        mesh=mesh,
        in_specs=(rows, rows, rows, rows, P(), P(), P()),
        out_specs=(rows, rows),
        check_vma=False,
    )
```

```python
import functools

import jax
import jax.numpy as jnp
from jax import lax
from jax.experimental import pallas as pl
from jax.experimental.pallas import tpu as pltpu
from jax.sharding import PartitionSpec as P

shift = 4.0
f32 = jnp.float32
bf16 = jnp.bfloat16
normal = (((1,), (0,)), ((), ()))
right_t = (((1,), (1,)), ((), ()))
left_t = (((0,), (0,)), ((), ()))
vmem = pl.BlockSpec(memory_space=pltpu.VMEM)
smem = pl.BlockSpec(memory_space=pltpu.SMEM)
anywhere = pl.BlockSpec(memory_space=pl.ANY)
vmem_bytes = 40 * 2**20
all_vmem = 56 * 2**20


def params(limit=vmem_bytes):
    return pltpu.CompilerParams(vmem_limit_bytes=limit)


def swap(value, axis, mask):
    pairs = [(source, source ^ mask) for source in range(lax.axis_size(axis))]
    return lax.ppermute(value, axis, pairs)


def split(value):
    high = value.astype(bf16)
    return high, (value - high.astype(f32)).astype(bf16)


def dot16(left, right, dims):
    return lax.dot_general(left, right, dims, preferred_element_type=f32)


def dot32(left, right, dims=normal):
    return lax.dot_general(
        left, right, dims, preferred_element_type=f32, precision=lax.Precision.HIGHEST
    )


def split_rows(vectors):
    high, low = split(vectors)
    return jnp.concatenate([high, low], axis=0)


def times_tile(rows, tile, dims):
    count = rows.shape[0] // 2
    high, low = split(tile)
    left = jnp.concatenate([rows[:count], rows[count:], rows[:count]], axis=1)
    return dot16(left, jnp.concatenate([high, high, low], axis=dims[0][1][0]), dims)


def dot24(left, right):
    high, low = split(left)
    other_high, other_low = split(right)
    left = jnp.concatenate([high, low, high], axis=1)
    return dot16(left, jnp.concatenate([other_high, other_high, other_low], axis=1), right_t)


def pack(gram):
    half = gram.shape[0] // 2
    return jnp.concatenate([gram[:half], gram[half:]], axis=1)


def unpack(packed):
    half = packed.shape[1] // 2
    return jnp.concatenate([packed[:, :half], packed[:, half:]], axis=0)


def above(count):
    rows = lax.broadcasted_iota(jnp.int32, (count, count), 0)
    cols = lax.broadcasted_iota(jnp.int32, (count, count), 1)
    return cols > rows, cols == rows


def identity(count):
    return above(count)[1].astype(f32)


def join_symmetric(upper, lower):
    over, diagonal = above(upper.shape[0])
    row = jnp.sum(jnp.where(diagonal, upper, 0.0), axis=0, keepdims=True)
    return jnp.where(over, upper, lower), row


def part_symmetric(joined, row):
    over, diagonal = above(joined.shape[0])
    turned = joined.T
    upper = jnp.where(diagonal, row, jnp.where(over, joined, turned))
    return upper, jnp.where(over, turned, joined)


def sym(gram):
    return 0.5 * (gram + gram.T)


def first_slot(row_count):
    device = lax.axis_index("group") * lax.axis_size("bulk") + lax.axis_index("bulk")
    return device * row_count


def live(load_ref, slot, tile):
    return jnp.where(tile < load_ref[slot], 1.0, 0.0)


def far_masks(bulk_count):
    masks = []
    bit = bulk_count // 2
    while bit >= 4:
        masks += [bit | bit // 2, bit // 2]
        bit //= 4
    return masks + ([bit] if bit == 2 else [])


def owed_place(rel, bulk_count):
    place = 0
    index = 0
    bit = bulk_count.bit_length() - 2
    while bit >= 2:
        high = (rel >> bit) & 1
        low = (rel >> (bit - 1)) & 1
        place = place | (high << index) | ((high ^ low) << (index + 1))
        index += 2
        bit -= 2
    if bit == 1:
        place = place | (((rel >> 1) & 1) << index)
        index += 1
    return place | ((rel & 1) << index)


def returned_kernel(bulk_count, moved, vectors, tiles, col, load, new_slot, *refs):
    keep, send, total = refs[-3:]
    row_count = vectors.shape[0]
    me = lax.axis_index("bulk")
    base = lax.axis_index("group") * bulk_count * row_count
    s = pl.program_id(0)
    slot = first_slot(row_count) + s

    @pl.when(s == 0)
    def _():
        total[...] = jnp.zeros_like(total)

    rows = split_rows(vectors[s])
    for t in range(tiles.shape[1]):
        product = times_tile(rows, tiles[0, t], normal)
        target = col[t, slot]
        if moved:
            target = new_slot[target]
        target = target - base
        owner = target // row_count
        place = owed_place(owner ^ me, bulk_count) * row_count + target - owner * row_count
        total[place] += live(load, slot, t) * product

    @pl.when(s == row_count - 1)
    def _():
        half = total.shape[0] // 2
        keep[...] = total[:half]
        send[...] = total[half:]


def returned(vectors, tiles, col, load, new_slot, bulk_count, moved, *earlier):
    row_count, count, order = vectors.shape
    tile_count = tiles.shape[1]
    half = (bulk_count * row_count // 2, count, order)
    return pl.pallas_call(
        functools.partial(returned_kernel, bulk_count, moved),
        grid=(row_count,),
        out_shape=[jax.ShapeDtypeStruct(half, f32) if moved else pltpu.VMEM(half, f32)] * 2,
        in_specs=[
            vmem,
            pl.BlockSpec((1, tile_count, order, order), lambda s: (s, 0, 0, 0)),
            smem,
            smem,
            smem,
        ]
        + [anywhere] * len(earlier),
        out_specs=[vmem] * 2,
        scratch_shapes=[pltpu.VMEM((2 * half[0], count, order), f32)],
        compiler_params=params(vmem_bytes if moved else all_vmem),
        name="returned_moved" if moved else "returned",
    )(vectors, tiles, col, load, new_slot, *earlier)


def near_kernel(bulk_count, pieces, second, *refs):
    panel, refs = refs[:pieces], refs[pieces:]
    vectors, tiles, diag, col, load, new_slot, near, moving, packed, *more, rows_of, gram = refs
    row_count, count = vectors.shape[:2]
    me = lax.axis_index("bulk")
    mine = lax.axis_index("group")
    base = mine * bulk_count * row_count
    s = pl.program_id(0)
    slot = first_slot(row_count) + s
    half_rows = bulk_count * row_count // 2
    held = [piece.shape[0] // count for piece in panel]
    starts = [sum(held[:index]) for index in range(pieces)]

    def place_of(target):
        target = target - base
        owner = target // row_count
        rel = owner ^ me
        return (rel & 1) * half_rows + (rel >> 1) * row_count + target - owner * row_count

    @pl.when(s == 0)
    def _():
        for piece, first, rows in zip(panel, starts, held):
            for k in range(rows):
                rows_of[first + k] = split_rows(piece[k * count : (k + 1) * count])
        gram[...] = jnp.zeros_like(gram)

    left, right = [], []
    for t in range(tiles.shape[1]):
        rows = rows_of[place_of(col[t, slot])]
        rows = jnp.where(t < load[slot], rows, jnp.zeros_like(rows))
        high, low = split(tiles[0, t])
        left += [rows[:count], rows[count:], rows[:count]]
        right += [high, high, low]
    direct = dot16(jnp.concatenate(left, axis=1), jnp.concatenate(right, axis=1), right_t)
    value = vectors[s]
    near_value = times_tile(split_rows(value), diag[0], right_t)
    near[s] = near_value + direct
    if second:
        gram[...] += dot24(value, near_value + 2.0 * direct)
    else:
        gram[...] += dot24(value, value)

    arriving = new_slot[slot]
    incoming = place_of(arriving)
    for piece, first, rows in zip(panel, starts, held):

        @pl.when((incoming >= first) & (incoming < first + rows))
        def _(piece=piece, first=first):
            start = pl.multiple_of((incoming - first) * count, count)
            moving[s] = piece[pl.ds(start, count)]

    if not second:
        (flags,) = more

        @pl.when(arriving != slot)
        def _():
            route = owed_place(((arriving - base) // row_count) ^ me, bulk_count)
            steps = flags.shape[0] // 8
            for index in range(steps):
                bit = ((route >> (steps - 1 - index)) & 1).astype(f32)
                flags[8 * index : 8 * index + 8] = jnp.full((8, flags.shape[1]), bit, f32)

    @pl.when(s == row_count - 1)
    def _():
        packed[...] = pack(gram[...])


def near_part(panel, vectors, tiles, diag, col, load, new_slot, second):
    row_count, count, order = vectors.shape
    bulk_count = sum(piece.shape[0] for piece in panel) // (row_count * count)
    tile_count = tiles.shape[1]
    shapes = [vectors.shape, vectors.shape, (count // 2, order)]
    if not second:
        shapes += [(8 * (bulk_count.bit_length() - 1), order)]
    return pl.pallas_call(
        functools.partial(near_kernel, bulk_count, len(panel), second),
        grid=(row_count,),
        out_shape=[jax.ShapeDtypeStruct(shape, f32) for shape in shapes],
        in_specs=[vmem] * len(panel)
        + [
            vmem,
            pl.BlockSpec((1, tile_count, order, order), lambda s: (s, 0, 0, 0)),
            pl.BlockSpec((1, order, order), lambda s: (s, 0, 0)),
            smem,
            smem,
            smem,
        ],
        out_specs=[vmem] * len(shapes),
        scratch_shapes=[
            pltpu.VMEM((bulk_count * row_count, 2 * count, order), bf16),
            pltpu.VMEM((count, count), f32),
        ],
        compiler_params=params(),
        name="near_second" if second else "near_first",
    )(*panel, vectors, tiles, diag, col, load, new_slot)


def crossed(side, coupling, k):
    edge_rows, part_count = coupling.shape[:2]
    count = side.shape[1] // 2
    mine = lax.axis_index("group")
    total = None
    for h in range(part_count):
        start = (h * edge_rows + k) * count
        rows = split_rows(side[start : start + count])
        term = times_tile(rows, coupling[k, mine ^ h], right_t)
        total = term if total is None else total + term
    return total


def gather_first_kernel(vectors, near, keep, *refs):
    received = refs[:-5]
    coupling, old_side, packed, first, side = refs[-5:]
    row_count, count = vectors.shape[:2]
    half = count // 2
    edge_rows = (side.shape[0] - 2 * half - 8) // count
    grams = [None, None]
    for k in range(row_count):
        value = near[k] + keep[k]
        for ref in received:
            value = value + ref[k]
        if k < edge_rows:
            value = value + crossed(old_side, coupling, k)
        first[k] = value
        if k < edge_rows:
            side[k * count : (k + 1) * count] = value
        terms = (dot24(vectors[k], value), dot24(value, value))
        grams = [term if old is None else old + term for old, term in zip(grams, terms)]
    start = edge_rows * count
    joined, row = join_symmetric(unpack(packed[...]), grams[1])
    side[start : start + half] = pack(joined)
    side[start + half : start + 2 * half] = pack(sym(grams[0]))
    rows = jnp.concatenate([row, jnp.zeros_like(row)], axis=1)
    side[start + 2 * half :] = jnp.broadcast_to(rows, (8, 2 * count))


def gather_first(vectors, near, terms, coupling, old_side, packed):
    row_count, count, order = vectors.shape
    edge_rows = coupling.shape[0]
    shapes = [vectors.shape, (edge_rows * count + count + 8, order)]
    specs = [pl.BlockSpec((row_count, count, order), lambda s: (0, 0, 0))] * (2 + len(terms))
    return pl.pallas_call(
        gather_first_kernel,
        grid=(1,),
        out_shape=[jax.ShapeDtypeStruct(shape, f32) for shape in shapes],
        in_specs=specs + [vmem] * 3,
        out_specs=[vmem] * 2,
        compiler_params=params(),
        name="gather_first",
    )(vectors, near, *terms, coupling, old_side, packed)


def edge_second_kernel(first, near, packed, coupling, side, new_slot, more, extra):
    row_count, count = first.shape[:2]
    edge_rows, part_count = coupling.shape[:2]
    half = count // 2
    gram = unpack(packed[...])
    for k in range(edge_rows):
        value = crossed(side, coupling, k)
        gram = gram + dot24(first[k], value)
        more[k] = value
    start = part_count * edge_rows * count
    joined, row = join_symmetric(unpack(side[start + half : start + 2 * half]), sym(gram))
    extra[:count] = jnp.concatenate([unpack(side[start : start + half]), joined], axis=1)
    row = jnp.concatenate([jnp.zeros_like(row), row], axis=1)
    extra[count : count + 8] = side[start + 2 * half :] + jnp.broadcast_to(row, (8, 2 * count))
    slot = first_slot(row_count)
    for k in range(edge_rows, row_count):

        @pl.when(new_slot[slot + k] != slot + k)
        def _(k=k):
            extra[count + 8 :] = near[k]


def edge_second(first, near, packed, coupling, side, new_slot):
    count, order = first.shape[1:]
    shapes = [(coupling.shape[0], count, order), (2 * count + 8, order)]
    return pl.pallas_call(
        edge_second_kernel,
        out_shape=[jax.ShapeDtypeStruct(shape, f32) for shape in shapes],
        in_specs=[vmem] * 5 + [smem],
        out_specs=[vmem] * 2,
        compiler_params=params(),
        name="edge_second",
    )(first, near, packed, coupling, side, new_slot)


def spread_row(rows, index):
    return jnp.broadcast_to(rows[index : index + 1], rows.shape)


def inverse_factors(matrices):
    count = matrices[0].shape[0]
    step = 8
    shape = (step, 2 * count)
    eye = identity(count)
    sub = lax.broadcasted_iota(jnp.int32, shape, 0)
    work = []
    for matrix in matrices:
        both = jnp.concatenate([matrix, eye], axis=1)
        work.append([both[i : i + step] for i in range(0, count, step)])
    for block in range(count // step):
        start = block * step
        for w in work:
            cols = [
                [jnp.broadcast_to(rows[:, start + m : start + m + 1], shape) for m in range(step)]
                for rows in w[block:]
            ]
            factor = [[None] * step for _ in range(step)]
            scales, pivots = [], []
            for m in range(step):
                value = spread_row(cols[0][m], m)
                row = spread_row(w[block], m)
                for u in range(m):
                    value = value - factor[m][u] * factor[m][u]
                    row = row - factor[m][u] * pivots[u]
                scales.append(lax.rsqrt(value))
                pivots.append(row * scales[m])
                for v in range(m + 1, step):
                    value = spread_row(cols[0][m], v)
                    for u in range(m):
                        value = value - factor[v][u] * factor[m][u]
                    factor[v][m] = value * scales[m]
            for i in range(block + 1, count // step):
                left = []
                for m in range(step):
                    value = cols[i - block][m]
                    for u in range(m):
                        value = value - left[u] * factor[m][u]
                    left.append(value * scales[m])
                terms = [one * pivot for one, pivot in zip(left, pivots)]
                while len(terms) > 1:
                    terms = [x + y for x, y in zip(terms[::2], terms[1::2])]
                w[i] = w[i] - terms[0]
            rows = pivots[0]
            for m in range(1, step):
                rows = jnp.where(sub == m, pivots[m], rows)
            w[block] = rows
    return [jnp.concatenate(w, axis=0)[:, count:] for w in work]


def solve(inverse_factor, right):
    return dot32(inverse_factor, dot32(inverse_factor, right), left_t)


def grams_of(sums):
    count = sums.shape[1] // 2
    row = sums[count : count + 1]
    g0, g2 = part_symmetric(sums[:count, :count], row[:, :count])
    g1, g3 = part_symmetric(sums[:count, count:], row[:, count:])
    return g0, g1, g2, g3


def first_solves_kernel(extra, out):
    g0, g1, _, _ = grams_of(extra[...])
    factor_pq, factor_rr = inverse_factors([shift * g0 + g1, g0])
    out[0] = solve(factor_pq, g0)
    out[1] = dot32(factor_rr, factor_rr, left_t)


def next_gram_kernel(extra, solved, out):
    g0, g1, g2, _ = grams_of(extra[...])
    a, inverse_rr = solved[0], solved[1]
    count = a.shape[0]
    m = identity(count) - shift * a
    by_a = dot32(jnp.concatenate([g0, g1, g2], axis=0), a)
    g0a, g1a, g2a = (by_a[i * count : (i + 1) * count] for i in range(3))
    g0m, g1m = g0 - shift * g0a, g1 - shift * g1a
    left = jnp.concatenate([m, a], axis=0)
    g_new = sym(dot32(left, jnp.concatenate([g0m - g1a, g2a - g1m], axis=0), left_t))
    c = m + dot32(inverse_rr, g_new)
    by_c = dot32(jnp.concatenate([shift * g0 + g1, shift * g1 + g2], axis=0), c)
    left = jnp.concatenate([c, a], axis=0)
    upper = by_c[:count] - (shift * g1a + g2a)
    lower = shift * g2a - by_c[count:]
    out[0] = c
    out[1] = g_new
    out[2] = dot32(left, jnp.concatenate([upper, lower], axis=0), left_t)


def small_call(kernel, count, matrices, name, *operands):
    return pl.pallas_call(
        kernel,
        out_shape=jax.ShapeDtypeStruct((matrices, count, count), f32),
        in_specs=[vmem] * len(operands),
        out_specs=vmem,
        compiler_params=params(),
        name=name,
    )(*operands)


def final_kernel(gram, solved, following, moving, first, near, more, new_slot, row, *refs):
    last_row, flags, *terms, solution, resid = refs
    row_count, count = moving.shape[:2]
    arrived = jnp.where(flags[flags.shape[0] - 8 :][:1] > 0.5, last_row[0], row[...])
    a, c, g_new = solved[0], following[0], following[1]
    g3 = sym(unpack(gram[...]))
    g_pq = sym(following[2] + dot32(a, dot32(g3, a), left_t))
    (factor,) = inverse_factors([g_pq])
    a1 = solve(factor, g_new)
    by_a1 = dot32(jnp.concatenate([a, c], axis=0), a1)
    aa1, ca1 = by_a1[:count], by_a1[count:]
    m = identity(count) - shift * a
    top = jnp.concatenate([a + ca1, -aa1, jnp.zeros_like(a)], axis=0)
    low = jnp.concatenate([m - shift * ca1, shift * aa1 - a - ca1, aa1], axis=0)
    coef = jnp.concatenate([top, low], axis=1)
    slot = first_slot(row_count)
    basis = []
    for k in range(row_count):
        stays = new_slot[slot + k] == slot + k
        second = jnp.where(stays, near[k], arrived)
        if k < more.shape[0]:
            second = second + more[k]
        for ref in terms:
            second = second + ref[k]
        basis.append(jnp.concatenate([moving[k], first[k], second], axis=0))
    order = moving.shape[2]
    both = dot32(coef, jnp.concatenate(basis, axis=1), left_t)
    for k in range(row_count):
        solution[k] = both[:count, k * order : (k + 1) * order]
        resid[k] = both[count:, k * order : (k + 1) * order]


def final(gram, solved, following, moving, first, near, more, new_slot, row, flags, terms):
    block = pl.BlockSpec(near.shape, lambda s: (0, 0, 0))
    last = pl.BlockSpec((1,) + near.shape[1:], lambda s: (terms[-1].shape[0] - 1, 0, 0))
    return pl.pallas_call(
        final_kernel,
        grid=(1,),
        out_shape=[jax.ShapeDtypeStruct(near.shape, f32)] * 2,
        in_specs=[vmem] * 7 + [smem, vmem, last, vmem] + [block] * len(terms),
        out_specs=[vmem] * 2,
        compiler_params=params(),
        name="final",
    )(gram, solved, following, moving, first, near, more, new_slot, row, terms[-1], flags, *terms)


def add_kernel(count, *refs):
    total = refs[0][...]
    for ref in refs[1:count]:
        total = total + ref[...]
    refs[-1][...] = total


def add_upper(terms, rows, *earlier):
    shape = (rows,) + terms[0].shape[1:]
    block = pl.BlockSpec(shape, lambda s: (1, 0, 0))
    return pl.pallas_call(
        functools.partial(add_kernel, len(terms)),
        grid=(1,),
        out_shape=jax.ShapeDtypeStruct(shape, f32),
        in_specs=[block] * len(terms) + [anywhere] * len(earlier),
        out_specs=vmem,
        compiler_params=params(),
        name="add_upper",
    )(*terms, *earlier)


def add_with_row_kernel(step, count, row, other, flags, *refs):
    terms, out, held = refs[:count], refs[-2], refs[-1]
    total = terms[0][...]
    for ref in terms[1:]:
        total = total + ref[...]
    out[: total.shape[0]] = total
    value = row[...]
    if step > 1:
        value = jnp.where(flags[8 * step : 8 * step + 1] > 0.5, other[0], value)
    out[total.shape[0]] = value
    held[...] = value


def add_with_row(terms, rows, row, flags, step, *earlier):
    shape = (rows,) + terms[0].shape[1:]
    block = pl.BlockSpec(shape, lambda s: (1, 0, 0))
    last = pl.BlockSpec((1,) + shape[1:], lambda s: (terms[-1].shape[0] - 1, 0, 0))
    return pl.pallas_call(
        functools.partial(add_with_row_kernel, step, len(terms)),
        grid=(1,),
        out_shape=[
            jax.ShapeDtypeStruct((rows + 1,) + shape[1:], f32),
            jax.ShapeDtypeStruct(row.shape, f32),
        ],
        in_specs=[vmem, last, vmem] + [block] * len(terms) + [anywhere] * len(earlier),
        out_specs=[vmem] * 2,
        compiler_params=params(),
        name="add_with_row",
    )(row, terms[-1], flags, *terms, *earlier)


def settle_kernel(index, sums, extra, partner, flags, *refs):
    out = refs[-1]
    out[:sums] = extra[:sums] + partner[:sums]
    if extra.shape[0] > sums:
        chosen = flags[8 * index : 8 * index + 1] > 0.5
        out[sums:] = jnp.where(chosen, partner[sums:], extra[sums:])


def settle(extra, partner, flags, index, sums, *earlier):
    return pl.pallas_call(
        functools.partial(settle_kernel, index, sums),
        out_shape=jax.ShapeDtypeStruct(extra.shape, f32),
        in_specs=[vmem] * 3 + [anywhere] * len(earlier),
        out_specs=vmem,
        compiler_params=params(),
        name="settle",
    )(extra, partner, flags, *earlier)


def leave_row_kernel(sums, extra, partner, flags, out, row):
    out[...] = extra[:sums] + partner[:sums]
    row[...] = jnp.where(flags[8:9] > 0.5, partner[sums:], extra[sums:])


def leave_row(extra, partner, flags, sums):
    order = extra.shape[1]
    return pl.pallas_call(
        functools.partial(leave_row_kernel, sums),
        out_shape=[
            jax.ShapeDtypeStruct((sums, order), f32),
            jax.ShapeDtypeStruct((extra.shape[0] - sums, order), f32),
        ],
        in_specs=[vmem] * 3,
        out_specs=[vmem] * 2,
        compiler_params=params(),
        name="leave_row",
    )(extra, partner, flags)


def last_gram_kernel(sums, partner, out, gram):
    total = sums[...] + partner[...]
    out[...] = total
    gram[...] = pack(grams_of(total)[3])


def last_gram(sums, partner):
    rows, order = sums.shape
    return pl.pallas_call(
        last_gram_kernel,
        out_shape=[
            jax.ShapeDtypeStruct((rows, order), f32),
            jax.ShapeDtypeStruct((order // 4, order), f32),
        ],
        in_specs=[vmem] * 2,
        out_specs=[vmem] * 2,
        compiler_params=params(),
        name="last_gram",
    )(sums, partner)


def add_whole(left, right, *earlier):
    return pl.pallas_call(
        functools.partial(add_kernel, 2),
        out_shape=jax.ShapeDtypeStruct(left.shape, f32),
        in_specs=[vmem] * 2 + [anywhere] * len(earlier),
        out_specs=vmem,
        compiler_params=params(),
        name="add_whole",
    )(left, right, *earlier)


def pass_on(value, *earlier):
    return pl.pallas_call(
        functools.partial(add_kernel, 1),
        out_shape=jax.ShapeDtypeStruct(value.shape, f32),
        in_specs=[vmem] + [anywhere] * len(earlier),
        out_specs=vmem,
        compiler_params=params(),
        name="pass_on",
    )(value, *earlier)


def join_kernel(count, *refs):
    out = refs[-1]
    rows = refs[0].shape[0]
    for index, ref in enumerate(refs[:count]):
        out[index * rows : (index + 1) * rows] = ref[...]


def join(pieces, *earlier):
    rows, order = pieces[0].shape
    return pl.pallas_call(
        functools.partial(join_kernel, len(pieces)),
        out_shape=jax.ShapeDtypeStruct((len(pieces) * rows, order), f32),
        in_specs=[vmem] * len(pieces) + [anywhere] * len(earlier),
        out_specs=vmem,
        compiler_params=params(),
        name="join",
    )(*pieces, *earlier)


def merge_kernel(edge, mine, other, *refs):
    out = refs[-1]
    out[:edge] = mine[:edge]
    out[edge : 2 * edge] = other[:edge]
    if mine.shape[0] > edge:
        out[2 * edge :] = mine[edge:] + other[edge:]


def merge_side(side, other, edge, *earlier):
    return pl.pallas_call(
        functools.partial(merge_kernel, edge),
        out_shape=jax.ShapeDtypeStruct((side.shape[0] + edge, side.shape[1]), f32),
        in_specs=[vmem] * 2 + [anywhere] * len(earlier),
        out_specs=vmem,
        compiler_params=params(),
        name="merge_side",
    )(side, other, *earlier)


def share_side(side, edge, part_count):
    mask = 1
    while 2 * mask < part_count:
        side = merge_side(side, swap(side, "group", mask), mask * edge)
        mask *= 2
    return side, swap(side, "group", mask)


def share_panel(piece, bulk_count, pieces, *earlier):
    own = [piece] + [swap(piece, "bulk", rel) for rel in range(2, bulk_count, 2)]
    size = len(own) // pieces
    joined = [join(own[i * size : (i + 1) * size]) for i in range(pieces - 1)]
    joined.append(join(own[(pieces - 1) * size :], *earlier))
    return own + [swap(one, "bulk", 1) for one in joined], joined[-1]


def local(rhs, diag_tiles, offdiag_blocks, coupling, col_index, load, new_slot):
    row_count, count, order = rhs.shape
    edge_rows, part_count = coupling.shape[:2]
    bulk_count = lax.axis_size("bulk")
    steps = bulk_count.bit_length() - 1
    masks = far_masks(bulk_count)[::-1]
    edge = edge_rows * count
    half_edges = part_count // 2 * edge
    indices = (col_index.T, load, new_slot)

    flat = rhs.reshape(row_count * count, order)
    side, other_side = share_side(flat[:edge], edge, part_count)
    keep, send = returned(rhs, offdiag_blocks, *indices, bulk_count, False)
    panel, joined = share_panel(flat, bulk_count, 2, side)
    terms = [keep, swap(send, "bulk", 1)]
    rows = bulk_count // 2 * row_count
    for step, mask in enumerate(masks):
        rows //= 2
        total = add_upper(terms, rows, *([joined] if step else []))
        terms.append(swap(total, "bulk", mask))
    near, moving, packed, flags = near_part(
        panel, rhs, offdiag_blocks, diag_tiles, *indices, False
    )
    side = merge_side(side, other_side, half_edges, near)
    first, side = gather_first(rhs, near, terms, coupling, side, packed)

    side, other_side = share_side(side, edge, part_count)
    keep, send = returned(first, offdiag_blocks, *indices, bulk_count, True)
    panel, joined = share_panel(
        first.reshape(row_count * count, order), bulk_count, 1, side, keep
    )
    terms = [keep, swap(pass_on(send, joined), "bulk", 1)]
    rows = bulk_count // 4 * row_count
    terms.append(swap(add_upper(terms, rows), "bulk", masks[0]))
    near, moved, packed = near_part(panel, first, offdiag_blocks, diag_tiles, *indices, True)
    side = merge_side(side, other_side, half_edges, near)
    more, extra = edge_second(first, near, packed, coupling, side, new_slot)

    sums = count + 8
    extra = settle(extra, swap(extra, "bulk", 1), flags, 0, sums, terms[-1])
    extra, row = leave_row(extra, swap(extra, "bulk", masks[0]), flags, sums)
    mask = 4
    while 2 * mask < bulk_count:
        extra = settle(extra, swap(extra, "bulk", mask), flags, 0, sums)
        mask *= 2
    extra, gram = last_gram(extra, swap(extra, "bulk", mask))
    for step in range(1, steps - 1):
        rows //= 2
        total, row = add_with_row(terms, rows, row, flags, step, extra)
        terms.append(swap(total, "bulk", masks[step]))
    solved = small_call(first_solves_kernel, count, 2, "first_solves", extra)
    following = small_call(next_gram_kernel, count, 3, "next_gram", extra, solved)
    mask = 1
    while mask < part_count:
        partner = swap(gram, "group", mask)
        gram = add_whole(gram, partner, *([solved] if mask == 1 else []))
        mask *= 2
    return tuple(
        final(gram, solved, following, moving, moved, near, more, new_slot, row, flags, terms)
    )


def solution(mesh):
    rows = P(("group", "bulk"))
    return jax.shard_map(
        local,
        mesh=mesh,
        in_specs=(rows, rows, rows, rows, P(), P(), P()),
        out_specs=(rows, rows),
        check_vma=False,
    )
```

```python
import functools

import jax
import jax.numpy as jnp
from jax import lax
from jax.experimental import pallas as pl
from jax.experimental.pallas import tpu as pltpu
from jax.sharding import PartitionSpec as P

shift = 4.0
f32 = jnp.float32
bf16 = jnp.bfloat16
normal = (((1,), (0,)), ((), ()))
right_t = (((1,), (1,)), ((), ()))
left_t = (((0,), (0,)), ((), ()))
vmem = pl.BlockSpec(memory_space=pltpu.VMEM)
smem = pl.BlockSpec(memory_space=pltpu.SMEM)
anywhere = pl.BlockSpec(memory_space=pl.ANY)
vmem_bytes = 40 * 2**20
all_vmem = 56 * 2**20


def params(limit=vmem_bytes):
    return pltpu.CompilerParams(vmem_limit_bytes=limit)


def swap(value, axis, mask):
    pairs = [(source, source ^ mask) for source in range(lax.axis_size(axis))]
    return lax.ppermute(value, axis, pairs)


def split(value):
    high = value.astype(bf16)
    return high, (value - high.astype(f32)).astype(bf16)


def dot16(left, right, dims):
    return lax.dot_general(left, right, dims, preferred_element_type=f32)


def dot32(left, right, dims=normal):
    return lax.dot_general(
        left, right, dims, preferred_element_type=f32, precision=lax.Precision.HIGHEST
    )


def split_rows(vectors):
    high, low = split(vectors)
    return jnp.concatenate([high, low], axis=0)


def times_tile(rows, tile, dims):
    count = rows.shape[0] // 2
    high, low = split(tile)
    left = jnp.concatenate([rows[:count], rows[count:], rows[:count]], axis=1)
    return dot16(left, jnp.concatenate([high, high, low], axis=dims[0][1][0]), dims)


def dot24(left, right):
    high, low = split(left)
    other_high, other_low = split(right)
    left = jnp.concatenate([high, low, high], axis=1)
    return dot16(left, jnp.concatenate([other_high, other_high, other_low], axis=1), right_t)


def pack(gram):
    half = gram.shape[0] // 2
    return jnp.concatenate([gram[:half], gram[half:]], axis=1)


def unpack(packed):
    half = packed.shape[1] // 2
    return jnp.concatenate([packed[:, :half], packed[:, half:]], axis=0)


def above(count):
    rows = lax.broadcasted_iota(jnp.int32, (count, count), 0)
    cols = lax.broadcasted_iota(jnp.int32, (count, count), 1)
    return cols > rows, cols == rows


def identity(count):
    return above(count)[1].astype(f32)


def join_symmetric(upper, lower):
    over, diagonal = above(upper.shape[0])
    row = jnp.sum(jnp.where(diagonal, upper, 0.0), axis=0, keepdims=True)
    return jnp.where(over, upper, lower), row


def part_symmetric(joined, row):
    over, diagonal = above(joined.shape[0])
    turned = joined.T
    upper = jnp.where(diagonal, row, jnp.where(over, joined, turned))
    return upper, jnp.where(over, turned, joined)


def sym(gram):
    return 0.5 * (gram + gram.T)


def first_slot(row_count):
    device = lax.axis_index("group") * lax.axis_size("bulk") + lax.axis_index("bulk")
    return device * row_count


def live(load_ref, slot, tile):
    return jnp.where(tile < load_ref[slot], 1.0, 0.0)


def far_masks(bulk_count):
    masks = []
    bit = bulk_count // 2
    while bit >= 4:
        masks += [bit | bit // 2, bit // 2]
        bit //= 4
    return masks + ([bit] if bit == 2 else [])


def owed_place(rel, bulk_count):
    place = 0
    index = 0
    bit = bulk_count.bit_length() - 2
    while bit >= 2:
        high = (rel >> bit) & 1
        low = (rel >> (bit - 1)) & 1
        place = place | (high << index) | ((high ^ low) << (index + 1))
        index += 2
        bit -= 2
    if bit == 1:
        place = place | (((rel >> 1) & 1) << index)
        index += 1
    return place | ((rel & 1) << index)


def returned_kernel(bulk_count, moved, vectors, tiles, col, load, new_slot, *refs):
    keep, send, total = refs[-3:]
    row_count = vectors.shape[0]
    me = lax.axis_index("bulk")
    base = lax.axis_index("group") * bulk_count * row_count
    s = pl.program_id(0)
    slot = first_slot(row_count) + s

    @pl.when(s == 0)
    def _():
        total[...] = jnp.zeros_like(total)

    rows = split_rows(vectors[s])
    for t in range(tiles.shape[1]):
        product = times_tile(rows, tiles[0, t], normal)
        target = col[t, slot]
        if moved:
            target = new_slot[target]
        target = target - base
        owner = target // row_count
        place = owed_place(owner ^ me, bulk_count) * row_count + target - owner * row_count
        total[place] += live(load, slot, t) * product

    @pl.when(s == row_count - 1)
    def _():
        half = total.shape[0] // 2
        keep[...] = total[:half]
        send[...] = total[half:]


def returned(vectors, tiles, col, load, new_slot, bulk_count, moved, *earlier):
    row_count, count, order = vectors.shape
    tile_count = tiles.shape[1]
    half = (bulk_count * row_count // 2, count, order)
    return pl.pallas_call(
        functools.partial(returned_kernel, bulk_count, moved),
        grid=(row_count,),
        out_shape=[jax.ShapeDtypeStruct(half, f32) if moved else pltpu.VMEM(half, f32)] * 2,
        in_specs=[
            vmem,
            pl.BlockSpec((1, tile_count, order, order), lambda s: (s, 0, 0, 0)),
            smem,
            smem,
            smem,
        ]
        + [anywhere] * len(earlier),
        out_specs=[vmem] * 2,
        scratch_shapes=[pltpu.VMEM((2 * half[0], count, order), f32)],
        compiler_params=params(vmem_bytes if moved else all_vmem),
        name="returned_moved" if moved else "returned",
    )(vectors, tiles, col, load, new_slot, *earlier)


def near_kernel(bulk_count, pieces, second, *refs):
    panel, refs = refs[:pieces], refs[pieces:]
    vectors, tiles, diag, col, load, new_slot, near, moving, packed, *more, rows_of, gram = refs
    row_count, count = vectors.shape[:2]
    me = lax.axis_index("bulk")
    mine = lax.axis_index("group")
    base = mine * bulk_count * row_count
    s = pl.program_id(0)
    slot = first_slot(row_count) + s
    half_rows = bulk_count * row_count // 2
    held = [piece.shape[0] // count for piece in panel]
    starts = [sum(held[:index]) for index in range(pieces)]

    def place_of(target):
        target = target - base
        owner = target // row_count
        rel = owner ^ me
        return (rel & 1) * half_rows + (rel >> 1) * row_count + target - owner * row_count

    @pl.when(s == 0)
    def _():
        for piece, first, rows in zip(panel, starts, held):
            for k in range(rows):
                rows_of[first + k] = split_rows(piece[k * count : (k + 1) * count])
        gram[...] = jnp.zeros_like(gram)

    left, right = [], []
    for t in range(tiles.shape[1]):
        rows = rows_of[place_of(col[t, slot])]
        rows = jnp.where(t < load[slot], rows, jnp.zeros_like(rows))
        high, low = split(tiles[0, t])
        left += [rows[:count], rows[count:], rows[:count]]
        right += [high, high, low]
    direct = dot16(jnp.concatenate(left, axis=1), jnp.concatenate(right, axis=1), right_t)
    value = vectors[s]
    near_value = times_tile(split_rows(value), diag[0], right_t)
    near[s] = near_value + direct
    if second:
        gram[...] += dot24(value, near_value + 2.0 * direct)
    else:
        gram[...] += dot24(value, value)

    arriving = new_slot[slot]
    incoming = place_of(arriving)
    for piece, first, rows in zip(panel, starts, held):

        @pl.when((incoming >= first) & (incoming < first + rows))
        def _(piece=piece, first=first):
            start = pl.multiple_of((incoming - first) * count, count)
            moving[s] = piece[pl.ds(start, count)]

    if not second:
        (flags,) = more

        @pl.when(arriving != slot)
        def _():
            route = owed_place(((arriving - base) // row_count) ^ me, bulk_count)
            steps = flags.shape[0] // 8
            for index in range(steps):
                bit = ((route >> (steps - 1 - index)) & 1).astype(f32)
                flags[8 * index : 8 * index + 8] = jnp.full((8, flags.shape[1]), bit, f32)

    @pl.when(s == row_count - 1)
    def _():
        packed[...] = pack(gram[...])


def near_part(panel, vectors, tiles, diag, col, load, new_slot, second):
    row_count, count, order = vectors.shape
    bulk_count = sum(piece.shape[0] for piece in panel) // (row_count * count)
    tile_count = tiles.shape[1]
    shapes = [vectors.shape, vectors.shape, (count // 2, order)]
    if not second:
        shapes += [(8 * (bulk_count.bit_length() - 1), order)]
    return pl.pallas_call(
        functools.partial(near_kernel, bulk_count, len(panel), second),
        grid=(row_count,),
        out_shape=[jax.ShapeDtypeStruct(shape, f32) for shape in shapes],
        in_specs=[vmem] * len(panel)
        + [
            vmem,
            pl.BlockSpec((1, tile_count, order, order), lambda s: (s, 0, 0, 0)),
            pl.BlockSpec((1, order, order), lambda s: (s, 0, 0)),
            smem,
            smem,
            smem,
        ],
        out_specs=[vmem] * len(shapes),
        scratch_shapes=[
            pltpu.VMEM((bulk_count * row_count, 2 * count, order), bf16),
            pltpu.VMEM((count, count), f32),
        ],
        compiler_params=params(),
        name="near_second" if second else "near_first",
    )(*panel, vectors, tiles, diag, col, load, new_slot)


def crossed(side, coupling, k):
    edge_rows, part_count = coupling.shape[:2]
    count = side.shape[1] // 2
    mine = lax.axis_index("group")
    total = None
    for h in range(part_count):
        start = (h * edge_rows + k) * count
        rows = split_rows(side[start : start + count])
        term = times_tile(rows, coupling[k, mine ^ h], right_t)
        total = term if total is None else total + term
    return total


def gather_first_kernel(vectors, near, keep, *refs):
    received = refs[:-5]
    coupling, old_side, packed, first, side = refs[-5:]
    row_count, count = vectors.shape[:2]
    half = count // 2
    edge_rows = (side.shape[0] - 2 * half - 8) // count
    grams = [None, None]
    for k in range(row_count):
        value = near[k] + keep[k]
        for ref in received:
            value = value + ref[k]
        if k < edge_rows:
            value = value + crossed(old_side, coupling, k)
        first[k] = value
        if k < edge_rows:
            side[k * count : (k + 1) * count] = value
        terms = (dot24(vectors[k], value), dot24(value, value))
        grams = [term if old is None else old + term for old, term in zip(grams, terms)]
    start = edge_rows * count
    joined, row = join_symmetric(unpack(packed[...]), grams[1])
    side[start : start + half] = pack(joined)
    side[start + half : start + 2 * half] = pack(sym(grams[0]))
    rows = jnp.concatenate([row, jnp.zeros_like(row)], axis=1)
    side[start + 2 * half :] = jnp.broadcast_to(rows, (8, 2 * count))


def gather_first(vectors, near, terms, coupling, old_side, packed):
    row_count, count, order = vectors.shape
    edge_rows = coupling.shape[0]
    shapes = [vectors.shape, (edge_rows * count + count + 8, order)]
    specs = [pl.BlockSpec((row_count, count, order), lambda s: (0, 0, 0))] * (2 + len(terms))
    return pl.pallas_call(
        gather_first_kernel,
        grid=(1,),
        out_shape=[jax.ShapeDtypeStruct(shape, f32) for shape in shapes],
        in_specs=specs + [vmem] * 3,
        out_specs=[vmem] * 2,
        compiler_params=params(),
        name="gather_first",
    )(vectors, near, *terms, coupling, old_side, packed)


def edge_second_kernel(first, near, packed, coupling, side, new_slot, more, extra):
    row_count, count = first.shape[:2]
    edge_rows, part_count = coupling.shape[:2]
    half = count // 2
    gram = unpack(packed[...])
    for k in range(edge_rows):
        value = crossed(side, coupling, k)
        gram = gram + dot24(first[k], value)
        more[k] = value
    start = part_count * edge_rows * count
    joined, row = join_symmetric(unpack(side[start + half : start + 2 * half]), sym(gram))
    extra[:count] = jnp.concatenate([unpack(side[start : start + half]), joined], axis=1)
    row = jnp.concatenate([jnp.zeros_like(row), row], axis=1)
    extra[count : count + 8] = side[start + 2 * half :] + jnp.broadcast_to(row, (8, 2 * count))
    slot = first_slot(row_count)
    for k in range(edge_rows, row_count):

        @pl.when(new_slot[slot + k] != slot + k)
        def _(k=k):
            extra[count + 8 :] = near[k]


def edge_second(first, near, packed, coupling, side, new_slot):
    count, order = first.shape[1:]
    shapes = [(coupling.shape[0], count, order), (2 * count + 8, order)]
    return pl.pallas_call(
        edge_second_kernel,
        out_shape=[jax.ShapeDtypeStruct(shape, f32) for shape in shapes],
        in_specs=[vmem] * 5 + [smem],
        out_specs=[vmem] * 2,
        compiler_params=params(),
        name="edge_second",
    )(first, near, packed, coupling, side, new_slot)


def spread_row(rows, index):
    return jnp.broadcast_to(rows[index : index + 1], rows.shape)


def inverse_factors(matrices):
    count = matrices[0].shape[0]
    step = 8
    shape = (step, 2 * count)
    eye = identity(count)
    sub = lax.broadcasted_iota(jnp.int32, shape, 0)
    work = []
    for matrix in matrices:
        both = jnp.concatenate([matrix, eye], axis=1)
        work.append([both[i : i + step] for i in range(0, count, step)])
    for block in range(count // step):
        start = block * step
        for w in work:
            cols = [
                [jnp.broadcast_to(rows[:, start + m : start + m + 1], shape) for m in range(step)]
                for rows in w[block:]
            ]
            factor = [[None] * step for _ in range(step)]
            scales, pivots = [], []
            for m in range(step):
                value = spread_row(cols[0][m], m)
                row = spread_row(w[block], m)
                for u in range(m):
                    value = value - factor[m][u] * factor[m][u]
                    row = row - factor[m][u] * pivots[u]
                scales.append(lax.rsqrt(value))
                pivots.append(row * scales[m])
                for v in range(m + 1, step):
                    value = spread_row(cols[0][m], v)
                    for u in range(m):
                        value = value - factor[v][u] * factor[m][u]
                    factor[v][m] = value * scales[m]
            for i in range(block + 1, count // step):
                left = []
                for m in range(step):
                    value = cols[i - block][m]
                    for u in range(m):
                        value = value - left[u] * factor[m][u]
                    left.append(value * scales[m])
                terms = [one * pivot for one, pivot in zip(left, pivots)]
                while len(terms) > 1:
                    terms = [x + y for x, y in zip(terms[::2], terms[1::2])]
                w[i] = w[i] - terms[0]
            rows = pivots[0]
            for m in range(1, step):
                rows = jnp.where(sub == m, pivots[m], rows)
            w[block] = rows
    return [jnp.concatenate(w, axis=0)[:, count:] for w in work]


def solve(inverse_factor, right):
    return dot32(inverse_factor, dot32(inverse_factor, right), left_t)


def grams_of(sums):
    count = sums.shape[1] // 2
    row = sums[count : count + 1]
    g0, g2 = part_symmetric(sums[:count, :count], row[:, :count])
    g1, g3 = part_symmetric(sums[:count, count:], row[:, count:])
    return g0, g1, g2, g3


def first_solves_kernel(extra, out):
    g0, g1, _, _ = grams_of(extra[...])
    factor_pq, factor_rr = inverse_factors([shift * g0 + g1, g0])
    out[0] = solve(factor_pq, g0)
    out[1] = dot32(factor_rr, factor_rr, left_t)


def next_gram_kernel(extra, solved, out):
    g0, g1, g2, _ = grams_of(extra[...])
    a, inverse_rr = solved[0], solved[1]
    count = a.shape[0]
    m = identity(count) - shift * a
    by_a = dot32(jnp.concatenate([g0, g1, g2], axis=0), a)
    g0a, g1a, g2a = (by_a[i * count : (i + 1) * count] for i in range(3))
    g0m, g1m = g0 - shift * g0a, g1 - shift * g1a
    left = jnp.concatenate([m, a], axis=0)
    g_new = sym(dot32(left, jnp.concatenate([g0m - g1a, g2a - g1m], axis=0), left_t))
    c = m + dot32(inverse_rr, g_new)
    by_c = dot32(jnp.concatenate([shift * g0 + g1, shift * g1 + g2], axis=0), c)
    left = jnp.concatenate([c, a], axis=0)
    upper = by_c[:count] - (shift * g1a + g2a)
    lower = shift * g2a - by_c[count:]
    out[0] = c
    out[1] = g_new
    out[2] = dot32(left, jnp.concatenate([upper, lower], axis=0), left_t)


def small_call(kernel, count, matrices, name, *operands):
    return pl.pallas_call(
        kernel,
        out_shape=jax.ShapeDtypeStruct((matrices, count, count), f32),
        in_specs=[vmem] * len(operands),
        out_specs=vmem,
        compiler_params=params(),
        name=name,
    )(*operands)


def final_kernel(gram, solved, following, moving, first, near, more, new_slot, row, *refs):
    last_row, flags, *terms, solution, resid = refs
    row_count, count = moving.shape[:2]
    arrived = jnp.where(flags[flags.shape[0] - 8 :][:1] > 0.5, last_row[0], row[...])
    a, c, g_new = solved[0], following[0], following[1]
    g3 = sym(unpack(gram[...]))
    g_pq = sym(following[2] + dot32(a, dot32(g3, a), left_t))
    (factor,) = inverse_factors([g_pq])
    a1 = solve(factor, g_new)
    by_a1 = dot32(jnp.concatenate([a, c], axis=0), a1)
    aa1, ca1 = by_a1[:count], by_a1[count:]
    m = identity(count) - shift * a
    top = jnp.concatenate([a + ca1, -aa1, jnp.zeros_like(a)], axis=0)
    low = jnp.concatenate([m - shift * ca1, shift * aa1 - a - ca1, aa1], axis=0)
    coef = jnp.concatenate([top, low], axis=1)
    slot = first_slot(row_count)
    basis = []
    for k in range(row_count):
        stays = new_slot[slot + k] == slot + k
        second = jnp.where(stays, near[k], arrived)
        if k < more.shape[0]:
            second = second + more[k]
        for ref in terms:
            second = second + ref[k]
        basis.append(jnp.concatenate([moving[k], first[k], second], axis=0))
    order = moving.shape[2]
    both = dot32(coef, jnp.concatenate(basis, axis=1), left_t)
    for k in range(row_count):
        solution[k] = both[:count, k * order : (k + 1) * order]
        resid[k] = both[count:, k * order : (k + 1) * order]


def final(gram, solved, following, moving, first, near, more, new_slot, row, flags, terms):
    block = pl.BlockSpec(near.shape, lambda s: (0, 0, 0))
    last = pl.BlockSpec((1,) + near.shape[1:], lambda s: (terms[-1].shape[0] - 1, 0, 0))
    return pl.pallas_call(
        final_kernel,
        grid=(1,),
        out_shape=[jax.ShapeDtypeStruct(near.shape, f32)] * 2,
        in_specs=[vmem] * 7 + [smem, vmem, last, vmem] + [block] * len(terms),
        out_specs=[vmem] * 2,
        compiler_params=params(),
        name="final",
    )(gram, solved, following, moving, first, near, more, new_slot, row, terms[-1], flags, *terms)


def add_kernel(count, *refs):
    total = refs[0][...]
    for ref in refs[1:count]:
        total = total + ref[...]
    refs[-1][...] = total


def add_upper(terms, rows, *earlier):
    shape = (rows,) + terms[0].shape[1:]
    block = pl.BlockSpec(shape, lambda s: (1, 0, 0))
    return pl.pallas_call(
        functools.partial(add_kernel, len(terms)),
        grid=(1,),
        out_shape=jax.ShapeDtypeStruct(shape, f32),
        in_specs=[block] * len(terms) + [anywhere] * len(earlier),
        out_specs=vmem,
        compiler_params=params(),
        name="add_upper",
    )(*terms, *earlier)


def add_with_row_kernel(step, count, row, other, flags, *refs):
    terms, out, held = refs[:count], refs[-2], refs[-1]
    total = terms[0][...]
    for ref in terms[1:]:
        total = total + ref[...]
    out[: total.shape[0]] = total
    value = row[...]
    if step > 1:
        value = jnp.where(flags[8 * step : 8 * step + 1] > 0.5, other[0], value)
    out[total.shape[0]] = value
    held[...] = value


def add_with_row(terms, rows, row, flags, step, *earlier):
    shape = (rows,) + terms[0].shape[1:]
    block = pl.BlockSpec(shape, lambda s: (1, 0, 0))
    last = pl.BlockSpec((1,) + shape[1:], lambda s: (terms[-1].shape[0] - 1, 0, 0))
    return pl.pallas_call(
        functools.partial(add_with_row_kernel, step, len(terms)),
        grid=(1,),
        out_shape=[
            jax.ShapeDtypeStruct((rows + 1,) + shape[1:], f32),
            jax.ShapeDtypeStruct(row.shape, f32),
        ],
        in_specs=[vmem, last, vmem] + [block] * len(terms) + [anywhere] * len(earlier),
        out_specs=[vmem] * 2,
        compiler_params=params(),
        name="add_with_row",
    )(row, terms[-1], flags, *terms, *earlier)


def settle_kernel(index, sums, extra, partner, flags, *refs):
    out = refs[-1]
    out[:sums] = extra[:sums] + partner[:sums]
    if extra.shape[0] > sums:
        chosen = flags[8 * index : 8 * index + 1] > 0.5
        out[sums:] = jnp.where(chosen, partner[sums:], extra[sums:])


def settle(extra, partner, flags, index, sums, *earlier):
    return pl.pallas_call(
        functools.partial(settle_kernel, index, sums),
        out_shape=jax.ShapeDtypeStruct(extra.shape, f32),
        in_specs=[vmem] * 3 + [anywhere] * len(earlier),
        out_specs=vmem,
        compiler_params=params(),
        name="settle",
    )(extra, partner, flags, *earlier)


def leave_row_kernel(sums, extra, partner, flags, out, row):
    out[...] = extra[:sums] + partner[:sums]
    row[...] = jnp.where(flags[8:9] > 0.5, partner[sums:], extra[sums:])


def leave_row(extra, partner, flags, sums):
    order = extra.shape[1]
    return pl.pallas_call(
        functools.partial(leave_row_kernel, sums),
        out_shape=[
            jax.ShapeDtypeStruct((sums, order), f32),
            jax.ShapeDtypeStruct((extra.shape[0] - sums, order), f32),
        ],
        in_specs=[vmem] * 3,
        out_specs=[vmem] * 2,
        compiler_params=params(),
        name="leave_row",
    )(extra, partner, flags)


def last_gram_kernel(sums, partner, out, gram):
    total = sums[...] + partner[...]
    out[...] = total
    gram[...] = pack(grams_of(total)[3])


def last_gram(sums, partner):
    rows, order = sums.shape
    return pl.pallas_call(
        last_gram_kernel,
        out_shape=[
            jax.ShapeDtypeStruct((rows, order), f32),
            jax.ShapeDtypeStruct((order // 4, order), f32),
        ],
        in_specs=[vmem] * 2,
        out_specs=[vmem] * 2,
        compiler_params=params(),
        name="last_gram",
    )(sums, partner)


def add_whole(*terms):
    return pl.pallas_call(
        functools.partial(add_kernel, len(terms)),
        out_shape=jax.ShapeDtypeStruct(terms[0].shape, f32),
        in_specs=[vmem] * len(terms),
        out_specs=vmem,
        compiler_params=params(),
        name="add_whole",
    )(*terms)


def pass_on(value, *earlier):
    return pl.pallas_call(
        functools.partial(add_kernel, 1),
        out_shape=jax.ShapeDtypeStruct(value.shape, f32),
        in_specs=[vmem] + [anywhere] * len(earlier),
        out_specs=vmem,
        compiler_params=params(),
        name="pass_on",
    )(value, *earlier)


def join_kernel(count, *refs):
    out = refs[-1]
    rows = refs[0].shape[0]
    for index, ref in enumerate(refs[:count]):
        out[index * rows : (index + 1) * rows] = ref[...]


def join(pieces, *earlier):
    rows, order = pieces[0].shape
    return pl.pallas_call(
        functools.partial(join_kernel, len(pieces)),
        out_shape=jax.ShapeDtypeStruct((len(pieces) * rows, order), f32),
        in_specs=[vmem] * len(pieces) + [anywhere] * len(earlier),
        out_specs=vmem,
        compiler_params=params(),
        name="join",
    )(*pieces, *earlier)


def merge_kernel(edge, mine, other, *refs):
    out = refs[-1]
    out[:edge] = mine[:edge]
    out[edge : 2 * edge] = other[:edge]
    if mine.shape[0] > edge:
        out[2 * edge :] = mine[edge:] + other[edge:]


def merge_side(side, other, edge, *earlier):
    return pl.pallas_call(
        functools.partial(merge_kernel, edge),
        out_shape=jax.ShapeDtypeStruct((side.shape[0] + edge, side.shape[1]), f32),
        in_specs=[vmem] * 2 + [anywhere] * len(earlier),
        out_specs=vmem,
        compiler_params=params(),
        name="merge_side",
    )(side, other, *earlier)


def share_side(side, edge, part_count):
    mask = 1
    while 2 * mask < part_count:
        side = merge_side(side, swap(side, "group", mask), mask * edge)
        mask *= 2
    return side, swap(side, "group", mask)


def share_panel(piece, bulk_count, pieces, *earlier):
    own = [piece] + [swap(piece, "bulk", rel) for rel in range(2, bulk_count, 2)]
    size = len(own) // pieces
    joined = [join(own[i * size : (i + 1) * size]) for i in range(pieces - 1)]
    joined.append(join(own[(pieces - 1) * size :], *earlier))
    return own + [swap(one, "bulk", 1) for one in joined], joined[-1]


def local(rhs, diag_tiles, offdiag_blocks, coupling, col_index, load, new_slot):
    row_count, count, order = rhs.shape
    edge_rows, part_count = coupling.shape[:2]
    bulk_count = lax.axis_size("bulk")
    steps = bulk_count.bit_length() - 1
    masks = far_masks(bulk_count)[::-1]
    edge = edge_rows * count
    half_edges = part_count // 2 * edge
    indices = (col_index.T, load, new_slot)

    flat = rhs.reshape(row_count * count, order)
    side, other_side = share_side(flat[:edge], edge, part_count)
    keep, send = returned(rhs, offdiag_blocks, *indices, bulk_count, False)
    panel, joined = share_panel(flat, bulk_count, 2, side)
    terms = [keep, swap(send, "bulk", 1)]
    rows = bulk_count // 2 * row_count
    for step, mask in enumerate(masks):
        rows //= 2
        total = add_upper(terms, rows, *([joined] if step else []))
        terms.append(swap(total, "bulk", mask))
    near, moving, packed, flags = near_part(
        panel, rhs, offdiag_blocks, diag_tiles, *indices, False
    )
    side = merge_side(side, other_side, half_edges, near)
    first, side = gather_first(rhs, near, terms, coupling, side, packed)

    side, other_side = share_side(side, edge, part_count)
    keep, send = returned(first, offdiag_blocks, *indices, bulk_count, True)
    panel, joined = share_panel(
        first.reshape(row_count * count, order), bulk_count, 1, side, keep
    )
    terms = [keep, swap(pass_on(send, joined), "bulk", 1)]
    rows = bulk_count // 4 * row_count
    terms.append(swap(add_upper(terms, rows), "bulk", masks[0]))
    near, moved, packed = near_part(panel, first, offdiag_blocks, diag_tiles, *indices, True)
    side = merge_side(side, other_side, half_edges, near)
    more, extra = edge_second(first, near, packed, coupling, side, new_slot)

    sums = count + 8
    extra = settle(extra, swap(extra, "bulk", 1), flags, 0, sums, terms[-1])
    extra, row = leave_row(extra, swap(extra, "bulk", masks[0]), flags, sums)
    mask = 4
    while 2 * mask < bulk_count:
        extra = settle(extra, swap(extra, "bulk", mask), flags, 0, sums)
        mask *= 2
    extra, gram = last_gram(extra, swap(extra, "bulk", mask))
    for step in range(1, steps - 1):
        rows //= 2
        total, row = add_with_row(terms, rows, row, flags, step, extra)
        terms.append(swap(total, "bulk", masks[step]))
    solved = small_call(first_solves_kernel, count, 2, "first_solves", extra)
    following = small_call(next_gram_kernel, count, 3, "next_gram", extra, solved)
    gram = add_whole(gram, *(swap(gram, "group", mask) for mask in range(1, part_count)))
    return tuple(
        final(gram, solved, following, moving, moved, near, more, new_slot, row, flags, terms)
    )


def solution(mesh):
    rows = P(("group", "bulk"))
    return jax.shard_map(
        local,
        mesh=mesh,
        in_specs=(rows, rows, rows, rows, P(), P(), P()),
        out_specs=(rows, rows),
        check_vma=False,
    )
```

```python
import functools

import jax
import jax.numpy as jnp
from jax import lax
from jax.experimental import pallas as pl
from jax.experimental.pallas import tpu as pltpu
from jax.sharding import PartitionSpec as P

shift = 4.0
f32 = jnp.float32
bf16 = jnp.bfloat16
normal = (((1,), (0,)), ((), ()))
right_t = (((1,), (1,)), ((), ()))
left_t = (((0,), (0,)), ((), ()))
vmem = pl.BlockSpec(memory_space=pltpu.VMEM)
smem = pl.BlockSpec(memory_space=pltpu.SMEM)
anywhere = pl.BlockSpec(memory_space=pl.ANY)
vmem_bytes = 40 * 2**20
all_vmem = 56 * 2**20


def params(limit=vmem_bytes):
    return pltpu.CompilerParams(vmem_limit_bytes=limit)


def swap(value, axis, mask):
    pairs = [(source, source ^ mask) for source in range(lax.axis_size(axis))]
    return lax.ppermute(value, axis, pairs)


def split(value):
    high = value.astype(bf16)
    return high, (value - high.astype(f32)).astype(bf16)


def dot16(left, right, dims):
    return lax.dot_general(left, right, dims, preferred_element_type=f32)


def dot32(left, right, dims=normal):
    return lax.dot_general(
        left, right, dims, preferred_element_type=f32, precision=lax.Precision.HIGHEST
    )


def split_rows(vectors):
    high, low = split(vectors)
    return jnp.concatenate([high, low], axis=0)


def times_tile(rows, tile, dims):
    count = rows.shape[0] // 2
    high, low = split(tile)
    left = jnp.concatenate([rows[:count], rows[count:], rows[:count]], axis=1)
    return dot16(left, jnp.concatenate([high, high, low], axis=dims[0][1][0]), dims)


def dot24(left, right):
    high, low = split(left)
    other_high, other_low = split(right)
    left = jnp.concatenate([high, low, high], axis=1)
    return dot16(left, jnp.concatenate([other_high, other_high, other_low], axis=1), right_t)


def pack(gram):
    half = gram.shape[0] // 2
    return jnp.concatenate([gram[:half], gram[half:]], axis=1)


def unpack(packed):
    half = packed.shape[1] // 2
    return jnp.concatenate([packed[:, :half], packed[:, half:]], axis=0)


def above(count):
    rows = lax.broadcasted_iota(jnp.int32, (count, count), 0)
    cols = lax.broadcasted_iota(jnp.int32, (count, count), 1)
    return cols > rows, cols == rows


def identity(count):
    return above(count)[1].astype(f32)


def join_symmetric(upper, lower):
    over, diagonal = above(upper.shape[0])
    row = jnp.sum(jnp.where(diagonal, upper, 0.0), axis=0, keepdims=True)
    return jnp.where(over, upper, lower), row


def part_symmetric(joined, row):
    over, diagonal = above(joined.shape[0])
    turned = joined.T
    upper = jnp.where(diagonal, row, jnp.where(over, joined, turned))
    return upper, jnp.where(over, turned, joined)


def sym(gram):
    return 0.5 * (gram + gram.T)


def first_slot(row_count):
    device = lax.axis_index("group") * lax.axis_size("bulk") + lax.axis_index("bulk")
    return device * row_count


def live(load_ref, slot, tile):
    return jnp.where(tile < load_ref[slot], 1.0, 0.0)


def far_masks(bulk_count):
    masks = []
    bit = bulk_count // 2
    while bit >= 4:
        masks += [bit | bit // 2, bit // 2]
        bit //= 4
    return masks + ([bit] if bit == 2 else [])


def owed_place(rel, bulk_count):
    place = 0
    index = 0
    bit = bulk_count.bit_length() - 2
    while bit >= 2:
        high = (rel >> bit) & 1
        low = (rel >> (bit - 1)) & 1
        place = place | (high << index) | ((high ^ low) << (index + 1))
        index += 2
        bit -= 2
    if bit == 1:
        place = place | (((rel >> 1) & 1) << index)
        index += 1
    return place | ((rel & 1) << index)


def returned_kernel(bulk_count, moved, vectors, tiles, col, load, new_slot, *refs):
    keep, send, total = refs[-3:]
    row_count = vectors.shape[0]
    me = lax.axis_index("bulk")
    base = lax.axis_index("group") * bulk_count * row_count
    s = pl.program_id(0)
    slot = first_slot(row_count) + s

    @pl.when(s == 0)
    def _():
        total[...] = jnp.zeros_like(total)

    rows = split_rows(vectors[s])
    for t in range(tiles.shape[1]):
        product = times_tile(rows, tiles[0, t], normal)
        target = col[t, slot]
        if moved:
            target = new_slot[target]
        target = target - base
        owner = target // row_count
        place = owed_place(owner ^ me, bulk_count) * row_count + target - owner * row_count
        total[place] += live(load, slot, t) * product

    @pl.when(s == row_count - 1)
    def _():
        half = total.shape[0] // 2
        keep[...] = total[:half]
        send[...] = total[half:]


def returned(vectors, tiles, col, load, new_slot, bulk_count, moved, *earlier):
    row_count, count, order = vectors.shape
    tile_count = tiles.shape[1]
    half = (bulk_count * row_count // 2, count, order)
    return pl.pallas_call(
        functools.partial(returned_kernel, bulk_count, moved),
        grid=(row_count,),
        out_shape=[jax.ShapeDtypeStruct(half, f32) if moved else pltpu.VMEM(half, f32)] * 2,
        in_specs=[
            vmem,
            pl.BlockSpec((1, tile_count, order, order), lambda s: (s, 0, 0, 0)),
            smem,
            smem,
            smem,
        ]
        + [anywhere] * len(earlier),
        out_specs=[vmem] * 2,
        scratch_shapes=[pltpu.VMEM((2 * half[0], count, order), f32)],
        compiler_params=params(vmem_bytes if moved else all_vmem),
        name="returned_moved" if moved else "returned",
    )(vectors, tiles, col, load, new_slot, *earlier)


def near_kernel(bulk_count, pieces, second, *refs):
    panel, refs = refs[:pieces], refs[pieces:]
    vectors, tiles, diag, col, load, new_slot, near, moving, packed, *more, rows_of, gram = refs
    row_count, count = vectors.shape[:2]
    me = lax.axis_index("bulk")
    mine = lax.axis_index("group")
    base = mine * bulk_count * row_count
    s = pl.program_id(0)
    slot = first_slot(row_count) + s
    half_rows = bulk_count * row_count // 2
    held = [piece.shape[0] // count for piece in panel]
    starts = [sum(held[:index]) for index in range(pieces)]

    def place_of(target):
        target = target - base
        owner = target // row_count
        rel = owner ^ me
        return (rel & 1) * half_rows + (rel >> 1) * row_count + target - owner * row_count

    @pl.when(s == 0)
    def _():
        for piece, first, rows in zip(panel, starts, held):
            for k in range(rows):
                rows_of[first + k] = split_rows(piece[k * count : (k + 1) * count])
        gram[...] = jnp.zeros_like(gram)

    left, right = [], []
    for t in range(tiles.shape[1]):
        rows = rows_of[place_of(col[t, slot])]
        rows = jnp.where(t < load[slot], rows, jnp.zeros_like(rows))
        high, low = split(tiles[0, t])
        left += [rows[:count], rows[count:], rows[:count]]
        right += [high, high, low]
    direct = dot16(jnp.concatenate(left, axis=1), jnp.concatenate(right, axis=1), right_t)
    value = vectors[s]
    near_value = times_tile(split_rows(value), diag[0], right_t)
    near[s] = near_value + direct
    if second:
        gram[...] += dot24(value, near_value + 2.0 * direct)
    else:
        gram[...] += dot24(value, value)

    arriving = new_slot[slot]
    incoming = place_of(arriving)
    for piece, first, rows in zip(panel, starts, held):

        @pl.when((incoming >= first) & (incoming < first + rows))
        def _(piece=piece, first=first):
            start = pl.multiple_of((incoming - first) * count, count)
            moving[s] = piece[pl.ds(start, count)]

    if not second:
        (flags,) = more

        @pl.when(arriving != slot)
        def _():
            route = owed_place(((arriving - base) // row_count) ^ me, bulk_count)
            steps = flags.shape[0] // 8
            for index in range(steps):
                bit = ((route >> (steps - 1 - index)) & 1).astype(f32)
                flags[8 * index : 8 * index + 8] = jnp.full((8, flags.shape[1]), bit, f32)

    @pl.when(s == row_count - 1)
    def _():
        packed[...] = pack(gram[...])


def near_part(panel, vectors, tiles, diag, col, load, new_slot, second):
    row_count, count, order = vectors.shape
    bulk_count = sum(piece.shape[0] for piece in panel) // (row_count * count)
    tile_count = tiles.shape[1]
    shapes = [vectors.shape, vectors.shape, (count // 2, order)]
    if not second:
        shapes += [(8 * (bulk_count.bit_length() - 1), order)]
    return pl.pallas_call(
        functools.partial(near_kernel, bulk_count, len(panel), second),
        grid=(row_count,),
        out_shape=[jax.ShapeDtypeStruct(shape, f32) for shape in shapes],
        in_specs=[vmem] * len(panel)
        + [
            vmem,
            pl.BlockSpec((1, tile_count, order, order), lambda s: (s, 0, 0, 0)),
            pl.BlockSpec((1, order, order), lambda s: (s, 0, 0)),
            smem,
            smem,
            smem,
        ],
        out_specs=[vmem] * len(shapes),
        scratch_shapes=[
            pltpu.VMEM((bulk_count * row_count, 2 * count, order), bf16),
            pltpu.VMEM((count, count), f32),
        ],
        compiler_params=params(),
        name="near_second" if second else "near_first",
    )(*panel, vectors, tiles, diag, col, load, new_slot)


def crossed(side, coupling, k):
    edge_rows, part_count = coupling.shape[:2]
    count = side.shape[1] // 2
    mine = lax.axis_index("group")
    total = None
    for h in range(part_count):
        start = (h * edge_rows + k) * count
        rows = split_rows(side[start : start + count])
        term = times_tile(rows, coupling[k, mine ^ h], right_t)
        total = term if total is None else total + term
    return total


def gather_first_kernel(vectors, near, keep, *refs):
    received = refs[:-5]
    coupling, old_side, packed, first, side = refs[-5:]
    row_count, count = vectors.shape[:2]
    half = count // 2
    edge_rows = (side.shape[0] - 2 * half - 8) // count
    grams = [None, None]
    for k in range(row_count):
        value = near[k] + keep[k]
        for ref in received:
            value = value + ref[k]
        if k < edge_rows:
            value = value + crossed(old_side, coupling, k)
        first[k] = value
        if k < edge_rows:
            side[k * count : (k + 1) * count] = value
        terms = (dot24(vectors[k], value), dot24(value, value))
        grams = [term if old is None else old + term for old, term in zip(grams, terms)]
    start = edge_rows * count
    joined, row = join_symmetric(unpack(packed[...]), grams[1])
    side[start : start + half] = pack(joined)
    side[start + half : start + 2 * half] = pack(sym(grams[0]))
    rows = jnp.concatenate([row, jnp.zeros_like(row)], axis=1)
    side[start + 2 * half :] = jnp.broadcast_to(rows, (8, 2 * count))


def gather_first(vectors, near, terms, coupling, old_side, packed):
    row_count, count, order = vectors.shape
    edge_rows = coupling.shape[0]
    shapes = [vectors.shape, (edge_rows * count + count + 8, order)]
    specs = [pl.BlockSpec((row_count, count, order), lambda s: (0, 0, 0))] * (2 + len(terms))
    return pl.pallas_call(
        gather_first_kernel,
        grid=(1,),
        out_shape=[jax.ShapeDtypeStruct(shape, f32) for shape in shapes],
        in_specs=specs + [vmem] * 3,
        out_specs=[vmem] * 2,
        compiler_params=params(),
        name="gather_first",
    )(vectors, near, *terms, coupling, old_side, packed)


def edge_second_kernel(first, near, packed, coupling, side, new_slot, more, extra):
    row_count, count = first.shape[:2]
    edge_rows, part_count = coupling.shape[:2]
    half = count // 2
    gram = unpack(packed[...])
    for k in range(edge_rows):
        value = crossed(side, coupling, k)
        gram = gram + dot24(first[k], value)
        more[k] = value
    start = part_count * edge_rows * count
    joined, row = join_symmetric(unpack(side[start + half : start + 2 * half]), sym(gram))
    extra[:count] = jnp.concatenate([unpack(side[start : start + half]), joined], axis=1)
    row = jnp.concatenate([jnp.zeros_like(row), row], axis=1)
    extra[count : count + 8] = side[start + 2 * half :] + jnp.broadcast_to(row, (8, 2 * count))
    slot = first_slot(row_count)
    for k in range(edge_rows, row_count):

        @pl.when(new_slot[slot + k] != slot + k)
        def _(k=k):
            extra[count + 8 :] = near[k]


def edge_second(first, near, packed, coupling, side, new_slot):
    count, order = first.shape[1:]
    shapes = [(coupling.shape[0], count, order), (2 * count + 8, order)]
    return pl.pallas_call(
        edge_second_kernel,
        out_shape=[jax.ShapeDtypeStruct(shape, f32) for shape in shapes],
        in_specs=[vmem] * 5 + [smem],
        out_specs=[vmem] * 2,
        compiler_params=params(),
        name="edge_second",
    )(first, near, packed, coupling, side, new_slot)


def spread_row(rows, index):
    return jnp.broadcast_to(rows[index : index + 1], rows.shape)


def inverse_factors(matrices):
    count = matrices[0].shape[0]
    step = 8
    shape = (step, 2 * count)
    eye = identity(count)
    sub = lax.broadcasted_iota(jnp.int32, shape, 0)
    work = []
    for matrix in matrices:
        both = jnp.concatenate([matrix, eye], axis=1)
        work.append([both[i : i + step] for i in range(0, count, step)])
    for block in range(count // step):
        start = block * step
        for w in work:
            cols = [
                [jnp.broadcast_to(rows[:, start + m : start + m + 1], shape) for m in range(step)]
                for rows in w[block:]
            ]
            factor = [[None] * step for _ in range(step)]
            scales, pivots = [], []
            for m in range(step):
                value = spread_row(cols[0][m], m)
                row = spread_row(w[block], m)
                for u in range(m):
                    value = value - factor[m][u] * factor[m][u]
                    row = row - factor[m][u] * pivots[u]
                scales.append(lax.rsqrt(value))
                pivots.append(row * scales[m])
                for v in range(m + 1, step):
                    value = spread_row(cols[0][m], v)
                    for u in range(m):
                        value = value - factor[v][u] * factor[m][u]
                    factor[v][m] = value * scales[m]
            for i in range(block + 1, count // step):
                left = []
                for m in range(step):
                    value = cols[i - block][m]
                    for u in range(m):
                        value = value - left[u] * factor[m][u]
                    left.append(value * scales[m])
                terms = [one * pivot for one, pivot in zip(left, pivots)]
                while len(terms) > 1:
                    terms = [x + y for x, y in zip(terms[::2], terms[1::2])]
                w[i] = w[i] - terms[0]
            rows = pivots[0]
            for m in range(1, step):
                rows = jnp.where(sub == m, pivots[m], rows)
            w[block] = rows
    return [jnp.concatenate(w, axis=0)[:, count:] for w in work]


def solve(inverse_factor, right):
    return dot32(inverse_factor, dot32(inverse_factor, right), left_t)


def grams_of(sums):
    count = sums.shape[1] // 2
    row = sums[count : count + 1]
    g0, g2 = part_symmetric(sums[:count, :count], row[:, :count])
    g1, g3 = part_symmetric(sums[:count, count:], row[:, count:])
    return g0, g1, g2, g3


def first_solves_kernel(extra, out):
    g0, g1, _, _ = grams_of(extra[...])
    factor_pq, factor_rr = inverse_factors([shift * g0 + g1, g0])
    out[0] = solve(factor_pq, g0)
    out[1] = dot32(factor_rr, factor_rr, left_t)


def next_gram_kernel(extra, solved, out):
    g0, g1, g2, _ = grams_of(extra[...])
    a, inverse_rr = solved[0], solved[1]
    count = a.shape[0]
    m = identity(count) - shift * a
    by_a = dot32(jnp.concatenate([g0, g1, g2], axis=0), a)
    g0a, g1a, g2a = (by_a[i * count : (i + 1) * count] for i in range(3))
    g0m, g1m = g0 - shift * g0a, g1 - shift * g1a
    left = jnp.concatenate([m, a], axis=0)
    g_new = sym(dot32(left, jnp.concatenate([g0m - g1a, g2a - g1m], axis=0), left_t))
    c = m + dot32(inverse_rr, g_new)
    by_c = dot32(jnp.concatenate([shift * g0 + g1, shift * g1 + g2], axis=0), c)
    left = jnp.concatenate([c, a], axis=0)
    upper = by_c[:count] - (shift * g1a + g2a)
    lower = shift * g2a - by_c[count:]
    out[0] = c
    out[1] = g_new
    out[2] = dot32(left, jnp.concatenate([upper, lower], axis=0), left_t)


def early_solves_kernel(extra, solved, following):
    first_solves_kernel(extra, solved)
    next_gram_kernel(extra, solved, following)


def early_solves(extra, count):
    return pl.pallas_call(
        early_solves_kernel,
        out_shape=[jax.ShapeDtypeStruct((matrices, count, count), f32) for matrices in (2, 3)],
        in_specs=[vmem],
        out_specs=[vmem] * 2,
        compiler_params=params(),
        name="early_solves",
    )(extra)


def final_kernel(gram, solved, following, moving, first, near, more, new_slot, row, *refs):
    last_row, flags, *terms, solution, resid = refs
    row_count, count = moving.shape[:2]
    arrived = jnp.where(flags[flags.shape[0] - 8 :][:1] > 0.5, last_row[0], row[...])
    a, c, g_new = solved[0], following[0], following[1]
    g3 = sym(unpack(gram[...]))
    g_pq = sym(following[2] + dot32(a, dot32(g3, a), left_t))
    (factor,) = inverse_factors([g_pq])
    a1 = solve(factor, g_new)
    by_a1 = dot32(jnp.concatenate([a, c], axis=0), a1)
    aa1, ca1 = by_a1[:count], by_a1[count:]
    m = identity(count) - shift * a
    top = jnp.concatenate([a + ca1, -aa1, jnp.zeros_like(a)], axis=0)
    low = jnp.concatenate([m - shift * ca1, shift * aa1 - a - ca1, aa1], axis=0)
    coef = jnp.concatenate([top, low], axis=1)
    slot = first_slot(row_count)
    basis = []
    for k in range(row_count):
        stays = new_slot[slot + k] == slot + k
        second = jnp.where(stays, near[k], arrived)
        if k < more.shape[0]:
            second = second + more[k]
        for ref in terms:
            second = second + ref[k]
        basis.append(jnp.concatenate([moving[k], first[k], second], axis=0))
    order = moving.shape[2]
    both = dot32(coef, jnp.concatenate(basis, axis=1), left_t)
    for k in range(row_count):
        solution[k] = both[:count, k * order : (k + 1) * order]
        resid[k] = both[count:, k * order : (k + 1) * order]


def final(gram, solved, following, moving, first, near, more, new_slot, row, flags, terms):
    block = pl.BlockSpec(near.shape, lambda s: (0, 0, 0))
    last = pl.BlockSpec((1,) + near.shape[1:], lambda s: (terms[-1].shape[0] - 1, 0, 0))
    return pl.pallas_call(
        final_kernel,
        grid=(1,),
        out_shape=[jax.ShapeDtypeStruct(near.shape, f32)] * 2,
        in_specs=[vmem] * 7 + [smem, vmem, last, vmem] + [block] * len(terms),
        out_specs=[vmem] * 2,
        compiler_params=params(),
        name="final",
    )(gram, solved, following, moving, first, near, more, new_slot, row, terms[-1], flags, *terms)


def add_kernel(count, *refs):
    total = refs[0][...]
    for ref in refs[1:count]:
        total = total + ref[...]
    refs[-1][...] = total


def add_upper(terms, rows, *earlier):
    shape = (rows,) + terms[0].shape[1:]
    block = pl.BlockSpec(shape, lambda s: (1, 0, 0))
    return pl.pallas_call(
        functools.partial(add_kernel, len(terms)),
        grid=(1,),
        out_shape=jax.ShapeDtypeStruct(shape, f32),
        in_specs=[block] * len(terms) + [anywhere] * len(earlier),
        out_specs=vmem,
        compiler_params=params(),
        name="add_upper",
    )(*terms, *earlier)


def add_with_row_kernel(step, count, row, other, flags, *refs):
    terms, out, held = refs[:count], refs[-2], refs[-1]
    total = terms[0][...]
    for ref in terms[1:]:
        total = total + ref[...]
    out[: total.shape[0]] = total
    value = row[...]
    if step > 1:
        value = jnp.where(flags[8 * step : 8 * step + 1] > 0.5, other[0], value)
    out[total.shape[0]] = value
    held[...] = value


def add_with_row(terms, rows, row, flags, step, *earlier):
    shape = (rows,) + terms[0].shape[1:]
    block = pl.BlockSpec(shape, lambda s: (1, 0, 0))
    last = pl.BlockSpec((1,) + shape[1:], lambda s: (terms[-1].shape[0] - 1, 0, 0))
    return pl.pallas_call(
        functools.partial(add_with_row_kernel, step, len(terms)),
        grid=(1,),
        out_shape=[
            jax.ShapeDtypeStruct((rows + 1,) + shape[1:], f32),
            jax.ShapeDtypeStruct(row.shape, f32),
        ],
        in_specs=[vmem, last, vmem] + [block] * len(terms) + [anywhere] * len(earlier),
        out_specs=[vmem] * 2,
        compiler_params=params(),
        name="add_with_row",
    )(row, terms[-1], flags, *terms, *earlier)


def settle_kernel(index, sums, extra, partner, flags, *refs):
    out = refs[-1]
    out[:sums] = extra[:sums] + partner[:sums]
    if extra.shape[0] > sums:
        chosen = flags[8 * index : 8 * index + 1] > 0.5
        out[sums:] = jnp.where(chosen, partner[sums:], extra[sums:])


def settle(extra, partner, flags, index, sums, *earlier):
    return pl.pallas_call(
        functools.partial(settle_kernel, index, sums),
        out_shape=jax.ShapeDtypeStruct(extra.shape, f32),
        in_specs=[vmem] * 3 + [anywhere] * len(earlier),
        out_specs=vmem,
        compiler_params=params(),
        name="settle",
    )(extra, partner, flags, *earlier)


def leave_row_kernel(sums, extra, partner, flags, out, row):
    out[...] = extra[:sums] + partner[:sums]
    row[...] = jnp.where(flags[8:9] > 0.5, partner[sums:], extra[sums:])


def leave_row(extra, partner, flags, sums):
    order = extra.shape[1]
    return pl.pallas_call(
        functools.partial(leave_row_kernel, sums),
        out_shape=[
            jax.ShapeDtypeStruct((sums, order), f32),
            jax.ShapeDtypeStruct((extra.shape[0] - sums, order), f32),
        ],
        in_specs=[vmem] * 3,
        out_specs=[vmem] * 2,
        compiler_params=params(),
        name="leave_row",
    )(extra, partner, flags)


def last_gram_kernel(sums, partner, out, gram):
    total = sums[...] + partner[...]
    out[...] = total
    gram[...] = pack(grams_of(total)[3])


def last_gram(sums, partner):
    rows, order = sums.shape
    return pl.pallas_call(
        last_gram_kernel,
        out_shape=[
            jax.ShapeDtypeStruct((rows, order), f32),
            jax.ShapeDtypeStruct((order // 4, order), f32),
        ],
        in_specs=[vmem] * 2,
        out_specs=[vmem] * 2,
        compiler_params=params(),
        name="last_gram",
    )(sums, partner)


def add_whole(*terms):
    return pl.pallas_call(
        functools.partial(add_kernel, len(terms)),
        out_shape=jax.ShapeDtypeStruct(terms[0].shape, f32),
        in_specs=[vmem] * len(terms),
        out_specs=vmem,
        compiler_params=params(),
        name="add_whole",
    )(*terms)


def pass_on(value, *earlier):
    return pl.pallas_call(
        functools.partial(add_kernel, 1),
        out_shape=jax.ShapeDtypeStruct(value.shape, f32),
        in_specs=[vmem] + [anywhere] * len(earlier),
        out_specs=vmem,
        compiler_params=params(),
        name="pass_on",
    )(value, *earlier)


def join_kernel(count, *refs):
    out = refs[-1]
    rows = refs[0].shape[0]
    for index, ref in enumerate(refs[:count]):
        out[index * rows : (index + 1) * rows] = ref[...]


def join(pieces, *earlier):
    rows, order = pieces[0].shape
    return pl.pallas_call(
        functools.partial(join_kernel, len(pieces)),
        out_shape=jax.ShapeDtypeStruct((len(pieces) * rows, order), f32),
        in_specs=[vmem] * len(pieces) + [anywhere] * len(earlier),
        out_specs=vmem,
        compiler_params=params(),
        name="join",
    )(*pieces, *earlier)


def merge_kernel(edge, mine, other, *refs):
    out = refs[-1]
    out[:edge] = mine[:edge]
    out[edge : 2 * edge] = other[:edge]
    if mine.shape[0] > edge:
        out[2 * edge :] = mine[edge:] + other[edge:]


def merge_side(side, other, edge, *earlier):
    return pl.pallas_call(
        functools.partial(merge_kernel, edge),
        out_shape=jax.ShapeDtypeStruct((side.shape[0] + edge, side.shape[1]), f32),
        in_specs=[vmem] * 2 + [anywhere] * len(earlier),
        out_specs=vmem,
        compiler_params=params(),
        name="merge_side",
    )(side, other, *earlier)


def share_side(side, edge, part_count):
    mask = 1
    while 2 * mask < part_count:
        side = merge_side(side, swap(side, "group", mask), mask * edge)
        mask *= 2
    return side, swap(side, "group", mask)


def share_panel(piece, bulk_count, pieces, *earlier):
    own = [piece] + [swap(piece, "bulk", rel) for rel in range(2, bulk_count, 2)]
    size = len(own) // pieces
    joined = [join(own[i * size : (i + 1) * size]) for i in range(pieces - 1)]
    joined.append(join(own[(pieces - 1) * size :], *earlier))
    return own + [swap(one, "bulk", 1) for one in joined], joined[-1]


def local(rhs, diag_tiles, offdiag_blocks, coupling, col_index, load, new_slot):
    row_count, count, order = rhs.shape
    edge_rows, part_count = coupling.shape[:2]
    bulk_count = lax.axis_size("bulk")
    steps = bulk_count.bit_length() - 1
    masks = far_masks(bulk_count)[::-1]
    edge = edge_rows * count
    half_edges = part_count // 2 * edge
    indices = (col_index.T, load, new_slot)

    flat = rhs.reshape(row_count * count, order)
    side, other_side = share_side(flat[:edge], edge, part_count)
    keep, send = returned(rhs, offdiag_blocks, *indices, bulk_count, False)
    panel, joined = share_panel(flat, bulk_count, 2, side)
    terms = [keep, swap(send, "bulk", 1)]
    rows = bulk_count // 2 * row_count
    for step, mask in enumerate(masks):
        rows //= 2
        total = add_upper(terms, rows, *([joined] if step else []))
        terms.append(swap(total, "bulk", mask))
    near, moving, packed, flags = near_part(
        panel, rhs, offdiag_blocks, diag_tiles, *indices, False
    )
    side = merge_side(side, other_side, half_edges, near)
    first, side = gather_first(rhs, near, terms, coupling, side, packed)

    side, other_side = share_side(side, edge, part_count)
    keep, send = returned(first, offdiag_blocks, *indices, bulk_count, True)
    panel, joined = share_panel(
        first.reshape(row_count * count, order), bulk_count, 1, side, keep
    )
    terms = [keep, swap(pass_on(send, joined), "bulk", 1)]
    rows = bulk_count // 4 * row_count
    terms.append(swap(add_upper(terms, rows), "bulk", masks[0]))
    near, moved, packed = near_part(panel, first, offdiag_blocks, diag_tiles, *indices, True)
    side = merge_side(side, other_side, half_edges, near)
    more, extra = edge_second(first, near, packed, coupling, side, new_slot)

    sums = count + 8
    extra = settle(extra, swap(extra, "bulk", 1), flags, 0, sums, terms[-1])
    extra, row = leave_row(extra, swap(extra, "bulk", masks[0]), flags, sums)
    mask = 4
    while 2 * mask < bulk_count:
        extra = settle(extra, swap(extra, "bulk", mask), flags, 0, sums)
        mask *= 2
    extra, gram = last_gram(extra, swap(extra, "bulk", mask))
    for step in range(1, steps - 1):
        rows //= 2
        total, row = add_with_row(terms, rows, row, flags, step, extra)
        terms.append(swap(total, "bulk", masks[step]))
    solved, following = early_solves(extra, count)
    gram = add_whole(gram, *(swap(gram, "group", mask) for mask in range(1, part_count)))
    return tuple(
        final(gram, solved, following, moving, moved, near, more, new_slot, row, flags, terms)
    )


def solution(mesh):
    rows = P(("group", "bulk"))
    return jax.shard_map(
        local,
        mesh=mesh,
        in_specs=(rows, rows, rows, rows, P(), P(), P()),
        out_specs=(rows, rows),
        check_vma=False,
    )
```
